128 devices in a mesh: dp: 32 (over y, x, core), sub: 4 (over z).
Axes of the slice: x: 4, y: 4, z: 4, core: 2. Of those that a mesh axis runs over, the one named last changes fastest.
Arguments:
- queries: float32 [16384, 4096], P(('dp', 'sub')), may hold values from -1 to 1
- passages: float32 [16384, 4096], P(('dp', 'sub')), may hold values from -1 to 1
- counts: int32 [128, 128], P(('dp', 'sub')), may hold values from 1 to 64, as said below
- hard_owner: int32 [128, 256, 1], P(('dp', 'sub')), may hold values from 0 to 127; in each aligned block of 256 rows (0 to 255, 256 to 511, ..., all dimensions but the last counted through in order) at most 4 rows name the same one
- hard_local: int32 [128, 256], P(('dp', 'sub')), may hold values from 0 to 127
Outputs:
- loss: float32 [], replicated
- query_grad: float32 [16384, 4096], P(('dp', 'sub'))
- passage_grad: float32 [16384, 4096], P(('dp', 'sub'))
The draws below stay inside these ranges and needn't reach their ends.
Inputs may be any that keep to these rules, and one draw needn't show every extreme that they name: Each row of counts sums to 256, and its largest entry is 64. `hard_owner`: among the 256 slots of one row block at most 4 name the same owner block, and some owner block is named exactly 4 times.
All inputs are finite; a program needn't handle non-finite values.
Results may differ from the reference program's by a relative error of at most 0.0052.
The reference program's roundings to bfloat16 on the way count: a program that leaves them out, or rounds other values in their place, can miss the bound.
Values may be sent and summed in bfloat16 or wider, within the bound.
A program may use at most 128 MiB of HBM per device.

```python
import math
import jax
import jax.numpy as jnp
import numpy as np
from jax import lax

D = 4096
ROWS = 128
MOST_HARD = 64
TILES = 128
DISTRACTOR_SET = 512
NQ = 16384
HARD = 256
CAP = 4
N_DP = 32
N_SUB = 4


topic_span = 2


topic_weight = 0.5


own_weight = 0.1


noise_weight = 0.8


def topic_table(key):
    key = jax.random.fold_in(key, 101)
    order = jax.random.permutation(key, ROWS).astype(jnp.int32)
    topic = (order // topic_span).astype(jnp.int32)
    inverse = jnp.zeros((ROWS,), jnp.int32).at[order].set(jnp.arange(ROWS, dtype=jnp.int32))
    return (topic, inverse)


def count_table(key):
    key = jax.random.fold_in(key, 202)
    spare = HARD - MOST_HARD - ROWS + 1
    pool = jnp.arange((ROWS - 1) * (MOST_HARD - 1), dtype=jnp.int32) // (MOST_HARD - 1)
    ranks = jnp.arange(ROWS - 1, dtype=jnp.int32)

    def one_block(block_key):
        first, second = jax.random.split(block_key)
        order = jax.random.permutation(first, ROWS).astype(jnp.int32)
        picked = jax.random.permutation(second, pool)[:spare]
        extra = jnp.sum((picked[:, None] == ranks[None, :]).astype(jnp.int32), axis=0)
        values = jnp.concatenate([jnp.full((1,), MOST_HARD, jnp.int32), 1 + extra])
        return jnp.zeros((ROWS,), jnp.int32).at[order].set(values.astype(jnp.int32))
    return jax.vmap(one_block)(jax.random.split(key, TILES))


def shared_parts(key):
    key = jax.random.fold_in(key, 303)
    first, second, third = jax.random.split(key, 3)
    common = jax.random.truncated_normal(first, -4.0, 4.0, (1, D), jnp.float32)
    topics = jax.random.truncated_normal(second, -4.0, 4.0, (ROWS // topic_span, D), jnp.float32)
    own = jax.random.truncated_normal(third, -4.0, 4.0, (NQ, D), jnp.float32)
    return (common, topics, own)


def row_levels(key, lowest, highest, smallest, largest):
    first, second = jax.random.split(key)
    level = jax.random.uniform(first, (NQ, 1), jnp.float32, lowest, highest)
    scale = jnp.exp(jax.random.uniform(second, (NQ, 1), jnp.float32, math.log(smallest), math.log(largest)))
    return (level, scale)


def draw_counts(key, part):
    return count_table(key)


def draw_hard_local(key, part):
    counts = count_table(key)
    topic, inverse = topic_table(key)
    key = jax.random.fold_in(key, 11)
    ends = jnp.cumsum(counts, axis=1)
    slots = jnp.arange(HARD, dtype=jnp.int32)
    asking_row = jnp.sum((ends[:, None, :] <= slots[None, :, None]).astype(jnp.int32), axis=2)
    choose = jax.random.randint(key, (TILES, HARD), 0, topic_span)
    return inverse[topic[asking_row] * topic_span + choose].astype(jnp.int32)


def draw_passages(key, part):
    common, topics, own = shared_parts(key)
    topic, inverse = topic_table(key)
    key = jax.random.fold_in(key, 13)
    level, scale = row_levels(key, 0.85, 1.15, 0.5, 5.0)
    values = level * common + own + topic_weight * topics[jnp.tile(topic, TILES)]
    return (scale * values / math.sqrt(D)).astype(jnp.float32)


def draw_queries(key, part):
    common, topics, own = shared_parts(key)
    topic, inverse = topic_table(key)
    key = jax.random.fold_in(key, 17)
    first, second = jax.random.split(key)
    level, scale = row_levels(first, 0.85, 1.15, 0.5, 5.0)
    noise = jax.random.truncated_normal(second, -4.0, 4.0, (NQ, D), jnp.float32)
    values = level * common + own_weight * own + topic_weight * topics[jnp.tile(topic, TILES)] + noise_weight * noise
    return (scale * values / math.sqrt(D)).astype(jnp.float32)


def routed_block(key, own, number, rows, amount, top, bound, lean):
    sequence = jax.random.permutation(key, amount)
    heavy_load, ordinary = portions_of(amount, rows * top, bound, lean, True), portions_of(amount, rows * top, bound, lean, False)
    places = jnp.arange(amount)

    def named(tallies, rotation):
        used = int((tallies > 0).sum())
        fixed = max(1, used // 4)
        passed = fixed + (places - fixed + rotation * (used - fixed)) % max(1, amount - fixed)
        return jnp.zeros((amount,), jnp.int32).at[sequence[jnp.where(places < fixed, places, passed)]].set(jnp.asarray(tallies, jnp.int32))

    tallies = jnp.where(number % 4 == 0, named(heavy_load, number // 4), named(ordinary, number - number // 4 - 1))
    mixed = jax.random.permutation(jax.random.fold_in(own, 3), amount)
    donor, receiver = mixed[0:amount // 2 * 2:2], mixed[1:amount // 2 * 2:2]
    room = jnp.minimum(tallies[donor] - 1, bound - tallies[receiver]) // 2
    room = jnp.where((donor == sequence[0]) | (receiver == sequence[0]) | (tallies[receiver] == 0), 0, jnp.maximum(room, 0))
    passed = jax.random.randint(jax.random.fold_in(own, 4), (amount // 2,), 0, 1 << 20) % (room + 1)
    tallies = tallies.at[donor].add(-passed).at[receiver].add(passed)
    items = jnp.searchsorted(jnp.cumsum(tallies), jnp.arange(rows * top), side="right").astype(jnp.int32)
    listing = items.reshape(top, rows).T
    listing = listing[jax.random.permutation(jax.random.fold_in(own, 1), rows)]
    rotation = jax.random.randint(jax.random.fold_in(own, 2), (rows, 1), 0, top)
    return jnp.take_along_axis(listing, (jnp.arange(top)[None, :] + rotation) % top, axis=1)


def portions_of(count, total, limit, slope, full):
    portions = [(1 << 20) // math.isqrt(rank ** slope) + 1 for rank in range(1, count + 1)]
    largest = limit if full else min(limit, max(-(-total // count), total * portions[0] // sum(portions)))
    least = 1 if total - largest >= count - 1 else 0
    given, rest = [largest] + [least] * (count - 1), total - largest - least * (count - 1)
    while rest > 0:
        movable = [i for i in range(1, count) if given[i] < largest] or [i for i in range(1, count) if given[i] < limit]
        mass, left = sum([portions[i] for i in movable]), rest
        for i in movable:
            addition = min(limit - given[i], max(1, left * portions[i] // mass), rest)
            given[i] = given[i] + addition
            rest = rest - addition
    return np.array(given)


def setup_inputs(seed: int = 0) -> dict:
    arg_keys = jax.random.split(jax.random.key(seed), 6)
    queries = draw_queries(jax.random.fold_in(arg_keys[5], 71), 0)
    passages = draw_passages(jax.random.fold_in(arg_keys[5], 71), 0)
    counts = draw_counts(jax.random.fold_in(arg_keys[5], 71), 0)
    hard_owner_keys = jax.random.split(jax.random.fold_in(arg_keys[3], 1), TILES * HARD // HARD)
    hard_owner_turns = jax.random.permutation(jax.random.fold_in(arg_keys[3], 3), TILES * HARD // HARD)
    hard_owner = jax.vmap(lambda own, number: routed_block(jax.random.fold_in(arg_keys[3], 2), own, number, HARD, TILES, 1, CAP, 2))(hard_owner_keys, hard_owner_turns).reshape((TILES, HARD, 1))
    hard_local = draw_hard_local(jax.random.fold_in(arg_keys[5], 71), 0)
    return dict(queries=queries, passages=passages, counts=counts, hard_owner=hard_owner, hard_local=hard_local)


sharpness_divisor = 0.02
epsilon = 1e-06

def unit_rows(values):
    norms = jnp.sqrt(lax.optimization_barrier(jnp.sum(values * values, axis=1, keepdims=True)) + epsilon)
    return (values / norms, norms)

def raw_grad(grad, units, norms):
    inner = lax.optimization_barrier(jnp.sum(units * grad, axis=1, keepdims=True))
    return (grad - units * inner) / norms

def reference(queries, passages, counts, hard_owner, hard_local):
    query_dir, query_norm = unit_rows(queries)
    passage_dir, passage_norm = unit_rows(passages)
    query_unit = query_dir.astype(jnp.bfloat16)
    passage_unit = passage_dir.astype(jnp.bfloat16)
    ends = jnp.cumsum(counts, axis=1)
    slots = jnp.arange(HARD, dtype=jnp.int32)
    local_query = lax.optimization_barrier(jnp.sum((ends[:, None, :] <= slots[None, :, None]).astype(jnp.int32), axis=2))
    tile_ids = jnp.arange(TILES, dtype=jnp.int32)[:, None]
    slot_query = (tile_ids * ROWS + local_query).astype(jnp.int32).reshape(N_DP, N_SUB * HARD)
    slot_passage = (hard_owner[:, :, 0] * ROWS + hard_local).astype(jnp.int32).reshape(N_DP, N_SUB * HARD)
    diagonal = jnp.arange(DISTRACTOR_SET)[:, None] == jnp.arange(DISTRACTOR_SET)[None, :]

    def step(accum, index):
        start = (index * DISTRACTOR_SET).astype(jnp.int32)
        question_cluster_lines = lax.dynamic_slice_in_dim(query_unit, start, DISTRACTOR_SET, 0)
        cluster_likelihood = lax.dynamic_slice_in_dim(passage_unit, start, DISTRACTOR_SET, 0)
        slot_q = slot_query[index]
        slot_p = slot_passage[index]
        cosine_score_matrix = jnp.dot(question_cluster_lines, cluster_likelihood.T, preferred_element_type=jnp.float32) / sharpness_divisor
        mined_question_lines = query_unit[slot_q]
        mined_distractor_lines = passage_unit[slot_p]
        mined_cosine_scores = lax.optimization_barrier(jnp.sum(mined_question_lines.astype(jnp.float32) * mined_distractor_lines.astype(jnp.float32), axis=1)) / sharpness_divisor
        device_question_lines = (slot_q - start).astype(jnp.int32)
        exp_batch = jnp.exp(cosine_score_matrix)
        exp_hard = jnp.exp(mined_cosine_scores)
        total = lax.optimization_barrier(jnp.sum(exp_batch, axis=1)) + jax.ops.segment_sum(exp_hard, device_question_lines, num_segments=DISTRACTOR_SET)
        positive = lax.optimization_barrier(jnp.sum(jnp.where(diagonal, cosine_score_matrix, 0.0), axis=1))
        loss_part = jnp.sum(jnp.log(total) - positive)
        inbatch_weighting = (exp_batch / total[:, None] - diagonal.astype(jnp.float32)).astype(jnp.bfloat16)
        mined_weighting = (exp_hard / total[device_question_lines]).astype(jnp.bfloat16)
        mined_exponentials = mined_weighting.astype(jnp.float32)[:, None] * mined_distractor_lines.astype(jnp.float32)
        question_derivative = (jnp.dot(inbatch_weighting, cluster_likelihood, preferred_element_type=jnp.float32) + jax.ops.segment_sum(mined_exponentials, device_question_lines, num_segments=DISTRACTOR_SET)) / sharpness_divisor
        inbatch_likelihood = jnp.dot(inbatch_weighting.T, question_cluster_lines, preferred_element_type=jnp.float32) / sharpness_divisor
        position_derivative = (mined_weighting.astype(jnp.float32)[:, None] * mined_question_lines.astype(jnp.float32) / sharpness_divisor).astype(jnp.bfloat16)
        accum = accum.at[slot_p].add(position_derivative.astype(jnp.float32))
        return (accum, (loss_part, question_derivative, inbatch_likelihood))
    start_accum = jnp.zeros((TILES * ROWS, D), jnp.float32)
    accum, (losses, q_grads, p_batches) = lax.scan(step, start_accum, jnp.arange(N_DP, dtype=jnp.int32))
    query_unit_grad = q_grads.reshape(TILES * ROWS, D)
    unitlength_document_derivative = p_batches.reshape(TILES * ROWS, D) + accum
    loss = jnp.sum(losses) / (TILES * ROWS)
    return (loss, raw_grad(query_unit_grad, query_dir, query_norm), raw_grad(unitlength_document_derivative, passage_dir, passage_norm))
```

```python
import jax
import jax.numpy as jnp
from jax import lax
from jax.experimental import pallas as pl
from jax.experimental.pallas import tpu as pltpu
from jax.sharding import PartitionSpec as P

MESH = pl.DeviceIdType.MESH
F32 = jnp.float32
BF16 = jnp.bfloat16

sharpness_divisor = 0.02
epsilon = 1e-06

ROWS = 128
WIDTH = 4096
HARD = 256
CAP = 4
N_SUB = 4
N_DP = 32
GROUP = ROWS * N_SUB
SLOTS = N_DP * N_SUB * CAP
MSG = N_SUB * CAP
CHUNKS = 8
CW = WIDTH // CHUNKS


def plane_order():
    def loads(o):
        load = [0, 0, 0, 0]
        for d, axis in ((o[0], 0), (o[1], 2)):
            if d in (1, 2):
                load[axis] += 1
            if d in (3, 2):
                load[axis + 1] += 1
        return load

    rest = [(a, b, c) for a in range(4) for b in range(4) for c in range(2) if (a, b, c) != (0, 0, 0)]
    done, order = [0, 0, 0, 0], []
    while rest:

        def cost(o):
            after = [p + q for p, q in zip(done, loads(o))]
            return (max(after) - min(after), -sum(loads(o)), o[2])

        best = min(rest, key=cost)
        done = [p + q for p, q in zip(done, loads(best))]
        order.append(best)
        rest.remove(best)
    return order


ORDER = plane_order()


def dot(a, b):
    return lax.dot_general(a, b, (((1,), (0,)), ((), ())), preferred_element_type=F32)


def dot_nt(a, b):
    return lax.dot_general(a, b, (((1,), (1,)), ((), ())), preferred_element_type=F32)


def iota(shape, dim):
    return lax.broadcasted_iota(jnp.int32, shape, dim)


def one_hot(mask):
    return jnp.where(mask, 1.0, 0.0).astype(BF16)


def kernel(
    p_hbm, q_hbm, cnt_ref, own_ref, loc_ref,
    loss_ref, qg_hbm, pg_hbm,
    pf, qf, pall, qall, s1, r1, s2, r2,
    e_send, e_recv, f_send, f_recv, cb_send, cb_recv, g_send, g_recv, w_send, w_recv,
    l1_send, l1_recv, l2_send, l2_recv,
    qg, pg, sacc, hacc, es, fs, ftm, chm, cbm, wt, cbt, qinv, pinv,
    in_sem, out_sem, ag_s, ag_r, s1_s, s1_r, s2_s, s2_r, t_s, t_r,
):
    dp = lax.axis_index("dp")
    z = lax.axis_index("sub")
    core = lax.rem(dp, 2)
    x = lax.rem(dp // 2, 4)
    y = dp // 8
    peers = []
    for dx, dy, dc in ORDER:
        peers.append((lax.rem(y + dy, 4) * 4 + lax.rem(x + dx, 4)) * 2 + lax.rem(core + dc, 2))
    mates = [lax.rem(z + d, N_SUB) for d in (1, 3, 2)]

    barrier = pltpu.get_barrier_semaphore()
    for peer in peers:
        pl.semaphore_signal(barrier, inc=1, device_id=(peer, z), device_id_type=MESH)
    for mate in mates:
        pl.semaphore_signal(barrier, inc=1, device_id=(dp, mate), device_id_type=MESH)

    p_in = pltpu.make_async_copy(p_hbm, pf, in_sem.at[0])
    q_in = pltpu.make_async_copy(q_hbm, qf, in_sem.at[1])
    p_in.start()
    q_in.start()

    def rows_at(ref, index, rows):
        return ref.at[pl.ds(pl.multiple_of(index * rows, rows), rows)]

    def landed(ref, rows, sem):
        part = ref.at[pl.ds(0, rows)]
        pltpu.make_async_copy(part, part, sem).wait()

    def to_plane(src, dst, send, recv, rows):
        for peer in peers:
            pltpu.make_async_remote_copy(
                src_ref=rows_at(src, peer, rows), dst_ref=rows_at(dst, dp, rows),
                send_sem=send, recv_sem=recv, device_id=(peer, z), device_id_type=MESH,
            ).start()

    def to_mates(src, dst, send, recv, rows):
        for mate in mates:
            pltpu.make_async_remote_copy(
                src_ref=rows_at(src, mate, rows), dst_ref=rows_at(dst, z, rows),
                send_sem=send, recv_sem=recv, device_id=(dp, mate), device_id_type=MESH,
            ).start()

    def gather_start(buf, k, sem):
        for mate in mates:
            pltpu.make_async_remote_copy(
                src_ref=rows_at(buf.at[k], z, ROWS), dst_ref=rows_at(buf.at[k], z, ROWS),
                send_sem=ag_s.at[sem], recv_sem=ag_r.at[sem],
                device_id=(dp, mate), device_id_type=MESH,
            ).start()

    def keep(src, dst, index, rows):
        at = pl.ds(pl.multiple_of(index * rows, rows), rows)
        dst[at, :] = src[at, :]

    own_row = own_ref[...]
    loc_row = loc_ref[...]
    cnt_row = cnt_ref[...]
    square = (HARD, HARD)
    row_b = jnp.broadcast_to(own_row, square)
    own_col = jnp.sum(jnp.where(iota(square, 0) == iota(square, 1), row_b, 0), axis=1, keepdims=True)
    earlier = (own_col == row_b) & (iota(square, 0) < iota(square, 1))
    rank = jnp.sum(jnp.where(earlier, 1, 0), axis=0, keepdims=True)
    place = own_row * CAP + rank
    slot_at = one_hot(iota((SLOTS, HARD), 0) == place)
    local_t = one_hot(iota((ROWS, HARD), 0) == loc_row)
    cnt_b = jnp.broadcast_to(cnt_row, (ROWS, ROWS))
    upto = iota((ROWS, ROWS), 1) <= iota((ROWS, ROWS), 0)
    before = iota((ROWS, ROWS), 1) < iota((ROWS, ROWS), 0)
    ends = jnp.sum(jnp.where(upto, cnt_b, 0), axis=1, keepdims=True)
    starts = jnp.sum(jnp.where(before, cnt_b, 0), axis=1, keepdims=True)
    slot_id = iota((ROWS, HARD), 1)
    query_t = one_hot((slot_id >= starts) & (slot_id < ends))
    e_send[...] = dot_nt(slot_at, local_t).astype(BF16)
    ftm[...] = dot_nt(query_t, slot_at)
    rz = iota((SLOTS, SLOTS), 0)
    cz = iota((SLOTS, SLOTS), 1)
    by_z = one_hot((rz // ROWS == (cz // CAP) % N_SUB) & ((rz // CAP) % N_DP == cz // MSG) & (rz % CAP == cz % CAP))
    f_send[...] = dot(by_z, dot_nt(slot_at, query_t).astype(BF16)).astype(BF16)

    def normalize(src, inv_ref, dst):
        total = jnp.zeros((ROWS, 1), F32)
        for k in range(CHUNKS):
            v = src[:, k * CW : (k + 1) * CW]
            total += jnp.sum(v * v, axis=1, keepdims=True)
        inv = 1.0 / jnp.sqrt(total + epsilon)
        inv_ref[...] = jnp.broadcast_to(inv, (ROWS, 128))
        at = pl.ds(pl.multiple_of(z * ROWS, ROWS), ROWS)
        for k in range(CHUNKS):
            dst[k, at, :] = (src[:, k * CW : (k + 1) * CW] * inv).astype(BF16)

    p_in.wait()
    normalize(pf, pinv, pall)
    pl.semaphore_wait(barrier, len(peers) + len(mates))
    to_plane(e_send, e_recv, t_s.at[0], t_r.at[0], MSG)
    gather_start(pall, 0, 0)
    gather_start(pall, 1, 1)
    to_mates(f_send, f_recv, t_s.at[1], t_r.at[1], ROWS)
    keep(e_send, e_recv, dp, MSG)
    keep(f_send, f_recv, z, ROWS)
    q_in.wait()
    normalize(qf, qinv, qall)
    sacc[...] = jnp.zeros_like(sacc)
    hacc[...] = jnp.zeros_like(hacc)

    landed(e_recv, SLOTS - MSG, t_r.at[0])
    asked = e_recv[...]
    row_z = (iota((SLOTS, ROWS), 0) // CAP) % N_SUB
    for b in range(N_SUB):
        es[:, b * ROWS : (b + 1) * ROWS] = jnp.where(row_z == b, asked, jnp.zeros_like(asked))

    mine = pl.ds(pl.multiple_of(z * ROWS, ROWS), ROWS)

    def serve_passages(k, carry):
        landed(pall.at[k], GROUP - ROWS, ag_r.at[k])

        @pl.when(k + 2 < CHUNKS)
        def _():
            gather_start(pall, k + 2, k + 2)

        @pl.when(k + 2 >= CHUNKS)
        def _():
            gather_start(qall, k + 2 - CHUNKS, k + 2)

        s1[k] = dot(es[...], pall[k]).astype(BF16)
        to_plane(s1.at[k], r1.at[k], s1_s.at[k], s1_r.at[k], MSG)
        keep(s1.at[k], r1.at[k], dp, MSG)
        sacc[...] += dot_nt(qall[k, mine, :], pall[k])
        return carry

    lax.fori_loop(0, CHUNKS, serve_passages, 0)

    landed(f_recv, GROUP - ROWS, t_r.at[1])
    for b in range(N_SUB):
        ri = iota((SLOTS, ROWS), 0)
        ci = iota((SLOTS, ROWS), 1)
        spread = one_hot((ri // MSG == ci // CAP) & ((ri // CAP) % N_SUB == b) & (ri % CAP == ci % CAP))
        fs[:, b * ROWS : (b + 1) * ROWS] = dot(spread, f_recv[b * ROWS : (b + 1) * ROWS, :]).astype(BF16)

    def serve_queries(k, carry):
        landed(qall.at[k], GROUP - ROWS, ag_r.at[k + CHUNKS])

        @pl.when(k + 2 < CHUNKS)
        def _():
            gather_start(qall, k + 2, k + 2 + CHUNKS)

        s2[k] = dot(fs[...], qall[k]).astype(BF16)
        to_plane(s2.at[k], r2.at[k], s2_s.at[k], s2_r.at[k], MSG)
        keep(s2.at[k], r2.at[k], dp, MSG)
        landed(r1.at[k], SLOTS - MSG, s1_r.at[k])
        hacc[...] += dot_nt(qall[k, mine, :], r1[k])
        return carry

    lax.fori_loop(0, CHUNKS, serve_queries, 0)

    scores = sacc[...] / sharpness_divisor
    exp_batch = jnp.exp(scores)
    exp_hard = jnp.where(ftm[...] > 0.5, jnp.exp(hacc[...] / sharpness_divisor), 0.0)
    total = jnp.sum(exp_batch, axis=1, keepdims=True) + jnp.sum(exp_hard, axis=1, keepdims=True)
    diagonal = iota((ROWS, GROUP), 1) == iota((ROWS, GROUP), 0) + z * ROWS
    positive = jnp.sum(jnp.where(diagonal, scores, 0.0), axis=1, keepdims=True)
    loss_part = jnp.sum(jnp.log(total) - positive, axis=0, keepdims=True)
    l1_send[...] = jnp.broadcast_to(loss_part, (8, 128))
    batch_coef = (exp_batch / total - jnp.where(diagonal, 1.0, 0.0)).astype(BF16)
    hard_coef = (exp_hard / total).astype(BF16)
    cbm[...] = batch_coef
    chm[...] = hard_coef
    for b in range(N_SUB):
        cb_send[b * ROWS : (b + 1) * ROWS, :] = batch_coef[:, b * ROWS : (b + 1) * ROWS]
    spread_coef = lax.dot_general(
        hard_coef, jnp.ones((ROWS, ROWS), BF16), (((0,), (0,)), ((), ())), preferred_element_type=F32
    )
    weighted = (spread_coef * e_send[...].astype(F32)).astype(BF16)
    rz = iota((SLOTS, SLOTS), 0)
    cz = iota((SLOTS, SLOTS), 1)
    by_z = one_hot((rz // ROWS == (cz // CAP) % N_SUB) & ((rz // CAP) % N_DP == cz // MSG) & (rz % CAP == cz % CAP))
    g_send[...] = dot(by_z, weighted).astype(BF16)
    to_mates(g_send, g_recv, t_s.at[2], t_r.at[2], ROWS)
    to_mates(cb_send, cb_recv, t_s.at[3], t_r.at[3], ROWS)
    for mate in mates:
        pltpu.make_async_remote_copy(
            src_ref=l1_send, dst_ref=l1_recv.at[z], send_sem=t_s.at[4], recv_sem=t_r.at[4],
            device_id=(dp, mate), device_id_type=MESH,
        ).start()
    keep(g_send, g_recv, z, ROWS)
    keep(cb_send, cb_recv, z, ROWS)
    l1_recv[z] = l1_send[...]

    landed(g_recv, GROUP - ROWS, t_r.at[2])
    by_dp = one_hot((cz // ROWS == (rz // CAP) % N_SUB) & ((cz // CAP) % N_DP == rz // MSG) & (rz % CAP == cz % CAP))
    w_send[...] = dot(by_dp, g_recv[...]).astype(BF16)
    to_plane(w_send, w_recv, t_s.at[5], t_r.at[5], MSG)
    keep(w_send, w_recv, dp, MSG)
    landed(l1_recv, N_SUB - 1, t_r.at[4])
    l2_send[...] = l1_recv[0] + l1_recv[1] + l1_recv[2] + l1_recv[3]
    for peer in peers:
        pltpu.make_async_remote_copy(
            src_ref=l2_send, dst_ref=l2_recv.at[dp], send_sem=t_s.at[6], recv_sem=t_r.at[6],
            device_id=(peer, z), device_id_type=MESH,
        ).start()
    l2_recv[dp] = l2_send[...]

    scale = 1.0 / sharpness_divisor
    inv = qinv[:, :1]
    inner = jnp.zeros((ROWS, 1), F32)
    for k in range(CHUNKS):
        cols = slice(k * CW, (k + 1) * CW)
        grad = (dot(cbm[...], pall[k]) + dot(chm[...], r1[k])) * scale
        qg[:, cols] = grad
        inner += jnp.sum(qf[:, cols] * inv * grad, axis=1, keepdims=True)
    for k in range(CHUNKS):
        cols = slice(k * CW, (k + 1) * CW)
        qg[:, cols] = (qg[:, cols] - qf[:, cols] * inv * inner) * inv
    q_out = pltpu.make_async_copy(qg, qg_hbm, out_sem.at[0])
    q_out.start()

    landed(cb_recv, GROUP - ROWS, t_r.at[3])
    cbt[...] = jnp.transpose(cb_recv[...].astype(F32)).astype(BF16)
    for k in range(CHUNKS):
        pg[:, k * CW : (k + 1) * CW] = dot(cbt[...], qall[k])
    landed(w_recv, SLOTS - MSG, t_r.at[5])
    wt[...] = jnp.transpose(w_recv[...].astype(F32)).astype(BF16)
    landed(l2_recv, N_DP - 1, t_r.at[6])
    loss_sum = l2_recv[0]
    for d in range(1, N_DP):
        loss_sum = loss_sum + l2_recv[d]
    loss_ref[...] = loss_sum / (ROWS * N_DP * N_SUB)

    inv = pinv[:, :1]
    inner = jnp.zeros((ROWS, 1), F32)
    for k in range(CHUNKS):
        cols = slice(k * CW, (k + 1) * CW)
        landed(r2.at[k], SLOTS - MSG, s2_r.at[k])
        grad = (pg[:, cols] + dot(wt[...], r2[k])) * scale
        pg[:, cols] = grad
        inner += jnp.sum(pf[:, cols] * inv * grad, axis=1, keepdims=True)
    for k in range(CHUNKS):
        cols = slice(k * CW, (k + 1) * CW)
        pg[:, cols] = (pg[:, cols] - pf[:, cols] * inv * inner) * inv
    p_out = pltpu.make_async_copy(pg, pg_hbm, out_sem.at[1])
    p_out.start()

    landed(e_send, SLOTS - MSG, t_s.at[0])
    landed(f_send, GROUP - ROWS, t_s.at[1])
    landed(g_send, GROUP - ROWS, t_s.at[2])
    landed(cb_send, GROUP - ROWS, t_s.at[3])
    landed(l1_recv, N_SUB - 1, t_s.at[4])
    landed(w_send, SLOTS - MSG, t_s.at[5])
    landed(l2_recv, N_DP - 1, t_s.at[6])

    def sent(k, carry):
        landed(pall.at[k], GROUP - ROWS, ag_s.at[k])
        landed(qall.at[k], GROUP - ROWS, ag_s.at[k + CHUNKS])
        landed(s1.at[k], SLOTS - MSG, s1_s.at[k])
        landed(s2.at[k], SLOTS - MSG, s2_s.at[k])
        return carry

    lax.fori_loop(0, CHUNKS, sent, 0)
    q_out.wait()
    p_out.wait()


def local(queries, passages, counts, hard_owner, hard_local):
    vmem = pl.BlockSpec(memory_space=pltpu.VMEM)
    any_space = pl.BlockSpec(memory_space=pl.ANY)
    dma = pltpu.SemaphoreType.DMA
    table = pltpu.VMEM((SLOTS, 128), BF16)
    chunked = pltpu.VMEM((CHUNKS, GROUP, CW), BF16)
    loss, query_grad, passage_grad = pl.pallas_call(
        kernel,
        out_shape=(
            jax.ShapeDtypeStruct((8, 128), F32),
            jax.ShapeDtypeStruct((ROWS, WIDTH), F32),
            jax.ShapeDtypeStruct((ROWS, WIDTH), F32),
        ),
        in_specs=[any_space, any_space, vmem, vmem, vmem],
        out_specs=(vmem, any_space, any_space),
        scratch_shapes=[
            pltpu.VMEM((ROWS, WIDTH), F32), pltpu.VMEM((ROWS, WIDTH), F32),
            chunked, chunked, chunked, chunked, chunked, chunked,
            table, table, table, table, table, table, table, table, table, table,
            pltpu.VMEM((8, 128), F32), pltpu.VMEM((N_SUB, 8, 128), F32),
            pltpu.VMEM((8, 128), F32), pltpu.VMEM((N_DP, 8, 128), F32),
            pltpu.VMEM((ROWS, WIDTH), F32), pltpu.VMEM((ROWS, WIDTH), F32),
            pltpu.VMEM((ROWS, GROUP), F32), pltpu.VMEM((ROWS, SLOTS), F32),
            pltpu.VMEM((SLOTS, GROUP), BF16), pltpu.VMEM((SLOTS, GROUP), BF16),
            pltpu.VMEM((ROWS, SLOTS), F32), pltpu.VMEM((ROWS, SLOTS), BF16), pltpu.VMEM((ROWS, GROUP), BF16),
            pltpu.VMEM((ROWS, SLOTS), BF16), pltpu.VMEM((ROWS, GROUP), BF16),
            pltpu.VMEM((ROWS, 128), F32), pltpu.VMEM((ROWS, 128), F32),
            dma((2,)), dma((2,)), dma((2 * CHUNKS,)), dma((2 * CHUNKS,)),
            dma((CHUNKS,)), dma((CHUNKS,)), dma((CHUNKS,)), dma((CHUNKS,)), dma((7,)), dma((7,)),
        ],
        compiler_params=pltpu.CompilerParams(
            collective_id=0, has_side_effects=True, vmem_limit_bytes=58 * 2**20
        ),
        name="contrastive",
    )(passages, queries, counts, hard_owner.reshape(1, HARD), hard_local)
    return loss[0, 0], query_grad, passage_grad


def solution(mesh):
    in_specs = (
        P(("dp", "sub"), None),
        P(("dp", "sub"), None),
        P(("dp", "sub"), None),
        P(("dp", "sub"), None, None),
        P(("dp", "sub"), None),
    )
    out_specs = (P(), P(("dp", "sub"), None), P(("dp", "sub"), None))
    return jax.shard_map(local, mesh=mesh, in_specs=in_specs, out_specs=out_specs, check_vma=False)
```

```python
import jax
import jax.numpy as jnp
from jax import lax
from jax.experimental import pallas as pl
from jax.experimental.pallas import tpu as pltpu
from jax.sharding import PartitionSpec as P

MESH = pl.DeviceIdType.MESH
F32 = jnp.float32
BF16 = jnp.bfloat16

sharpness_divisor = 0.02
epsilon = 1e-06

ROWS = 128
WIDTH = 4096
HARD = 256
CAP = 4
N_SUB = 4
N_DP = 32
GROUP = ROWS * N_SUB
SLOTS = N_DP * N_SUB * CAP
MSG = N_SUB * CAP
CHUNKS = 8
CW = WIDTH // CHUNKS
HW = CW // 2
SIDE = 4


def dot(a, b):
    return lax.dot_general(a, b, (((1,), (0,)), ((), ())), preferred_element_type=F32)


def dot_nt(a, b):
    return lax.dot_general(a, b, (((1,), (1,)), ((), ())), preferred_element_type=F32)


def iota(shape, dim):
    return lax.broadcasted_iota(jnp.int32, shape, dim)


def one_hot(mask):
    return jnp.where(mask, 1.0, 0.0).astype(BF16)


def kernel(
    p_hbm, q_hbm, cnt_hbm, own_hbm, loc_hbm,
    loss_ref, qg, pg,
    cnt_ref, own_ref, loc_ref, pf, qf, pall, qall, s1, m1, r1, s2, m2, r2,
    e_send, e_recv, f_send, f_recv, cb_send, cb_recv, g_send, g_recv, w_send, w_recv,
    loss_send, loss_z, loss_x, loss_y, loss_c,
    sacc, hacc, es, fs, ftm, chm, cbm, wt, cbt, qinv, pinv,
    in_sem, sent, ag_r, a_r, b_r, t_s, t_r,
):
    dp = lax.axis_index("dp")
    z = lax.axis_index("sub")
    core = lax.rem(dp, 2)
    x = lax.rem(dp // 2, SIDE)
    y = dp // (2 * SIDE)
    mates = [lax.rem(z + d, N_SUB) for d in (1, 3, 2)]
    mates_x = [lax.rem(x + d, SIDE) for d in (1, 3, 2)]
    mates_y = [lax.rem(y + d, SIDE) for d in (1, 3, 2)]

    def at(x_, y_, c_):
        return ((y_ * SIDE + x_) * 2 + c_, z)

    def each_peer(body):
        def one(i, carry):
            body(lax.rem(dp + i, N_DP))
            return carry

        lax.fori_loop(1, N_DP, one, 0)

    def send(src, dst, send_sem, recv_sem, device):
        pltpu.make_async_remote_copy(
            src_ref=src, dst_ref=dst, send_sem=send_sem, recv_sem=recv_sem,
            device_id=device, device_id_type=MESH,
        ).start()

    def landed(part, sem):
        pltpu.make_async_copy(part, part, sem).wait()

    ints_in = [
        pltpu.make_async_copy(src, dst, in_sem.at[2 + i])
        for i, (src, dst) in enumerate(((cnt_hbm, cnt_ref), (own_hbm, own_ref), (loc_hbm, loc_ref)))
    ]
    p_in = pltpu.make_async_copy(p_hbm, pf, in_sem.at[0])
    q_in = pltpu.make_async_copy(q_hbm, qf, in_sem.at[1])
    for copy in (*ints_in, p_in):
        copy.start()

    barrier = pltpu.get_barrier_semaphore()
    each_peer(lambda peer: pl.semaphore_signal(barrier, inc=1, device_id=(peer, z), device_id_type=MESH))
    for mate in mates:
        pl.semaphore_signal(barrier, inc=1, device_id=(dp, mate), device_id_type=MESH)


    def span(index, rows):
        return pl.ds(pl.multiple_of(index * rows, rows), rows)

    def to_plane(src, dst, sem):
        each_peer(
            lambda peer: send(src.at[span(peer, MSG)], dst.at[span(dp, MSG)], t_s.at[sem], t_r.at[sem], (peer, z))
        )
        dst[span(dp, MSG), :] = src[span(dp, MSG), :]

    def to_mates(src, dst, sem):
        for mate in mates:
            send(src.at[span(mate, ROWS)], dst.at[span(z, ROWS)], t_s.at[sem], t_r.at[sem], (dp, mate))
        dst[span(z, ROWS), :] = src[span(z, ROWS), :]

    def gather_start(buf, k, which):
        mine = buf.at[k, span(z, ROWS)]
        for i in range(2):
            send(mine, mine, sent.at[which], ag_r.at[k, i], (dp, mates[i]))

    def gather_pass_on(buf, k, which):
        for i in range(2):
            landed(buf.at[k, pl.ds(0, ROWS)], ag_r.at[k, i])
            half = ROWS // 2
            part = buf.at[k, pl.ds(pl.multiple_of(mates[1 - i] * ROWS + i * half, half), half)]
            send(part, part, sent.at[which], ag_r.at[k, 2], (dp, mates[i]))

    def gather_done(buf, k):
        landed(buf.at[k, pl.ds(0, ROWS)], ag_r.at[k, 2])

    low, high = pl.ds(0, SIDE), pl.ds(SIDE, SIDE)

    def first_leg(src, mid, k, which):
        for i in range(3):
            send(src.at[k, low, mates_x[i]], mid.at[k, x], sent.at[which], a_r.at[k], at(mates_x[i], y, core))
            send(
                src.at[k, SIDE + mates_y[i]], mid.at[k, SIDE + y], sent.at[which], a_r.at[k], at(x, mates_y[i], core)
            )
        mid[k, x] = src[k, low, x]
        mid[k, SIDE + y] = src[k, SIDE + y]

    def second_leg(mid, dst, k, which):
        mine = span(core, MSG)
        other = span(1 - core, MSG)
        landed(mid.at[k, pl.ds(0, 6)], a_r.at[k])
        done = b_r.at[k + (which - 4) * CHUNKS]

        def pair(x_, y_, part, c):
            send(mid.at[k, low, y_, part], dst.at[k, y, :, mine], sent.at[which], done, at(x, y_, c))
            send(mid.at[k, high, x_, part], dst.at[k, high, x, mine], sent.at[which], done, at(x_, y, c))

        for i in range(3):
            pair(mates_x[i], mates_y[i], mine, core)
            pair(mates_x[i], mates_y[i], other, 1 - core)
        pair(x, y, other, 1 - core)
        dst[k, y, :, mine] = mid[k, low, y, mine]
        dst[k, high, x, mine] = mid[k, high, x, mine]

    def arrived(dst, k, which):
        landed(dst.at[k, pl.ds(0, 7)], b_r.at[k + (which - 4) * CHUNKS])

    def serve(table, buf, dst, k):
        rows = dot(table[...], buf[k]).astype(BF16)
        for h in range(2):
            dst[k, pl.ds(h * SIDE, SIDE)] = rows[:, h * HW : (h + 1) * HW].reshape(SIDE, SIDE, 2 * MSG, HW)

    def rows_of(buf, k, h):
        return buf[k, pl.ds(h * SIDE, SIDE)].reshape(SLOTS, HW)

    with jax.named_scope("integers_in"):
        for copy in ints_in:
            copy.wait()
    own_row = own_ref[...]
    loc_row = loc_ref[...]
    cnt_row = cnt_ref[...]
    square = (HARD, HARD)
    row_b = jnp.broadcast_to(own_row, square)
    own_col = jnp.sum(jnp.where(iota(square, 0) == iota(square, 1), row_b, 0), axis=1, keepdims=True)
    earlier = (own_col == row_b) & (iota(square, 0) < iota(square, 1))
    rank = jnp.sum(jnp.where(earlier, 1, 0), axis=0, keepdims=True)
    place = own_row * CAP + rank
    slot_at = one_hot(iota((SLOTS, HARD), 0) == place)
    local_t = one_hot(iota((ROWS, HARD), 0) == loc_row)
    cnt_b = jnp.broadcast_to(cnt_row, (ROWS, ROWS))
    upto = iota((ROWS, ROWS), 1) <= iota((ROWS, ROWS), 0)
    before = iota((ROWS, ROWS), 1) < iota((ROWS, ROWS), 0)
    ends = jnp.sum(jnp.where(upto, cnt_b, 0), axis=1, keepdims=True)
    starts = jnp.sum(jnp.where(before, cnt_b, 0), axis=1, keepdims=True)
    slot_id = iota((ROWS, HARD), 1)
    query_t = one_hot((slot_id >= starts) & (slot_id < ends))
    e_send[...] = dot_nt(slot_at, local_t).astype(BF16)

    def normalize(src, inv_ref, dst):
        total = jnp.zeros((ROWS, 1), F32)
        for k in range(CHUNKS):
            v = src[:, k * CW : (k + 1) * CW]
            total += jnp.sum(v * v, axis=1, keepdims=True)
        inv = 1.0 / jnp.sqrt(total + epsilon)
        inv_ref[...] = jnp.broadcast_to(inv, (ROWS, 128))
        for k in range(CHUNKS):
            dst[k, span(z, ROWS), :] = (src[:, k * CW : (k + 1) * CW] * inv).astype(BF16)

    with jax.named_scope("entry_barrier"):
        pl.semaphore_wait(barrier, N_DP - 1 + N_SUB - 1)
    to_plane(e_send, e_recv, 0)
    with jax.named_scope("passages_in"):
        p_in.wait()
    q_in.start()
    normalize(pf, pinv, pall)
    gather_start(pall, 0, 0)

    def by_z():
        r, c = iota((SLOTS, SLOTS), 0), iota((SLOTS, SLOTS), 1)
        return one_hot((r // ROWS == (c // CAP) % N_SUB) & ((r // CAP) % N_DP == c // MSG) & (r % CAP == c % CAP))

    def by_dp():
        r, c = iota((SLOTS, SLOTS), 0), iota((SLOTS, SLOTS), 1)
        return one_hot((c // ROWS == (r // CAP) % N_SUB) & ((c // CAP) % N_DP == r // MSG) & (r % CAP == c % CAP))

    ftm[...] = dot_nt(query_t, slot_at)
    f_send[...] = dot(by_z(), dot_nt(slot_at, query_t).astype(BF16)).astype(BF16)
    to_mates(f_send, f_recv, 1)
    q_in.wait()
    normalize(qf, qinv, qall)
    sacc[...] = jnp.zeros_like(sacc)
    hacc[...] = jnp.zeros_like(hacc)

    landed(e_recv.at[pl.ds(0, SLOTS - MSG)], t_r.at[0])
    asked = e_recv[...]
    row_z = (iota((SLOTS, ROWS), 0) // CAP) % N_SUB
    for b in range(N_SUB):
        es[:, b * ROWS : (b + 1) * ROWS] = jnp.where(row_z == b, asked, jnp.zeros_like(asked))

    others = pl.ds(0, GROUP - ROWS)
    gather_pass_on(pall, 0, 0)
    gather_start(pall, 1, 0)
    gather_start(pall, 2, 0)

    def serve_passages(k, carry):
        gather_done(pall, k)
        serve(es, pall, s1, k)
        first_leg(s1, m1, k, 2)

        @pl.when(k + 1 < CHUNKS)
        def _():
            gather_pass_on(pall, k + 1, 0)

        @pl.when(k + 1 == CHUNKS)
        def _():
            gather_pass_on(qall, 0, 1)

        @pl.when(k + 3 < CHUNKS)
        def _():
            gather_start(pall, k + 3, 0)

        @pl.when(k + 3 >= CHUNKS)
        def _():
            gather_start(qall, k + 3 - CHUNKS, 1)

        @pl.when(k > 0)
        def _():
            second_leg(m1, r1, k - 1, 4)

        sacc[...] += dot_nt(qall[k, span(z, ROWS), :], pall[k])
        return carry

    lax.fori_loop(0, CHUNKS, serve_passages, 0)

    landed(f_recv.at[others], t_r.at[1])
    for b in range(N_SUB):
        ri = iota((SLOTS, ROWS), 0)
        ci = iota((SLOTS, ROWS), 1)
        spread = one_hot((ri // MSG == ci // CAP) & ((ri // CAP) % N_SUB == b) & (ri % CAP == ci % CAP))
        fs[:, b * ROWS : (b + 1) * ROWS] = dot(spread, f_recv[b * ROWS : (b + 1) * ROWS, :]).astype(BF16)

    def serve_queries(k, carry):
        gather_done(qall, k)
        serve(fs, qall, s2, k)
        first_leg(s2, m2, k, 3)

        @pl.when(k + 1 < CHUNKS)
        def _():
            gather_pass_on(qall, k + 1, 1)

        @pl.when(k + 3 < CHUNKS)
        def _():
            gather_start(qall, k + 3, 1)

        @pl.when(k == 0)
        def _():
            second_leg(m1, r1, CHUNKS - 1, 4)

        @pl.when(k > 0)
        def _():
            second_leg(m2, r2, k - 1, 5)

        return carry

    def score_hard(k):
        arrived(r1, k, 4)
        for h in range(2):
            hacc[...] += dot_nt(qall[k, span(z, ROWS), h * HW : (h + 1) * HW], rows_of(r1, k, h))

    def serve_and_score(k, carry):
        serve_queries(k, carry)
        score_hard(2 * k)
        score_hard(2 * k + 1)
        return carry

    half = CHUNKS // 2
    lax.fori_loop(0, half, serve_and_score, 0)

    scores = sacc[...] / sharpness_divisor
    exp_batch = jnp.exp(scores)
    exp_hard = jnp.where(ftm[...] > 0.5, jnp.exp(hacc[...] / sharpness_divisor), 0.0)
    total = jnp.sum(exp_batch, axis=1, keepdims=True) + jnp.sum(exp_hard, axis=1, keepdims=True)
    diagonal = iota((ROWS, GROUP), 1) == iota((ROWS, GROUP), 0) + z * ROWS
    positive = jnp.sum(jnp.where(diagonal, scores, 0.0), axis=1, keepdims=True)
    loss_part = jnp.sum(jnp.log(total) - positive, axis=0, keepdims=True)
    loss_send[...] = jnp.broadcast_to(loss_part, (8, 128))
    batch_coef = (exp_batch / total - jnp.where(diagonal, 1.0, 0.0)).astype(BF16)
    hard_coef = (exp_hard / total).astype(BF16)
    cbm[...] = batch_coef
    chm[...] = hard_coef
    for b in range(N_SUB):
        cb_send[b * ROWS : (b + 1) * ROWS, :] = batch_coef[:, b * ROWS : (b + 1) * ROWS]
    spread_coef = lax.dot_general(
        hard_coef, jnp.ones((ROWS, ROWS), BF16), (((0,), (0,)), ((), ())), preferred_element_type=F32
    )
    weighted = (spread_coef * e_send[...].astype(F32)).astype(BF16)
    g_send[...] = dot(by_z(), weighted).astype(BF16)
    to_mates(g_send, g_recv, 2)
    to_mates(cb_send, cb_recv, 3)

    def share_loss(dst, index, sem, devices):
        for device in devices:
            send(loss_send, dst.at[index], t_s.at[sem], t_r.at[sem], device)
        dst[index] = loss_send[...]

    def add_loss(src, sem, count):
        landed(src.at[pl.ds(0, count - 1)], t_r.at[sem])
        landed(src.at[pl.ds(0, count - 1)], t_s.at[sem])
        total = src[0]
        for i in range(1, count):
            total = total + src[i]
        loss_send[...] = total

    share_loss(loss_z, z, 4, [(dp, mate) for mate in mates])

    scale = 1.0 / sharpness_divisor

    def columns(k):
        return pl.ds(pl.multiple_of(k * CW, CW), CW)

    def query_terms(k):
        for h in range(2):
            cols = pl.ds(pl.multiple_of(k * CW + h * HW, HW), HW)
            batch = dot(cbm[...], pall[k, :, h * HW : (h + 1) * HW])
            qg[:, cols] = (batch + dot(chm[...], rows_of(r1, k, h))) * scale

    def serve_and_grad(k, carry):
        serve_queries(k, carry)
        query_terms(2 * k - CHUNKS)
        query_terms(2 * k - CHUNKS + 1)
        return carry

    middle = half + 2
    lax.fori_loop(half, middle, serve_and_grad, 0)

    landed(g_recv.at[others], t_r.at[2])
    w_send[...] = dot(by_dp(), g_recv[...]).astype(BF16)
    to_plane(w_send, w_recv, 5)
    add_loss(loss_z, 4, N_SUB)
    share_loss(loss_x, x, 6, [at(mate, y, core) for mate in mates_x])

    lax.fori_loop(middle, CHUNKS, serve_and_grad, 0)

    landed(cb_recv.at[others], t_r.at[3])
    cbt[...] = jnp.transpose(cb_recv[...].astype(F32)).astype(BF16)
    add_loss(loss_x, 6, SIDE)
    share_loss(loss_y, y, 7, [at(x, mate, core) for mate in mates_y])
    second_leg(m2, r2, CHUNKS - 1, 5)

    inv = qinv[:, :1]
    inner = jnp.zeros((ROWS, 1), F32)
    for k in range(CHUNKS):
        inner += jnp.sum(qf[:, columns(k)] * inv * qg[:, columns(k)], axis=1, keepdims=True)
    for k in range(CHUNKS):
        qg[:, columns(k)] = (qg[:, columns(k)] - qf[:, columns(k)] * inv * inner) * inv

    add_loss(loss_y, 7, SIDE)
    share_loss(loss_c, core, 8, [at(x, y, 1 - core)])
    for k in range(CHUNKS):
        pg[:, columns(k)] = dot(cbt[...], qall[k])
    landed(w_recv.at[pl.ds(0, SLOTS - MSG)], t_r.at[5])
    wt[...] = jnp.transpose(w_recv[...].astype(F32)).astype(BF16)
    add_loss(loss_c, 8, 2)
    loss_ref[...] = loss_send[...] / (ROWS * N_DP * N_SUB)

    inv = pinv[:, :1]
    inner = jnp.zeros((ROWS, 1), F32)
    for k in range(CHUNKS):
        arrived(r2, k, 5)
        for h in range(2):
            cols = slice(k * CW + h * HW, k * CW + (h + 1) * HW)
            grad = (pg[:, cols] + dot(wt[...], rows_of(r2, k, h))) * scale
            pg[:, cols] = grad
            inner += jnp.sum(pf[:, cols] * inv * grad, axis=1, keepdims=True)
    for k in range(CHUNKS):
        pg[:, columns(k)] = (pg[:, columns(k)] - pf[:, columns(k)] * inv * inner) * inv

    landed(e_send.at[pl.ds(0, SLOTS - MSG)], t_s.at[0])
    landed(f_send.at[others], t_s.at[1])
    landed(g_send.at[others], t_s.at[2])
    landed(cb_send.at[others], t_s.at[3])
    landed(w_send.at[pl.ds(0, SLOTS - MSG)], t_s.at[5])
    for i, part in enumerate((pall, qall, m1, m2)):
        landed(part.at[pl.ds(0, 6)], sent.at[i])
    for i, part in enumerate((m1, m2)):
        landed(part.at[pl.ds(0, 7)], sent.at[4 + i])


def write_out(loss_in, q_in, p_in, loss_ref, q_hbm, p_hbm, sem):
    copies = [
        pltpu.make_async_copy(src.at[pl.ds(i * 32, 32)], dst.at[pl.ds(i * 32, 32)], sem.at[j, i])
        for j, (src, dst) in enumerate(((q_in, q_hbm), (p_in, p_hbm)))
        for i in range(4)
    ]
    for copy in copies:
        copy.start()
    loss_ref[0, 0] = loss_in[0, 0]
    for copy in copies:
        copy.wait()


def local(queries, passages, counts, hard_owner, hard_local):
    vmem = pl.BlockSpec(memory_space=pltpu.VMEM)
    any_space = pl.BlockSpec(memory_space=pl.ANY)
    hbm = pl.BlockSpec(memory_space=pltpu.HBM)
    dma = pltpu.SemaphoreType.DMA
    table = pltpu.VMEM((SLOTS, 128), BF16)
    chunked = pltpu.VMEM((CHUNKS, GROUP, CW), BF16)
    routed = pltpu.VMEM((CHUNKS, 2 * SIDE, SIDE, 2 * MSG, HW), BF16)
    grad = pltpu.VMEM((ROWS, WIDTH), F32)
    loss, query_grad, passage_grad = pl.pallas_call(
        kernel,
        out_shape=(pltpu.VMEM((8, 128), F32), grad, grad),
        in_specs=[hbm] * 5,
        out_specs=(vmem, vmem, vmem),
        scratch_shapes=[
            pltpu.VMEM((1, ROWS), jnp.int32), pltpu.VMEM((1, HARD), jnp.int32), pltpu.VMEM((1, HARD), jnp.int32),
            pltpu.VMEM((ROWS, WIDTH), F32), pltpu.VMEM((ROWS, WIDTH), F32),
            chunked, chunked, routed, routed, routed, routed, routed, routed,
            table, table, table, table, table, table, table, table, table, table,
            pltpu.VMEM((8, 128), F32), pltpu.VMEM((N_SUB, 8, 128), F32),
            pltpu.VMEM((SIDE, 8, 128), F32), pltpu.VMEM((SIDE, 8, 128), F32), pltpu.VMEM((2, 8, 128), F32),
            pltpu.VMEM((ROWS, GROUP), F32), pltpu.VMEM((ROWS, SLOTS), F32),
            pltpu.VMEM((SLOTS, GROUP), BF16), pltpu.VMEM((SLOTS, GROUP), BF16),
            pltpu.VMEM((ROWS, SLOTS), F32), pltpu.VMEM((ROWS, SLOTS), BF16), pltpu.VMEM((ROWS, GROUP), BF16),
            pltpu.VMEM((ROWS, SLOTS), BF16), pltpu.VMEM((ROWS, GROUP), BF16),
            pltpu.VMEM((ROWS, 128), F32), pltpu.VMEM((ROWS, 128), F32),
            dma((5,)), dma((6,)), dma((CHUNKS, 3)), dma((CHUNKS,)), dma((2 * CHUNKS,)), dma((9,)), dma((9,)),
        ],
        compiler_params=pltpu.CompilerParams(
            collective_id=0, has_side_effects=True, vmem_limit_bytes=48 * 2**20
        ),
        name="contrastive",
    )(*[
        pltpu.with_memory_space_constraint(v, pltpu.HBM)
        for v in (passages, queries, counts, hard_owner.reshape(1, HARD), hard_local)
    ])
    held = [pltpu.with_memory_space_constraint(v, pltpu.VMEM) for v in (loss, query_grad, passage_grad)]
    loss, query_grad, passage_grad = pl.pallas_call(
        write_out,
        out_shape=(
            jax.ShapeDtypeStruct((1, 1), F32),
            jax.ShapeDtypeStruct((ROWS, WIDTH), F32),
            jax.ShapeDtypeStruct((ROWS, WIDTH), F32),
        ),
        in_specs=[vmem, vmem, vmem],
        out_specs=(pl.BlockSpec(memory_space=pltpu.SMEM), any_space, any_space),
        scratch_shapes=[dma((2, 4))],
        compiler_params=pltpu.CompilerParams(vmem_limit_bytes=8 * 2**20),
        name="write_out",
    )(*held)
    return loss.reshape(()), query_grad, passage_grad


def solution(mesh):
    in_specs = (
        P(("dp", "sub"), None),
        P(("dp", "sub"), None),
        P(("dp", "sub"), None),
        P(("dp", "sub"), None, None),
        P(("dp", "sub"), None),
    )
    out_specs = (P(), P(("dp", "sub"), None), P(("dp", "sub"), None))
    return jax.shard_map(local, mesh=mesh, in_specs=in_specs, out_specs=out_specs, check_vma=False)
```

```python
import jax
import jax.numpy as jnp
from jax import lax
from jax.experimental import pallas as pl
from jax.experimental.pallas import tpu as pltpu
from jax.sharding import PartitionSpec as P

MESH = pl.DeviceIdType.MESH
F32 = jnp.float32
BF16 = jnp.bfloat16

sharpness_divisor = 0.02
epsilon = 1e-06

ROWS = 128
WIDTH = 4096
HARD = 256
CAP = 4
N_SUB = 4
N_DP = 32
SIDE = 4
GROUP = ROWS * N_SUB
SLOTS = N_DP * N_SUB * CAP
MSG = N_SUB * CAP
HALVES = 2
SLICES = 4
CW = WIDTH // (HALVES * SLICES)
HW = CW // 2
ITEMS = 16


def dot(a, b):
    return lax.dot_general(a, b, (((1,), (0,)), ((), ())), preferred_element_type=F32)


def dot_nt(a, b):
    return lax.dot_general(a, b, (((1,), (1,)), ((), ())), preferred_element_type=F32)


def iota(shape, dim):
    return lax.broadcasted_iota(jnp.int32, shape, dim)


def one_hot(mask):
    return jnp.where(mask, 1.0, 0.0).astype(BF16)


def columns(a, j):
    start = (j * HALVES + a) * CW
    return slice(start, start + CW)


def block(j):
    return slice(j * ROWS, (j + 1) * ROWS)


def kernel(
    p_hbm, q_hbm, cnt_hbm, own_hbm, loc_hbm,
    loss_ref, qg, pacc, pf, stats,
    cnt_ref, own_ref, loc_ref, qf, pall, qall, sbuf, mbuf, rbuf,
    e_send, e_recv, e_own, f_send, f_recv, cb_send, cb_recv, g_send, g_recv, w_send, w_recv,
    loss_send, loss_z, loss_x, loss_y, loss_c,
    sacc, hacc, es, fs, fk, ft, cbm, cbt, qinv,
    in_sem, sent, ag_r, a_r, b_r, t_s, t_r,
):
    dp = lax.axis_index("dp")
    z = lax.axis_index("sub")
    core = lax.rem(dp, 2)
    x = lax.rem(dp // 2, SIDE)
    y = dp // (2 * SIDE)
    above, below = lax.rem(z + 1, N_SUB), lax.rem(z + 3, N_SUB)
    mates = [(e, lax.rem(z + e, N_SUB)) for e in (1, 3, 2)]
    mates_x = [lax.rem(x + d, SIDE) for d in (1, 3, 2)]
    mates_y = [lax.rem(y + d, SIDE) for d in (1, 3, 2)]

    def at(x_, y_, c_):
        return ((y_ * SIDE + x_) * 2 + c_, z)

    def each_peer(body):
        def one(i, carry):
            body(lax.rem(dp + i, N_DP))
            return carry

        lax.fori_loop(1, N_DP, one, 0)

    def send(src, dst, send_sem, recv_sem, device):
        pltpu.make_async_remote_copy(
            src_ref=src, dst_ref=dst, send_sem=send_sem, recv_sem=recv_sem,
            device_id=device, device_id_type=MESH,
        ).start()

    def landed(part, sem):
        pltpu.make_async_copy(part, part, sem).wait()

    ints_in = [
        pltpu.make_async_copy(src, dst, in_sem.at[2 + i])
        for i, (src, dst) in enumerate(((cnt_hbm, cnt_ref), (own_hbm, own_ref), (loc_hbm, loc_ref)))
    ]
    p_in = pltpu.make_async_copy(p_hbm, pf, in_sem.at[0])
    q_in = pltpu.make_async_copy(q_hbm, qf, in_sem.at[1])
    for copy in (*ints_in, q_in):
        copy.start()

    barrier = pltpu.get_barrier_semaphore()
    each_peer(lambda peer: pl.semaphore_signal(barrier, inc=1, device_id=(peer, z), device_id_type=MESH))
    for _, mate in mates:
        pl.semaphore_signal(barrier, inc=1, device_id=(dp, mate), device_id_type=MESH)

    def span(index, rows):
        return pl.ds(pl.multiple_of(index * rows, rows), rows)

    def to_plane(src, dst, sem):
        each_peer(
            lambda peer: send(src.at[span(peer, MSG)], dst.at[span(dp, MSG)], t_s.at[sem], t_r.at[sem], (peer, z))
        )
        dst[span(dp, MSG), :] = src[span(dp, MSG), :]

    def to_mates(src, dst, sem):
        for e, mate in mates:
            send(
                src.at[pl.ds(e * ROWS, ROWS)], dst.at[pl.ds((N_SUB - e) * ROWS, ROWS)],
                t_s.at[sem], t_r.at[sem], (dp, mate),
            )
        dst[block(0), :] = src[block(0), :]

    def gather_start(buf, a, which):
        send(buf.at[0, a], buf.at[3, a], sent.at[which], ag_r.at[which, a, 0], (dp, above))
        send(buf.at[0, a], buf.at[1, a], sent.at[which], ag_r.at[which, a, 1], (dp, below))

    def gather_pass_on(buf, a, which):
        landed(buf.at[3, a], ag_r.at[which, a, 0])
        upper, lower = pl.ds(0, GROUP // 2), pl.ds(GROUP // 2, GROUP // 2)
        send(buf.at[3, a, upper], buf.at[2, a, upper], sent.at[which], ag_r.at[which, a, 2], (dp, above))
        landed(buf.at[1, a], ag_r.at[which, a, 1])
        send(buf.at[1, a, lower], buf.at[2, a, lower], sent.at[which], ag_r.at[which, a, 2], (dp, below))

    def gather_done(buf, a, which):
        landed(buf.at[2, a], ag_r.at[which, a, 2])

    low, high = pl.ds(0, SIDE), pl.ds(SIDE, SIDE)

    def first_leg(n):
        for i in range(3):
            send(sbuf.at[n, low, mates_x[i]], mbuf.at[n, x], sent.at[2], a_r.at[n], at(mates_x[i], y, core))
            send(sbuf.at[n, SIDE + mates_y[i]], mbuf.at[n, SIDE + y], sent.at[2], a_r.at[n], at(x, mates_y[i], core))
        mbuf[n, x] = sbuf[n, low, x]
        mbuf[n, SIDE + y] = sbuf[n, SIDE + y]

    def second_leg(n):
        mine = span(core, MSG)
        other = span(1 - core, MSG)
        landed(mbuf.at[n, pl.ds(0, 6)], a_r.at[n])

        def pair(x_, y_, part, c):
            send(mbuf.at[n, low, y_, part], rbuf.at[n, y, :, mine], sent.at[3], b_r.at[n], at(x, y_, c))
            send(mbuf.at[n, high, x_, part], rbuf.at[n, high, x, mine], sent.at[3], b_r.at[n], at(x_, y, c))

        for i in range(3):
            pair(mates_x[i], mates_y[i], mine, core)
            pair(mates_x[i], mates_y[i], other, 1 - core)
        pair(x, y, other, 1 - core)
        rbuf[n, y, :, mine] = mbuf[n, low, y, mine]
        rbuf[n, high, x, mine] = mbuf[n, high, x, mine]

    def arrived(n):
        landed(rbuf.at[n, pl.ds(0, 7)], b_r.at[n])

    def serve(n, table, src):
        rows = dot(table, src).astype(BF16)
        for h in range(2):
            sbuf[n, pl.ds(h * SIDE, SIDE)] = rows[:, h * HW : (h + 1) * HW].reshape(SIDE, SIDE, 2 * MSG, HW)

    def rows_of(n):
        parts = [rbuf[n, pl.ds(h * SIDE, SIDE)].reshape(SLOTS, HW) for h in range(2)]
        return jnp.concatenate(parts, axis=1)

    def normalize(src, dst):
        total = jnp.zeros((ROWS, 1), F32)
        for a in range(HALVES):
            for j in range(SLICES):
                v = src[:, columns(a, j)]
                total += jnp.sum(v * v, axis=1, keepdims=True)
        inv = 1.0 / jnp.sqrt(total + epsilon)
        for a in range(HALVES):
            for j in range(SLICES):
                dst[0, a, block(j), :] = (src[:, columns(a, j)] * inv).astype(BF16)
        return jnp.broadcast_to(inv, (ROWS, 128))

    with jax.named_scope("integers_in"):
        for copy in ints_in:
            copy.wait()
    own_row = own_ref[...]
    loc_row = loc_ref[...]
    cnt_row = cnt_ref[...]
    square = (HARD, HARD)
    row_b = jnp.broadcast_to(own_row, square)
    own_col = jnp.sum(jnp.where(iota(square, 0) == iota(square, 1), row_b, 0), axis=1, keepdims=True)
    earlier = (own_col == row_b) & (iota(square, 0) < iota(square, 1))
    rank = jnp.sum(jnp.where(earlier, 1, 0), axis=0, keepdims=True)
    up = (own_row + (N_SUB - z)) % N_SUB
    owner_dp = own_row // N_SUB
    slot_by_up = one_hot(iota((SLOTS, HARD), 0) == up * ROWS + owner_dp * CAP + rank)
    slot_by_dp = one_hot(iota((SLOTS, HARD), 0) == owner_dp * MSG + up * CAP + rank)
    local_t = one_hot(iota((ROWS, HARD), 0) == loc_row)
    cnt_b = jnp.broadcast_to(cnt_row, (ROWS, ROWS))
    upto = iota((ROWS, ROWS), 1) <= iota((ROWS, ROWS), 0)
    before = iota((ROWS, ROWS), 1) < iota((ROWS, ROWS), 0)
    ends = jnp.sum(jnp.where(upto, cnt_b, 0), axis=1, keepdims=True)
    starts = jnp.sum(jnp.where(before, cnt_b, 0), axis=1, keepdims=True)
    slot_id = iota((ROWS, HARD), 1)
    query_t = one_hot((slot_id >= starts) & (slot_id < ends))

    def match(n_dp, n_mid, shape, dim):
        i = iota(shape, dim)
        return i // (n_mid * CAP), (i // CAP) % n_mid, i % CAP

    def spread():
        r = match(N_DP, SLICES, (SLOTS, ROWS), 0)
        c = match(N_DP, 1, (SLOTS, ROWS), 1)
        return one_hot((r[0] == c[0]) & (r[2] == c[2]))

    def spread_t():
        r = match(N_DP, 1, (ROWS, SLOTS), 0)
        c = match(N_DP, SLICES, (ROWS, SLOTS), 1)
        return one_hot((r[0] == c[0]) & (r[2] == c[2]))

    def by_slice(dst, d, rows):
        slice_of = (iota((SLOTS, ROWS), 0) // CAP) % SLICES
        rows = rows.astype(BF16)
        for j in range(SLICES):
            dst[d, :, block(j)] = jnp.where(slice_of == j, rows, jnp.zeros_like(rows))

    def by_slice_t(dst, d, rows):
        slice_of = (iota((ROWS, SLOTS), 1) // CAP) % SLICES
        rows = rows.astype(BF16)
        for j in range(SLICES):
            dst[d, block(j), :] = jnp.where(slice_of == j, rows, jnp.zeros_like(rows))

    f_send[...] = dot_nt(slot_by_up, query_t).astype(BF16)
    by_slice(fs, 0, dot(spread(), f_send[block(0), :]))

    with jax.named_scope("queries_in"):
        q_in.wait()
    p_in.start()
    qinv[...] = normalize(qf, qall)
    serve(0, fs[0], qall[0, 0])
    with jax.named_scope("entry_barrier"):
        pl.semaphore_wait(barrier, N_DP - 1 + N_SUB - 1)
    first_leg(0)
    e_send[...] = dot_nt(slot_by_dp, local_t).astype(BF16)
    to_plane(e_send, e_recv, 0)
    with jax.named_scope("passages_in"):
        p_in.wait()
    stats[0] = normalize(pf, pall)
    gather_start(pall, 0, 0)
    to_mates(f_send, f_recv, 1)
    serve(1, fs[0], qall[0, 1])
    first_leg(1)
    second_leg(0)
    second_leg(1)

    def asked_passages(d):
        r = match(N_DP, SLICES, (SLOTS, SLOTS), 0)
        c = match(N_DP, N_SUB, (SLOTS, SLOTS), 1)
        pick = one_hot((r[0] == c[0]) & (r[2] == c[2]) & (c[1] == d))
        by_slice(es, d, dot(pick, e_recv[...]))

    landed(e_recv.at[pl.ds(0, SLOTS - MSG)], t_r.at[0])
    asked_passages(0)

    def score_batch(d, a):
        part = jnp.zeros((ROWS, ROWS), F32)
        for j in range(SLICES):
            part += dot_nt(qall[0, a, block(j), :], pall[d, a, block(j), :])
        sacc[d] += part

    def score_hard(n, d, a):
        arrived(n)
        pairs = dot_nt(qall[0, a], rows_of(n)) * fk[d].astype(F32)
        hacc[pl.ds(d, 1), :] += jnp.sum(pairs, axis=0, keepdims=True)

    sacc[...] = jnp.zeros_like(sacc)
    hacc[...] = jnp.zeros_like(hacc)
    serve(2, es[0], pall[0, 0])
    first_leg(2)
    e_own[...] = dot_nt(slot_by_up, local_t).astype(BF16)
    for d in range(N_SUB):
        mine = dot_nt(query_t, slot_by_up[block(d), :])
        ft[d] = mine
        by_slice_t(fk, d, dot(mine.astype(BF16), spread_t()))
    gather_pass_on(pall, 0, 0)
    gather_start(pall, 1, 0)
    serve(3, es[0], pall[0, 1])
    first_leg(3)
    second_leg(2)
    for d in range(1, N_SUB):
        asked_passages(d)
    score_batch(0, 0)
    score_batch(0, 1)

    def turn(t):
        i = t % 3
        return 1 + 2 * i - 3 * (i // 2), t // 3, i

    def passages(t, carry):
        d, a, i = turn(t)

        @pl.when(i == 2)
        def _():
            gather_done(pall, a, 0)

        serve(4 + t, es[d], pall[d, a])
        first_leg(4 + t)
        second_leg(3 + t)
        score_batch(d, a)

        @pl.when(t == 2)
        def _():
            gather_pass_on(pall, 1, 0)
            gather_start(qall, 0, 1)

        @pl.when(t == 5)
        def _():
            gather_pass_on(qall, 0, 1)
            gather_start(qall, 1, 1)

        @pl.when((t == 1) | (t == 2))
        def _():
            score_hard(1 + t, 0, t - 1)

        @pl.when(t >= 3)
        def _():
            before_d, before_a, _ = turn(t - 3)
            score_hard(1 + t, before_d, before_a)

        return carry

    lax.fori_loop(0, 6, passages, 0)

    landed(f_recv.at[pl.ds(0, GROUP - ROWS)], t_r.at[1])
    for d in range(1, N_SUB):
        by_slice(fs, d, dot(spread(), f_recv[block(d), :]))

    def queries(t):
        d, a, i = turn(t)
        serve(10 + t, fs[d], qall[d, a])
        first_leg(10 + t)
        second_leg(9 + t)

    def queries_first(t, carry):
        @pl.when(t == 2)
        def _():
            gather_done(qall, 0, 1)

        queries(t)
        before_d, before_a, _ = turn(t + 3)
        score_hard(7 + t, before_d, before_a)
        return carry

    lax.fori_loop(0, 3, queries_first, 0)

    scores = [sacc[d] / sharpness_divisor for d in range(N_SUB)]
    exp_batch = [jnp.exp(v) for v in scores]
    fold = spread().astype(F32)
    hard_scores = (
        lax.dot_general(
            hacc[...], fold, (((1,), (0,)), ((), ())),
            precision=lax.Precision.HIGHEST, preferred_element_type=F32,
        )
        / sharpness_divisor
    )
    used = [jnp.sum(ft[d], axis=0, keepdims=True) for d in range(N_SUB)]
    exp_hard = [jnp.where(used[d] > 0.5, jnp.exp(hard_scores[d : d + 1, :]), 0.0) for d in range(N_SUB)]
    total = jnp.zeros((ROWS, 1), F32)
    for d in range(N_SUB):
        total += jnp.sum(exp_batch[d] + ft[d] * exp_hard[d], axis=1, keepdims=True)
    diagonal = iota((ROWS, ROWS), 1) == iota((ROWS, ROWS), 0)
    positive = jnp.sum(jnp.where(diagonal, scores[0], 0.0), axis=1, keepdims=True)
    loss_part = jnp.sum(jnp.log(total) - positive, axis=0, keepdims=True)
    loss_send[...] = jnp.broadcast_to(loss_part, (8, 128))
    for d in range(N_SUB):
        coef = exp_batch[d] / total
        if d == 0:
            coef = coef - jnp.where(diagonal, 1.0, 0.0)
        cb_send[block(d), :] = coef.astype(BF16)
        cbm[:, block(d)] = coef.astype(BF16)
        slot_total = jnp.sum(ft[d] * total, axis=0, keepdims=True) + (1.0 - used[d])
        hard_coef = (exp_hard[d] / slot_total).astype(BF16)
        hard_row = jnp.broadcast_to(hard_coef.astype(F32), (ROWS, ROWS))
        hard_col = jnp.sum(jnp.where(diagonal, hard_row, 0.0), axis=1, keepdims=True)
        g_send[block(d), :] = (hard_col * e_own[block(d), :].astype(F32)).astype(BF16)
        weight = dot(jnp.broadcast_to(hard_coef, (8, ROWS)), spread_t())[0:1, :]
        fk[d] = (fk[d].astype(F32) * weight).astype(BF16)
    to_mates(g_send, g_recv, 2)
    to_mates(cb_send, cb_recv, 3)

    def share_loss(dst, index, sem, devices):
        for device in devices:
            send(loss_send, dst.at[index], t_s.at[sem], t_r.at[sem], device)
        dst[index] = loss_send[...]

    def add_loss(src, sem, count):
        landed(src.at[pl.ds(0, count - 1)], t_r.at[sem])
        landed(src.at[pl.ds(0, count - 1)], t_s.at[sem])
        added = src[0]
        for i in range(1, count):
            added = added + src[i]
        loss_send[...] = added

    share_loss(loss_z, z, 4, [(dp, mate) for _, mate in mates])

    scale = 1.0 / sharpness_divisor

    def query_terms(a):
        grad = jnp.zeros((GROUP, CW), F32)
        for n, d in ((2 + a, 0), (4 + 3 * a, 1), (5 + 3 * a, 3), (6 + 3 * a, 2)):
            grad += dot(fk[d], rows_of(n))
        for j in range(SLICES):
            batch = dot(cbm[...], pall[:, a, block(j), :].reshape(GROUP, CW))
            qg[:, columns(a, j)] = (grad[block(j), :] + batch) * scale

    gather_pass_on(qall, 1, 1)
    queries(3)
    landed(g_recv.at[pl.ds(0, GROUP - ROWS)], t_r.at[2])
    r = match(N_DP, N_SUB, (SLOTS, SLOTS), 0)
    c = iota((SLOTS, SLOTS), 1)
    by_dp = one_hot((c // ROWS == r[1]) & ((c // CAP) % N_DP == r[0]) & (c % CAP == r[2]))
    w_send[...] = dot(by_dp, g_recv[...]).astype(BF16)
    to_plane(w_send, w_recv, 5)
    add_loss(loss_z, 4, N_SUB)
    share_loss(loss_x, x, 6, [at(mate, y, core) for mate in mates_x])
    query_terms(0)

    queries(4)
    query_terms(1)

    gather_done(qall, 1, 1)
    queries(5)
    add_loss(loss_x, 6, SIDE)
    share_loss(loss_y, y, 7, [at(x, mate, core) for mate in mates_y])

    landed(cb_recv.at[pl.ds(0, GROUP - ROWS)], t_r.at[3])
    cbt[...] = jnp.transpose(cb_recv[...].astype(F32)).astype(BF16)
    for a in range(HALVES):
        for j in range(SLICES):
            pacc[a, block(j), :] = dot(cbt[...], qall[:, a, block(j), :].reshape(GROUP, CW))

    landed(w_recv.at[pl.ds(0, SLOTS - MSG)], t_r.at[5])
    weights_t = jnp.transpose(w_recv[...].astype(F32)).astype(BF16)
    for d in range(N_SUB):
        r = match(N_DP, N_SUB, (SLOTS, SLOTS), 0)
        c = match(N_DP, SLICES, (SLOTS, SLOTS), 1)
        pick = one_hot((r[0] == c[0]) & (r[2] == c[2]) & (r[1] == d))
        by_slice_t(es, d, dot(weights_t, pick))

    def passage_terms(n, d, a):
        arrived(n)
        pacc[a] += dot(es[d], rows_of(n))

    passage_terms(0, 0, 0)
    second_leg(15)
    add_loss(loss_y, 7, SIDE)
    share_loss(loss_c, core, 8, [at(x, y, 1 - core)])
    passage_terms(1, 0, 1)

    inv = qinv[:, :1]
    inner = jnp.zeros((ROWS, 1), F32)
    for a in range(HALVES):
        for j in range(SLICES):
            inner += jnp.sum(qf[:, columns(a, j)] * inv * qg[:, columns(a, j)], axis=1, keepdims=True)
    for a in range(HALVES):
        for j in range(SLICES):
            cols = columns(a, j)
            qg[:, cols] = (qg[:, cols] - qf[:, cols] * inv * inner) * inv

    def more_passage_terms(t, carry):
        d, a, _ = turn(t)
        passage_terms(10 + t, d, a)
        return carry

    inv = stats[0, :, :1]

    def passage_inner(a):
        inner = jnp.zeros((ROWS, 1), F32)
        for j in range(SLICES):
            inner += jnp.sum(pf[:, columns(a, j)] * inv * pacc[a, block(j), :], axis=1, keepdims=True)
        return inner

    lax.fori_loop(0, 3, more_passage_terms, 0)
    first = passage_inner(0)
    add_loss(loss_c, 8, 2)
    loss_ref[...] = loss_send[...] / (ROWS * N_DP * N_SUB)
    lax.fori_loop(3, 6, more_passage_terms, 0)
    stats[1] = jnp.broadcast_to((first + passage_inner(1)) * scale, (ROWS, 128))

    landed(e_send.at[pl.ds(0, SLOTS - MSG)], t_s.at[0])
    landed(f_send.at[pl.ds(0, GROUP - ROWS)], t_s.at[1])
    landed(g_send.at[pl.ds(0, GROUP - ROWS)], t_s.at[2])
    landed(cb_send.at[pl.ds(0, GROUP - ROWS)], t_s.at[3])
    landed(w_send.at[pl.ds(0, SLOTS - MSG)], t_s.at[5])
    landed(pall.at[pl.ds(0, 3)], sent.at[0])
    landed(qall.at[pl.ds(0, 3)], sent.at[1])
    landed(mbuf.at[pl.ds(0, 12)], sent.at[2])
    landed(mbuf.at[pl.ds(0, 14)], sent.at[3])


def write_out(loss_in, q_in, pacc, pf, stats, loss_ref, q_hbm, p_hbm, out, sem):
    copies = [
        pltpu.make_async_copy(q_in.at[pl.ds(i * 32, 32)], q_hbm.at[pl.ds(i * 32, 32)], sem.at[0, i])
        for i in range(4)
    ]
    for copy in copies:
        copy.start()
    loss_ref[0, 0] = loss_in[0, 0]
    scale = 1.0 / sharpness_divisor
    for i in range(4):
        rows = slice(i * 32, (i + 1) * 32)
        inv = stats[0, rows, :1]
        inner = stats[1, rows, :1]
        for a in range(HALVES):
            for j in range(SLICES):
                cols = columns(a, j)
                grad = pacc[a, j * ROWS + i * 32 : j * ROWS + (i + 1) * 32, :] * scale
                out[rows, cols] = (grad - pf[rows, cols] * inv * inner) * inv
        copy = pltpu.make_async_copy(out.at[pl.ds(i * 32, 32)], p_hbm.at[pl.ds(i * 32, 32)], sem.at[1, i])
        copy.start()
        copies.append(copy)
    for copy in copies:
        copy.wait()


def local(queries, passages, counts, hard_owner, hard_local):
    vmem = pl.BlockSpec(memory_space=pltpu.VMEM)
    any_space = pl.BlockSpec(memory_space=pl.ANY)
    hbm = pl.BlockSpec(memory_space=pltpu.HBM)
    dma = pltpu.SemaphoreType.DMA
    table = pltpu.VMEM((SLOTS, 128), BF16)
    gathered = pltpu.VMEM((N_SUB, HALVES, GROUP, CW), BF16)
    routed = pltpu.VMEM((ITEMS, 2 * SIDE, SIDE, 2 * MSG, HW), BF16)
    masks = pltpu.VMEM((N_SUB, SLOTS, GROUP), BF16)
    one_loss = pltpu.VMEM((8, 128), F32)
    rows = pltpu.VMEM((ROWS, WIDTH), F32)
    held = pl.pallas_call(
        kernel,
        out_shape=(
            one_loss, rows, pltpu.VMEM((HALVES, GROUP, CW), F32), rows, pltpu.VMEM((2, ROWS, 128), F32),
        ),
        in_specs=[hbm] * 5,
        out_specs=(vmem,) * 5,
        scratch_shapes=[
            pltpu.VMEM((1, ROWS), jnp.int32), pltpu.VMEM((1, HARD), jnp.int32), pltpu.VMEM((1, HARD), jnp.int32),
            rows, gathered, gathered, routed, routed, routed,
            table, table, table, table, table, table, table, table, table, table, table,
            one_loss, pltpu.VMEM((N_SUB, 8, 128), F32),
            pltpu.VMEM((SIDE, 8, 128), F32), pltpu.VMEM((SIDE, 8, 128), F32), pltpu.VMEM((2, 8, 128), F32),
            pltpu.VMEM((N_SUB, ROWS, ROWS), F32), pltpu.VMEM((8, SLOTS), F32), masks, masks, masks,
            pltpu.VMEM((N_SUB, ROWS, ROWS), F32), pltpu.VMEM((ROWS, GROUP), BF16), pltpu.VMEM((ROWS, GROUP), BF16),
            pltpu.VMEM((ROWS, 128), F32),
            dma((5,)), dma((4,)), dma((2, HALVES, 3)), dma((ITEMS,)), dma((ITEMS,)), dma((9,)), dma((9,)),
        ],
        compiler_params=pltpu.CompilerParams(
            collective_id=0, has_side_effects=True, vmem_limit_bytes=53 * 2**20
        ),
        name="contrastive",
    )(*[
        pltpu.with_memory_space_constraint(v, pltpu.HBM)
        for v in (passages, queries, counts, hard_owner.reshape(1, HARD), hard_local)
    ])
    loss, query_grad, passage_grad = pl.pallas_call(
        write_out,
        out_shape=(
            jax.ShapeDtypeStruct((1, 1), F32),
            jax.ShapeDtypeStruct((ROWS, WIDTH), F32),
            jax.ShapeDtypeStruct((ROWS, WIDTH), F32),
        ),
        in_specs=[vmem] * 5,
        out_specs=(pl.BlockSpec(memory_space=pltpu.SMEM), any_space, any_space),
        scratch_shapes=[rows, dma((2, 4))],
        compiler_params=pltpu.CompilerParams(vmem_limit_bytes=8 * 2**20),
        name="write_out",
    )(*[pltpu.with_memory_space_constraint(v, pltpu.VMEM) for v in held])
    return loss.reshape(()), query_grad, passage_grad


def solution(mesh):
    in_specs = (
        P(("dp", "sub"), None),
        P(("dp", "sub"), None),
        P(("dp", "sub"), None),
        P(("dp", "sub"), None, None),
        P(("dp", "sub"), None),
    )
    out_specs = (P(), P(("dp", "sub"), None), P(("dp", "sub"), None))
    return jax.shard_map(local, mesh=mesh, in_specs=in_specs, out_specs=out_specs, check_vma=False)
```

```python
import jax
import jax.numpy as jnp
from jax import lax
from jax.experimental import pallas as pl
from jax.experimental.pallas import tpu as pltpu
from jax.sharding import PartitionSpec as P

MESH = pl.DeviceIdType.MESH
F32 = jnp.float32
BF16 = jnp.bfloat16

sharpness_divisor = 0.02
epsilon = 1e-06

ROWS = 128
WIDTH = 4096
HARD = 256
CAP = 4
N_SUB = 4
N_DP = 32
SIDE = 4
GROUP = ROWS * N_SUB
SLOTS = N_DP * N_SUB * CAP
MSG = N_SUB * CAP
HALVES = 2
SLICES = 4
CW = WIDTH // (HALVES * SLICES)
HW = CW // 2
ITEMS = 16


def dot(a, b):
    return lax.dot_general(a, b, (((1,), (0,)), ((), ())), preferred_element_type=F32)


def dot_nt(a, b):
    return lax.dot_general(a, b, (((1,), (1,)), ((), ())), preferred_element_type=F32)


def iota(shape, dim):
    return lax.broadcasted_iota(jnp.int32, shape, dim)


def one_hot(mask):
    return jnp.where(mask, 1.0, 0.0).astype(BF16)


def columns(a, j):
    start = (j * HALVES + a) * CW
    return slice(start, start + CW)


def block(j):
    return slice(j * ROWS, (j + 1) * ROWS)


def kernel(
    p_hbm, q_hbm, cnt_hbm, own_hbm, loc_hbm,
    loss_ref, qg, pacc, pf, stats,
    cnt_ref, own_ref, loc_ref, qf, pall, qall, sbuf, mbuf, rbuf,
    e_send, e_recv, f_send, f_recv, cb_send, cb_recv, g_send, g_recv, w_send, w_recv,
    loss_send, loss_z, loss_x, loss_y, loss_c,
    sacc, hacc, es, fs, fk, ft, cbm, cbt, qinv,
    in_sem, sent, ag_r, a_r, b_r, t_s, t_r,
):
    dp = lax.axis_index("dp")
    z = lax.axis_index("sub")
    core = lax.rem(dp, 2)
    x = lax.rem(dp // 2, SIDE)
    y = dp // (2 * SIDE)
    above, below = lax.rem(z + 1, N_SUB), lax.rem(z + 3, N_SUB)
    mates = [(e, lax.rem(z + e, N_SUB)) for e in (1, 3, 2)]
    mates_x = [lax.rem(x + d, SIDE) for d in (2, 1, 3)]
    mates_y = [lax.rem(y + d, SIDE) for d in (2, 1, 3)]

    def at(x_, y_, c_):
        return ((y_ * SIDE + x_) * 2 + c_, z)

    def each_peer(body):
        def one(i, carry):
            body(lax.rem(dp + i, N_DP))
            return carry

        lax.fori_loop(1, N_DP, one, 0)

    def send(src, dst, send_sem, recv_sem, device):
        pltpu.make_async_remote_copy(
            src_ref=src, dst_ref=dst, send_sem=send_sem, recv_sem=recv_sem,
            device_id=device, device_id_type=MESH,
        ).start()

    def landed(part, sem):
        pltpu.make_async_copy(part, part, sem).wait()

    ints_in = [
        pltpu.make_async_copy(src, dst, in_sem.at[2 + i])
        for i, (src, dst) in enumerate(((cnt_hbm, cnt_ref), (own_hbm, own_ref), (loc_hbm, loc_ref)))
    ]
    p_in = pltpu.make_async_copy(p_hbm, pf, in_sem.at[0])
    q_in = pltpu.make_async_copy(q_hbm, qf, in_sem.at[1])
    for copy in (*ints_in, q_in):
        copy.start()

    barrier = pltpu.get_barrier_semaphore()
    each_peer(lambda peer: pl.semaphore_signal(barrier, inc=1, device_id=(peer, z), device_id_type=MESH))
    for _, mate in mates:
        pl.semaphore_signal(barrier, inc=1, device_id=(dp, mate), device_id_type=MESH)

    def span(index, rows):
        return pl.ds(pl.multiple_of(index * rows, rows), rows)

    def to_plane(src, dst, sem):
        each_peer(lambda peer: send(src.at[peer], dst.at[dp], t_s.at[sem], t_r.at[sem], (peer, z)))
        dst[dp] = src[dp]

    def to_mates(src, dst, sem):
        for e, mate in mates:
            send(
                src.at[pl.ds(e * ROWS, ROWS)], dst.at[pl.ds((N_SUB - e) * ROWS, ROWS)],
                t_s.at[sem], t_r.at[sem], (dp, mate),
            )
        dst[block(0), :] = src[block(0), :]

    def gather_start(buf, a, which):
        send(buf.at[0, a], buf.at[3, a], sent.at[which], ag_r.at[which, a, 0], (dp, above))
        send(buf.at[0, a], buf.at[1, a], sent.at[which], ag_r.at[which, a, 1], (dp, below))

    def gather_pass_on(buf, a, which):
        landed(buf.at[3, a], ag_r.at[which, a, 0])
        upper, lower = pl.ds(0, GROUP // 2), pl.ds(GROUP // 2, GROUP // 2)
        send(buf.at[3, a, upper], buf.at[2, a, upper], sent.at[which], ag_r.at[which, a, 2], (dp, above))
        landed(buf.at[1, a], ag_r.at[which, a, 1])
        send(buf.at[1, a, lower], buf.at[2, a, lower], sent.at[which], ag_r.at[which, a, 2], (dp, below))

    def gather_done(buf, a, which):
        landed(buf.at[2, a], ag_r.at[which, a, 2])

    low, high = pl.ds(0, SIDE), pl.ds(SIDE, SIDE)

    def first_leg(n):
        for i in range(3):
            send(sbuf.at[n, low, mates_x[i]], mbuf.at[n, x], sent.at[2], a_r.at[n], at(mates_x[i], y, core))
            send(sbuf.at[n, SIDE + mates_y[i]], mbuf.at[n, SIDE + y], sent.at[2], a_r.at[n], at(x, mates_y[i], core))
        mbuf[n, x] = sbuf[n, low, x]
        mbuf[n, SIDE + y] = sbuf[n, SIDE + y]

    def second_leg(n):
        mine = span(core, MSG)
        other = span(1 - core, MSG)
        landed(mbuf.at[n, pl.ds(0, 6)], a_r.at[n])

        def pair(x_, y_, part, c):
            send(mbuf.at[n, low, y_, part], rbuf.at[n, y, :, mine], sent.at[3], b_r.at[n], at(x, y_, c))
            send(mbuf.at[n, high, x_, part], rbuf.at[n, high, x, mine], sent.at[3], b_r.at[n], at(x_, y, c))

        for part, c in ((other, 1 - core), (mine, core)):
            for i in range(3):
                pair(mates_x[i], mates_y[i], part, c)
        pair(x, y, other, 1 - core)
        rbuf[n, y, :, mine] = mbuf[n, low, y, mine]
        rbuf[n, high, x, mine] = mbuf[n, high, x, mine]

    def arrived(n):
        landed(rbuf.at[n, pl.ds(0, 7)], b_r.at[n])

    def serve(n, table, src):
        rows = dot(table, src).astype(BF16)
        for h in range(2):
            sbuf[n, pl.ds(h * SIDE, SIDE)] = rows[:, h * HW : (h + 1) * HW].reshape(SIDE, SIDE, 2 * MSG, HW)

    def rows_of(n):
        parts = [rbuf[n, pl.ds(h * SIDE, SIDE)].reshape(SLOTS, HW) for h in range(2)]
        return jnp.concatenate(parts, axis=1)

    def normalize(src, dst):
        total = jnp.zeros((ROWS, 1), F32)
        for a in range(HALVES):
            for j in range(SLICES):
                v = src[:, columns(a, j)]
                total += jnp.sum(v * v, axis=1, keepdims=True)
        inv = 1.0 / jnp.sqrt(total + epsilon)
        for a in range(HALVES):
            for j in range(SLICES):
                dst[0, a, block(j), :] = (src[:, columns(a, j)] * inv).astype(BF16)
        return jnp.broadcast_to(inv, (ROWS, 128))

    with jax.named_scope("integers_in"):
        for copy in ints_in:
            copy.wait()
    own_row = own_ref[...]
    loc_row = loc_ref[...]
    cnt_row = cnt_ref[...]
    square = (HARD, HARD)
    row_b = jnp.broadcast_to(own_row, square)
    own_col = jnp.sum(jnp.where(iota(square, 0) == iota(square, 1), row_b, 0), axis=1, keepdims=True)
    earlier = (own_col == row_b) & (iota(square, 0) < iota(square, 1))
    rank = jnp.sum(jnp.where(earlier, 1, 0), axis=0, keepdims=True)
    up = (own_row + (N_SUB - z)) % N_SUB
    owner_dp = own_row // N_SUB
    slot_at_own = one_hot(iota((ROWS, HARD), 0) == jnp.where(up == 0, owner_dp * CAP + rank, ROWS))
    cnt_b = jnp.broadcast_to(cnt_row, (ROWS, ROWS))
    upto = iota((ROWS, ROWS), 1) <= iota((ROWS, ROWS), 0)
    before = iota((ROWS, ROWS), 1) < iota((ROWS, ROWS), 0)
    ends = jnp.sum(jnp.where(upto, cnt_b, 0), axis=1, keepdims=True)
    starts = jnp.sum(jnp.where(before, cnt_b, 0), axis=1, keepdims=True)
    slot_id = iota((ROWS, HARD), 1)
    query_t = one_hot((slot_id >= starts) & (slot_id < ends))

    def match(n_dp, n_mid, shape, dim):
        i = iota(shape, dim)
        return i // (n_mid * CAP), (i // CAP) % n_mid, i % CAP

    def spread():
        r = match(N_DP, SLICES, (SLOTS, ROWS), 0)
        c = match(N_DP, 1, (SLOTS, ROWS), 1)
        return one_hot((r[0] == c[0]) & (r[2] == c[2]))

    def spread_t():
        r = match(N_DP, 1, (ROWS, SLOTS), 0)
        c = match(N_DP, SLICES, (ROWS, SLOTS), 1)
        return one_hot((r[0] == c[0]) & (r[2] == c[2]))

    def by_slice(dst, d, rows):
        slice_of = (iota((SLOTS, ROWS), 0) // CAP) % SLICES
        rows = rows.astype(BF16)
        for j in range(SLICES):
            dst[d, :, block(j)] = jnp.where(slice_of == j, rows, jnp.zeros_like(rows))

    def by_slice_t(dst, d, rows):
        slice_of = (iota((ROWS, SLOTS), 1) // CAP) % SLICES
        rows = rows.astype(BF16)
        for j in range(SLICES):
            dst[d, block(j), :] = jnp.where(slice_of == j, rows, jnp.zeros_like(rows))

    by_slice(fs, 0, dot(spread(), dot_nt(slot_at_own, query_t).astype(BF16)))

    with jax.named_scope("queries_in"):
        q_in.wait()
    p_in.start()
    qinv[...] = normalize(qf, qall)
    serve(0, fs[0], qall[0, 0])
    with jax.named_scope("entry_barrier"):
        pl.semaphore_wait(barrier, N_DP - 1 + N_SUB - 1)
    first_leg(0)
    asks = one_hot(iota((N_DP, HARD), 0) == owner_dp)
    row_at = jnp.where(iota((ROWS, HARD), 0) == up * CAP + rank, loc_row + 1, 0).astype(F32).astype(BF16)
    e_send[:, 0, :] = dot_nt(asks, row_at)
    to_plane(e_send, e_recv, 0)
    with jax.named_scope("passages_in"):
        p_in.wait()
    stats[0] = normalize(pf, pall)
    gather_start(pall, 0, 0)
    serve(1, fs[0], qall[0, 1])
    first_leg(1)
    slot_by_up = one_hot(iota((SLOTS, HARD), 0) == up * ROWS + owner_dp * CAP + rank)
    f_send[...] = dot_nt(slot_by_up, query_t).astype(BF16)
    to_mates(f_send, f_recv, 1)
    second_leg(0)
    second_leg(1)

    def asked_passages(d):
        r = match(N_DP, SLICES, (SLOTS, ROWS), 0)
        lane = iota((SLOTS, ROWS), 1)
        asked = dot(one_hot(iota((SLOTS, N_DP), 0) // MSG == iota((SLOTS, N_DP), 1)), e_recv[:, 0, :].astype(BF16))
        row = jnp.sum(jnp.where(lane == d * CAP + r[2], asked, 0.0), axis=1, keepdims=True)
        by_slice(es, d, one_hot((lane + 1).astype(F32) == row))

    landed(e_recv.at[pl.ds(0, N_DP - 1)], t_r.at[0])
    asked_passages(0)

    def score_batch(d, a):
        part = jnp.zeros((ROWS, ROWS), F32)
        for j in range(SLICES):
            part += dot_nt(qall[0, a, block(j), :], pall[d, a, block(j), :])
        sacc[d] += part

    def score_hard(n, d, a):
        arrived(n)
        pairs = dot_nt(qall[0, a], rows_of(n)) * fk[d].astype(F32)
        hacc[pl.ds(d, 1), :] += jnp.sum(pairs, axis=0, keepdims=True)

    sacc[...] = jnp.zeros_like(sacc)
    hacc[...] = jnp.zeros_like(hacc)
    serve(2, es[0], pall[0, 0])
    first_leg(2)
    for d in range(N_SUB):
        mine = dot_nt(query_t, slot_by_up[block(d), :])
        ft[d] = mine
        by_slice_t(fk, d, dot(mine.astype(BF16), spread_t()))
    serve(3, es[0], pall[0, 1])
    first_leg(3)
    gather_pass_on(pall, 0, 0)
    gather_start(pall, 1, 0)
    second_leg(2)
    for d in range(1, N_SUB):
        asked_passages(d)
    score_batch(0, 0)
    score_batch(0, 1)

    def turn(t):
        i = t % 3
        return 1 + 2 * i - 3 * (i // 2), t // 3, i

    def passages(t, carry):
        d, a, i = turn(t)

        @pl.when(i == 2)
        def _():
            gather_done(pall, a, 0)

        serve(4 + t, es[d], pall[d, a])
        first_leg(4 + t)
        second_leg(3 + t)
        score_batch(d, a)

        @pl.when(t == 2)
        def _():
            gather_pass_on(pall, 1, 0)
            gather_start(qall, 0, 1)

        @pl.when(t == 5)
        def _():
            gather_pass_on(qall, 0, 1)
            gather_start(qall, 1, 1)

        @pl.when((t == 1) | (t == 2))
        def _():
            score_hard(1 + t, 0, t - 1)

        @pl.when(t >= 3)
        def _():
            before_d, before_a, _ = turn(t - 3)
            score_hard(1 + t, before_d, before_a)

        return carry

    lax.fori_loop(0, 6, passages, 0)

    landed(f_recv.at[pl.ds(0, GROUP - ROWS)], t_r.at[1])
    for d in range(1, N_SUB):
        by_slice(fs, d, dot(spread(), f_recv[block(d), :]))

    def queries(t):
        d, a, i = turn(t)
        serve(10 + t, fs[d], qall[d, a])
        first_leg(10 + t)
        second_leg(9 + t)

    def queries_first(t, carry):
        @pl.when(t == 2)
        def _():
            gather_done(qall, 0, 1)

        queries(t)
        before_d, before_a, _ = turn(t + 3)
        score_hard(7 + t, before_d, before_a)
        return carry

    lax.fori_loop(0, 3, queries_first, 0)

    scores = [sacc[d] / sharpness_divisor for d in range(N_SUB)]
    exp_batch = [jnp.exp(v) for v in scores]
    fold = spread().astype(F32)
    hard_scores = (
        lax.dot_general(
            hacc[...], fold, (((1,), (0,)), ((), ())),
            precision=lax.Precision.HIGHEST, preferred_element_type=F32,
        )
        / sharpness_divisor
    )
    used = [jnp.sum(ft[d], axis=0, keepdims=True) for d in range(N_SUB)]
    exp_hard = [jnp.where(used[d] > 0.5, jnp.exp(hard_scores[d : d + 1, :]), 0.0) for d in range(N_SUB)]

    def lanes_for(d, row, start):
        shape = (N_DP, ROWS)
        spread_row = jnp.broadcast_to(row.astype(F32), shape)
        by_row = jnp.where(iota(shape, 0) == iota(shape, 1) // CAP, spread_row, 0.0).astype(BF16)
        place = one_hot(iota((ROWS, ROWS), 1) == start + d * CAP + iota((ROWS, ROWS), 0) % CAP)
        return dot(by_row, place)

    total = jnp.zeros((ROWS, 1), F32)
    for d in range(N_SUB):
        total += jnp.sum(exp_batch[d] + ft[d] * exp_hard[d], axis=1, keepdims=True)
    diagonal = iota((ROWS, ROWS), 1) == iota((ROWS, ROWS), 0)
    positive = jnp.sum(jnp.where(diagonal, scores[0], 0.0), axis=1, keepdims=True)
    loss_part = jnp.sum(jnp.log(total) - positive, axis=0, keepdims=True)
    loss_send[...] = jnp.broadcast_to(loss_part, (1, 128))
    for d in range(N_SUB):
        coef = exp_batch[d] / total
        if d == 0:
            coef = coef - jnp.where(diagonal, 1.0, 0.0)
        cb_send[block(d), :] = coef.astype(BF16)
        cbm[:, block(d)] = coef.astype(BF16)
        slot_total = jnp.sum(ft[d] * total, axis=0, keepdims=True) + (1.0 - used[d])
        hard_coef = (exp_hard[d] / slot_total).astype(BF16)
        hard_idx = dot_nt(jnp.broadcast_to(loc_row + 1, (8, HARD)).astype(F32).astype(BF16), slot_by_up[block(d), :])
        g_send[d] = lanes_for((N_SUB - d) % N_SUB, hard_coef, 0) + lanes_for(
            (N_SUB - d) % N_SUB, hard_idx[0:1, :].astype(BF16), MSG
        )
        weight = dot(jnp.broadcast_to(hard_coef, (8, ROWS)), spread_t())[0:1, :]
        fk[d] = (fk[d].astype(F32) * weight).astype(BF16)
    for e, mate in mates:
        send(g_send.at[e], g_recv.at[N_SUB - e], t_s.at[2], t_r.at[2], (dp, mate))
    g_recv[0] = g_send[0]
    to_mates(cb_send, cb_recv, 3)

    def share_loss(dst, index, sem, devices):
        for device in devices:
            send(loss_send, dst.at[index], t_s.at[sem], t_r.at[sem], device)
        dst[index] = loss_send[...]

    def add_loss(src, sem, count):
        landed(src.at[pl.ds(0, count - 1)], t_r.at[sem])
        landed(src.at[pl.ds(0, count - 1)], t_s.at[sem])
        added = src[0]
        for i in range(1, count):
            added = added + src[i]
        loss_send[...] = added

    share_loss(loss_z, z, 4, [(dp, mate) for _, mate in mates])

    scale = 1.0 / sharpness_divisor

    def query_terms(a):
        grad = jnp.zeros((GROUP, CW), F32)
        for n, d in ((2 + a, 0), (4 + 3 * a, 1), (5 + 3 * a, 3), (6 + 3 * a, 2)):
            grad += dot(fk[d], rows_of(n))
        for j in range(SLICES):
            batch = dot(cbm[...], pall[:, a, block(j), :].reshape(GROUP, CW))
            qg[:, columns(a, j)] = (grad[block(j), :] + batch) * scale

    gather_pass_on(qall, 1, 1)
    queries(3)
    landed(g_recv.at[pl.ds(0, N_SUB - 1)], t_r.at[2])
    w_send[:, 0, :] = g_recv[0] + g_recv[1] + g_recv[2] + g_recv[3]
    to_plane(w_send, w_recv, 5)
    add_loss(loss_z, 4, N_SUB)
    share_loss(loss_x, x, 6, [at(mate, y, core) for mate in mates_x])
    serve(14, fs[3], qall[3, 1])
    first_leg(14)
    query_terms(0)
    gather_done(qall, 1, 1)
    serve(15, fs[2], qall[2, 1])
    first_leg(15)
    second_leg(13)
    query_terms(1)
    add_loss(loss_x, 6, SIDE)
    share_loss(loss_y, y, 7, [at(x, mate, core) for mate in mates_y])

    landed(cb_recv.at[pl.ds(0, GROUP - ROWS)], t_r.at[3])
    cbt[...] = jnp.transpose(cb_recv[...].astype(F32)).astype(BF16)
    for a in range(HALVES):
        for j in range(SLICES):
            pacc[a, block(j), :] = dot(cbt[...], qall[:, a, block(j), :].reshape(GROUP, CW))

    second_leg(14)
    second_leg(15)

    landed(w_recv.at[pl.ds(0, N_DP - 1)], t_r.at[5])
    by_slot = lax.dot_general(
        w_recv[:, 0, :].astype(BF16), one_hot(iota((N_DP, SLOTS), 0) == iota((N_DP, SLOTS), 1) // MSG),
        (((0,), (0,)), ((), ())), preferred_element_type=F32,
    )
    for d in range(N_SUB):
        lane = iota((ROWS, SLOTS), 0)
        rank_of = d * CAP + iota((ROWS, SLOTS), 1) % CAP
        weight = jnp.sum(jnp.where(lane == rank_of, by_slot, 0.0), axis=0, keepdims=True)
        row = jnp.sum(jnp.where(lane == MSG + rank_of, by_slot, 0.0), axis=0, keepdims=True)
        by_slice_t(es, d, jnp.where((lane + 1).astype(F32) == row, weight, 0.0))

    def passage_terms(n, d, a):
        arrived(n)
        pacc[a] += dot(es[d], rows_of(n))

    passage_terms(0, 0, 0)
    add_loss(loss_y, 7, SIDE)
    share_loss(loss_c, core, 8, [at(x, y, 1 - core)])
    passage_terms(1, 0, 1)

    inv = qinv[:, :1]
    inner = jnp.zeros((ROWS, 1), F32)
    for a in range(HALVES):
        for j in range(SLICES):
            inner += jnp.sum(qf[:, columns(a, j)] * inv * qg[:, columns(a, j)], axis=1, keepdims=True)
    for a in range(HALVES):
        for j in range(SLICES):
            cols = columns(a, j)
            qg[:, cols] = (qg[:, cols] - qf[:, cols] * inv * inner) * inv

    def more_passage_terms(t, carry):
        d, a, _ = turn(t)
        passage_terms(10 + t, d, a)
        return carry

    inv = stats[0, :, :1]

    def passage_inner(a):
        inner = jnp.zeros((ROWS, 1), F32)
        for j in range(SLICES):
            inner += jnp.sum(pf[:, columns(a, j)] * inv * pacc[a, block(j), :], axis=1, keepdims=True)
        return inner

    lax.fori_loop(0, 3, more_passage_terms, 0)
    first = passage_inner(0)
    add_loss(loss_c, 8, 2)
    loss_ref[...] = loss_send[...] / (ROWS * N_DP * N_SUB)
    lax.fori_loop(3, 6, more_passage_terms, 0)
    stats[1] = jnp.broadcast_to((first + passage_inner(1)) * scale, (ROWS, 128))

    landed(e_send.at[pl.ds(0, N_DP - 1)], t_s.at[0])
    landed(f_send.at[pl.ds(0, GROUP - ROWS)], t_s.at[1])
    landed(g_send.at[pl.ds(0, N_SUB - 1)], t_s.at[2])
    landed(cb_send.at[pl.ds(0, GROUP - ROWS)], t_s.at[3])
    landed(w_send.at[pl.ds(0, N_DP - 1)], t_s.at[5])
    landed(pall.at[pl.ds(0, 3)], sent.at[0])
    landed(qall.at[pl.ds(0, 3)], sent.at[1])
    landed(mbuf.at[pl.ds(0, 12)], sent.at[2])
    landed(mbuf.at[pl.ds(0, 14)], sent.at[3])


def write_out(loss_in, q_in, pacc, pf, stats, loss_hbm, q_hbm, p_hbm, out, loss, sem):
    loss[...] = loss_in[:, :1]
    copies = [pltpu.make_async_copy(loss, loss_hbm, sem.at[2, 0])] + [
        pltpu.make_async_copy(q_in.at[pl.ds(i * 32, 32)], q_hbm.at[pl.ds(i * 32, 32)], sem.at[0, i])
        for i in range(4)
    ]
    for copy in copies:
        copy.start()
    scale = 1.0 / sharpness_divisor
    for i in range(4):
        rows = slice(i * 32, (i + 1) * 32)
        inv = stats[0, rows, :1]
        inner = stats[1, rows, :1]
        for a in range(HALVES):
            for j in range(SLICES):
                cols = columns(a, j)
                grad = pacc[a, j * ROWS + i * 32 : j * ROWS + (i + 1) * 32, :] * scale
                out[rows, cols] = (grad - pf[rows, cols] * inv * inner) * inv
        copy = pltpu.make_async_copy(out.at[pl.ds(i * 32, 32)], p_hbm.at[pl.ds(i * 32, 32)], sem.at[1, i])
        copy.start()
        copies.append(copy)
    for copy in copies:
        copy.wait()


def local(queries, passages, counts, hard_owner, hard_local):
    vmem = pl.BlockSpec(memory_space=pltpu.VMEM)
    any_space = pl.BlockSpec(memory_space=pl.ANY)
    hbm = pl.BlockSpec(memory_space=pltpu.HBM)
    dma = pltpu.SemaphoreType.DMA
    table = pltpu.VMEM((SLOTS, 128), BF16)
    gathered = pltpu.VMEM((N_SUB, HALVES, GROUP, CW), BF16)
    routed = pltpu.VMEM((ITEMS, 2 * SIDE, SIDE, 2 * MSG, HW), BF16)
    masks = pltpu.VMEM((N_SUB, SLOTS, GROUP), BF16)
    one_loss = pltpu.VMEM((1, 128), F32)
    plane = pltpu.VMEM((N_DP, 1, 128), F32)
    mate = pltpu.VMEM((N_SUB, N_DP, 128), F32)
    rows = pltpu.VMEM((ROWS, WIDTH), F32)
    held = pl.pallas_call(
        kernel,
        out_shape=(
            one_loss, rows, pltpu.VMEM((HALVES, GROUP, CW), F32), rows, pltpu.VMEM((2, ROWS, 128), F32),
        ),
        in_specs=[hbm] * 5,
        out_specs=(vmem,) * 5,
        scratch_shapes=[
            pltpu.VMEM((1, ROWS), jnp.int32), pltpu.VMEM((1, HARD), jnp.int32), pltpu.VMEM((1, HARD), jnp.int32),
            rows, gathered, gathered, routed, routed, routed,
            plane, plane, table, table, table, table, mate, mate, plane, plane,
            one_loss, pltpu.VMEM((N_SUB, 1, 128), F32),
            pltpu.VMEM((SIDE, 1, 128), F32), pltpu.VMEM((SIDE, 1, 128), F32), pltpu.VMEM((2, 1, 128), F32),
            pltpu.VMEM((N_SUB, ROWS, ROWS), F32), pltpu.VMEM((8, SLOTS), F32), masks, masks, masks,
            pltpu.VMEM((N_SUB, ROWS, ROWS), F32), pltpu.VMEM((ROWS, GROUP), BF16), pltpu.VMEM((ROWS, GROUP), BF16),
            pltpu.VMEM((ROWS, 128), F32),
            dma((5,)), dma((4,)), dma((2, HALVES, 3)), dma((ITEMS,)), dma((ITEMS,)), dma((9,)), dma((9,)),
        ],
        compiler_params=pltpu.CompilerParams(
            collective_id=0, has_side_effects=True, vmem_limit_bytes=53 * 2**20
        ),
        name="contrastive",
    )(*[
        pltpu.with_memory_space_constraint(v, pltpu.HBM)
        for v in (passages, queries, counts, hard_owner.reshape(1, HARD), hard_local)
    ])
    loss, query_grad, passage_grad = pl.pallas_call(
        write_out,
        out_shape=(
            jax.ShapeDtypeStruct((1, 1), F32),
            jax.ShapeDtypeStruct((ROWS, WIDTH), F32),
            jax.ShapeDtypeStruct((ROWS, WIDTH), F32),
        ),
        in_specs=[vmem] * 5,
        out_specs=(any_space,) * 3,
        scratch_shapes=[rows, pltpu.VMEM((1, 1), F32), dma((3, 4))],
        compiler_params=pltpu.CompilerParams(vmem_limit_bytes=8 * 2**20),
        name="write_out",
    )(*[pltpu.with_memory_space_constraint(v, pltpu.VMEM) for v in held])
    return loss.reshape(()), query_grad, passage_grad


def solution(mesh):
    in_specs = (
        P(("dp", "sub"), None),
        P(("dp", "sub"), None),
        P(("dp", "sub"), None),
        P(("dp", "sub"), None, None),
        P(("dp", "sub"), None),
    )
    out_specs = (P(), P(("dp", "sub"), None), P(("dp", "sub"), None))
    return jax.shard_map(local, mesh=mesh, in_specs=in_specs, out_specs=out_specs, check_vma=False)
```

```python
import jax
import jax.numpy as jnp
from jax import lax
from jax.experimental import pallas as pl
from jax.experimental.pallas import tpu as pltpu
from jax.sharding import PartitionSpec as P

MESH = pl.DeviceIdType.MESH
F32 = jnp.float32
BF16 = jnp.bfloat16

sharpness_divisor = 0.02
epsilon = 1e-06

ROWS = 128
WIDTH = 4096
HARD = 256
CAP = 4
N_SUB = 4
N_DP = 32
SIDE = 4
GROUP = ROWS * N_SUB
SLOTS = N_DP * N_SUB * CAP
MSG = N_SUB * CAP
HALVES = 2
SLICES = 4
CW = WIDTH // (HALVES * SLICES)
HW = CW // 2
ITEMS = 16


def dot(a, b):
    return lax.dot_general(a, b, (((1,), (0,)), ((), ())), preferred_element_type=F32)


def dot_nt(a, b):
    return lax.dot_general(a, b, (((1,), (1,)), ((), ())), preferred_element_type=F32)


def iota(shape, dim):
    return lax.broadcasted_iota(jnp.int32, shape, dim)


def one_hot(mask):
    return jnp.where(mask, 1.0, 0.0).astype(BF16)


def columns(a, j):
    start = (j * HALVES + a) * CW
    return slice(start, start + CW)


def block(j):
    return slice(j * ROWS, (j + 1) * ROWS)


def slot_grads(rows, weights):
    parts = [rows[:, c : c + 128].astype(F32) * weights for c in range(0, CW, 128)]
    return jnp.concatenate(parts, axis=1).astype(BF16)


def inner_with(pf, inv, grad, a):
    inner = jnp.zeros((ROWS, 1), F32)
    for j in range(SLICES):
        inner += jnp.sum(pf[:, columns(a, j)] * inv * grad[block(j), :], axis=1, keepdims=True)
    return inner


def kernel(
    p_hbm, q_hbm, cnt_hbm, own_hbm, loc_hbm,
    loss_ref, qg, pacc, pf, stats, last_rows, last_table, last_weight,
    cnt_ref, own_ref, loc_ref, qf, pall, qall, sbuf, mbuf, rbuf,
    e_send, e_recv, f_send, f_recv, cb_send, cb_recv, g_send, g_recv, w_send, w_recv,
    loss_send, loss_z, loss_x, loss_y, loss_c,
    sacc, hacc, es, fs, fk, ft, cbm, cbt, qinv, wcol,
    in_sem, sent, ag_r, a_r, b_r, t_s, t_r,
):
    dp = lax.axis_index("dp")
    z = lax.axis_index("sub")
    core = lax.rem(dp, 2)
    x = lax.rem(dp // 2, SIDE)
    y = dp // (2 * SIDE)
    above, below = lax.rem(z + 1, N_SUB), lax.rem(z + 3, N_SUB)
    mates = [(e, lax.rem(z + e, N_SUB)) for e in (1, 3, 2)]
    mates_x = [lax.rem(x + d, SIDE) for d in (2, 1, 3)]
    mates_y = [lax.rem(y + d, SIDE) for d in (2, 1, 3)]

    def at(x_, y_, c_):
        return ((y_ * SIDE + x_) * 2 + c_, z)

    def each_peer(body):
        def one(i, carry):
            body(lax.rem(dp + i, N_DP))
            return carry

        lax.fori_loop(1, N_DP, one, 0)

    def send(src, dst, send_sem, recv_sem, device):
        pltpu.make_async_remote_copy(
            src_ref=src, dst_ref=dst, send_sem=send_sem, recv_sem=recv_sem,
            device_id=device, device_id_type=MESH,
        ).start()

    def landed(part, sem):
        pltpu.make_async_copy(part, part, sem).wait()

    ints_in = [
        pltpu.make_async_copy(src, dst, in_sem.at[2 + i])
        for i, (src, dst) in enumerate(((cnt_hbm, cnt_ref), (own_hbm, own_ref), (loc_hbm, loc_ref)))
    ]
    p_in = pltpu.make_async_copy(p_hbm, pf, in_sem.at[0])
    q_in = pltpu.make_async_copy(q_hbm, qf, in_sem.at[1])
    for copy in (*ints_in, q_in):
        copy.start()

    barrier = pltpu.get_barrier_semaphore()
    each_peer(lambda peer: pl.semaphore_signal(barrier, inc=1, device_id=(peer, z), device_id_type=MESH))
    for _, mate in mates:
        pl.semaphore_signal(barrier, inc=1, device_id=(dp, mate), device_id_type=MESH)

    def span(index, rows):
        return pl.ds(pl.multiple_of(index * rows, rows), rows)

    def to_plane(src, dst, sem):
        each_peer(lambda peer: send(src.at[peer], dst.at[dp], t_s.at[sem], t_r.at[sem], (peer, z)))
        dst[dp] = src[dp]

    def to_mates(src, dst, sem):
        for e, mate in mates:
            send(
                src.at[pl.ds(e * ROWS, ROWS)], dst.at[pl.ds((N_SUB - e) * ROWS, ROWS)],
                t_s.at[sem], t_r.at[sem], (dp, mate),
            )
        dst[block(0), :] = src[block(0), :]

    def gather_start(buf, a, which):
        send(buf.at[0, a], buf.at[3, a], sent.at[which], ag_r.at[which, a, 0], (dp, above))
        send(buf.at[0, a], buf.at[1, a], sent.at[which], ag_r.at[which, a, 1], (dp, below))

    def gather_pass_on(buf, a, which):
        landed(buf.at[3, a], ag_r.at[which, a, 0])
        upper, lower = pl.ds(0, GROUP // 2), pl.ds(GROUP // 2, GROUP // 2)
        send(buf.at[3, a, upper], buf.at[2, a, upper], sent.at[which], ag_r.at[which, a, 2], (dp, above))
        landed(buf.at[1, a], ag_r.at[which, a, 1])
        send(buf.at[1, a, lower], buf.at[2, a, lower], sent.at[which], ag_r.at[which, a, 2], (dp, below))

    def gather_done(buf, a, which):
        landed(buf.at[2, a], ag_r.at[which, a, 2])

    low, high = pl.ds(0, SIDE), pl.ds(SIDE, SIDE)

    def first_leg(n):
        for i in range(3):
            send(sbuf.at[n, low, mates_x[i]], mbuf.at[n, x], sent.at[2], a_r.at[n], at(mates_x[i], y, core))
            send(sbuf.at[n, SIDE + mates_y[i]], mbuf.at[n, SIDE + y], sent.at[2], a_r.at[n], at(x, mates_y[i], core))
        mbuf[n, x] = sbuf[n, low, x]
        mbuf[n, SIDE + y] = sbuf[n, SIDE + y]

    def second_leg(n):
        mine = span(core, MSG)
        other = span(1 - core, MSG)
        landed(mbuf.at[n, pl.ds(0, 6)], a_r.at[n])

        def pair(x_, y_, part, c):
            send(mbuf.at[n, low, y_, part], rbuf.at[n, y, :, mine], sent.at[3], b_r.at[n], at(x, y_, c))
            send(mbuf.at[n, high, x_, part], rbuf.at[n, high, x, mine], sent.at[3], b_r.at[n], at(x_, y, c))

        for part, c in ((other, 1 - core), (mine, core)):
            for i in range(3):
                pair(mates_x[i], mates_y[i], part, c)
        pair(x, y, other, 1 - core)
        rbuf[n, y, :, mine] = mbuf[n, low, y, mine]
        rbuf[n, high, x, mine] = mbuf[n, high, x, mine]

    def arrived(n):
        landed(rbuf.at[n, pl.ds(0, 7)], b_r.at[n])

    def serve(n, table, src):
        rows = dot(table, src).astype(BF16)
        for h in range(2):
            sbuf[n, pl.ds(h * SIDE, SIDE)] = rows[:, h * HW : (h + 1) * HW].reshape(SIDE, SIDE, 2 * MSG, HW)

    def rows_of(n):
        parts = [rbuf[n, pl.ds(h * SIDE, SIDE)].reshape(SLOTS, HW) for h in range(2)]
        return jnp.concatenate(parts, axis=1)

    def normalize(src, dst):
        total = jnp.zeros((ROWS, 1), F32)
        for a in range(HALVES):
            for j in range(SLICES):
                v = src[:, columns(a, j)]
                total += jnp.sum(v * v, axis=1, keepdims=True)
        inv = 1.0 / jnp.sqrt(total + epsilon)
        for a in range(HALVES):
            for j in range(SLICES):
                dst[0, a, block(j), :] = (src[:, columns(a, j)] * inv).astype(BF16)
        return jnp.broadcast_to(inv, (ROWS, 128))

    with jax.named_scope("integers_in"):
        for copy in ints_in:
            copy.wait()
    own_row = own_ref[...]
    loc_row = loc_ref[...]
    cnt_row = cnt_ref[...]
    square = (HARD, HARD)
    row_b = jnp.broadcast_to(own_row, square)
    own_col = jnp.sum(jnp.where(iota(square, 0) == iota(square, 1), row_b, 0), axis=1, keepdims=True)
    earlier = (own_col == row_b) & (iota(square, 0) < iota(square, 1))
    rank = jnp.sum(jnp.where(earlier, 1, 0), axis=0, keepdims=True)
    up = (own_row + (N_SUB - z)) % N_SUB
    owner_dp = own_row // N_SUB
    slot_at_own = one_hot(iota((ROWS, HARD), 0) == jnp.where(up == 0, owner_dp * CAP + rank, ROWS))
    cnt_b = jnp.broadcast_to(cnt_row, (ROWS, ROWS))
    upto = iota((ROWS, ROWS), 1) <= iota((ROWS, ROWS), 0)
    before = iota((ROWS, ROWS), 1) < iota((ROWS, ROWS), 0)
    ends = jnp.sum(jnp.where(upto, cnt_b, 0), axis=1, keepdims=True)
    starts = jnp.sum(jnp.where(before, cnt_b, 0), axis=1, keepdims=True)
    slot_id = iota((ROWS, HARD), 1)
    query_t = one_hot((slot_id >= starts) & (slot_id < ends))

    def match(n_dp, n_mid, shape, dim):
        i = iota(shape, dim)
        return i // (n_mid * CAP), (i // CAP) % n_mid, i % CAP

    def spread():
        r = match(N_DP, SLICES, (SLOTS, ROWS), 0)
        c = match(N_DP, 1, (SLOTS, ROWS), 1)
        return one_hot((r[0] == c[0]) & (r[2] == c[2]))

    def spread_t():
        r = match(N_DP, 1, (ROWS, SLOTS), 0)
        c = match(N_DP, SLICES, (ROWS, SLOTS), 1)
        return one_hot((r[0] == c[0]) & (r[2] == c[2]))

    def by_slice(dst, d, rows):
        slice_of = (iota((SLOTS, ROWS), 0) // CAP) % SLICES
        rows = rows.astype(BF16)
        for j in range(SLICES):
            dst[d, :, block(j)] = jnp.where(slice_of == j, rows, jnp.zeros_like(rows))

    def by_slice_t(dst, d, rows):
        slice_of = (iota((ROWS, SLOTS), 1) // CAP) % SLICES
        rows = rows.astype(BF16)
        for j in range(SLICES):
            dst[d, block(j), :] = jnp.where(slice_of == j, rows, jnp.zeros_like(rows))

    by_slice(fs, 0, dot(spread(), dot_nt(slot_at_own, query_t).astype(BF16)))

    with jax.named_scope("queries_in"):
        q_in.wait()
    p_in.start()
    qinv[...] = normalize(qf, qall)
    serve(0, fs[0], qall[0, 0])
    with jax.named_scope("entry_barrier"):
        pl.semaphore_wait(barrier, N_DP - 1 + N_SUB - 1)
    first_leg(0)
    asks = one_hot(iota((N_DP, HARD), 0) == owner_dp)
    row_at = jnp.where(iota((ROWS, HARD), 0) == up * CAP + rank, loc_row + 1, 0).astype(F32).astype(BF16)
    e_send[:, 0, :] = dot_nt(asks, row_at)
    to_plane(e_send, e_recv, 0)
    with jax.named_scope("passages_in"):
        p_in.wait()
    stats[0] = normalize(pf, pall)
    gather_start(pall, 0, 0)
    serve(1, fs[0], qall[0, 1])
    first_leg(1)
    slot_by_up = one_hot(iota((SLOTS, HARD), 0) == up * ROWS + owner_dp * CAP + rank)
    f_send[...] = dot_nt(slot_by_up, query_t).astype(BF16)
    to_mates(f_send, f_recv, 1)
    second_leg(0)
    second_leg(1)

    def asked_passages(d):
        r = match(N_DP, SLICES, (SLOTS, ROWS), 0)
        lane = iota((SLOTS, ROWS), 1)
        asked = dot(one_hot(iota((SLOTS, N_DP), 0) // MSG == iota((SLOTS, N_DP), 1)), e_recv[:, 0, :].astype(BF16))
        row = jnp.sum(jnp.where(lane == d * CAP + r[2], asked, 0.0), axis=1, keepdims=True)
        by_slice(es, d, one_hot((lane + 1).astype(F32) == row))

    landed(e_recv.at[pl.ds(0, N_DP - 1)], t_r.at[0])
    asked_passages(0)

    def score_batch(d, a):
        part = jnp.zeros((ROWS, ROWS), F32)
        for j in range(SLICES):
            part += dot_nt(qall[0, a, block(j), :], pall[d, a, block(j), :])
        sacc[d] += part

    def score_hard(n, d, a):
        arrived(n)
        pairs = dot_nt(qall[0, a], rows_of(n)) * fk[d].astype(F32)
        hacc[pl.ds(d, 1), :] += jnp.sum(pairs, axis=0, keepdims=True)

    sacc[...] = jnp.zeros_like(sacc)
    hacc[...] = jnp.zeros_like(hacc)
    serve(2, es[0], pall[0, 0])
    first_leg(2)
    for d in range(N_SUB):
        mine = dot_nt(query_t, slot_by_up[block(d), :])
        ft[d] = mine
        by_slice_t(fk, d, dot(mine.astype(BF16), spread_t()))
    serve(3, es[0], pall[0, 1])
    first_leg(3)
    gather_pass_on(pall, 0, 0)
    gather_start(pall, 1, 0)
    second_leg(2)
    for d in range(1, N_SUB):
        asked_passages(d)
    score_batch(0, 0)
    score_batch(0, 1)

    def turn(t):
        i = t % 3
        return 1 + 2 * i - 3 * (i // 2), t // 3, i

    def passages(t, carry):
        d, a, i = turn(t)

        @pl.when(i == 2)
        def _():
            gather_done(pall, a, 0)

        serve(4 + t, es[d], pall[d, a])
        first_leg(4 + t)
        second_leg(3 + t)
        score_batch(d, a)

        @pl.when(t == 2)
        def _():
            gather_pass_on(pall, 1, 0)
            gather_start(qall, 0, 1)

        @pl.when(t == 5)
        def _():
            gather_pass_on(qall, 0, 1)
            gather_start(qall, 1, 1)

        @pl.when((t == 1) | (t == 2))
        def _():
            score_hard(1 + t, 0, t - 1)

        @pl.when(t >= 3)
        def _():
            before_d, before_a, _ = turn(t - 3)
            score_hard(1 + t, before_d, before_a)

        return carry

    lax.fori_loop(0, 6, passages, 0)

    landed(f_recv.at[pl.ds(0, GROUP - ROWS)], t_r.at[1])
    for d in range(1, N_SUB):
        by_slice(fs, d, dot(spread(), f_recv[block(d), :]))

    def queries(t):
        d, a, i = turn(t)
        serve(10 + t, fs[d], qall[d, a])
        first_leg(10 + t)
        second_leg(9 + t)

    def queries_first(t, carry):
        @pl.when(t == 2)
        def _():
            gather_done(qall, 0, 1)

        queries(t)
        before_d, before_a, _ = turn(t + 3)
        score_hard(7 + t, before_d, before_a)
        return carry

    lax.fori_loop(0, 3, queries_first, 0)

    scores = [sacc[d] / sharpness_divisor for d in range(N_SUB)]
    exp_batch = [jnp.exp(v) for v in scores]
    fold = spread().astype(F32)
    hard_scores = (
        lax.dot_general(
            hacc[...], fold, (((1,), (0,)), ((), ())),
            precision=lax.Precision.HIGHEST, preferred_element_type=F32,
        )
        / sharpness_divisor
    )
    used = [jnp.sum(ft[d], axis=0, keepdims=True) for d in range(N_SUB)]
    exp_hard = [jnp.where(used[d] > 0.5, jnp.exp(hard_scores[d : d + 1, :]), 0.0) for d in range(N_SUB)]

    def lanes_for(d, row, start):
        shape = (N_DP, ROWS)
        spread_row = jnp.broadcast_to(row.astype(F32), shape)
        by_row = jnp.where(iota(shape, 0) == iota(shape, 1) // CAP, spread_row, 0.0).astype(BF16)
        place = one_hot(iota((ROWS, ROWS), 1) == start + d * CAP + iota((ROWS, ROWS), 0) % CAP)
        return dot(by_row, place)

    total = jnp.zeros((ROWS, 1), F32)
    for d in range(N_SUB):
        total += jnp.sum(exp_batch[d] + ft[d] * exp_hard[d], axis=1, keepdims=True)
    diagonal = iota((ROWS, ROWS), 1) == iota((ROWS, ROWS), 0)
    positive = jnp.sum(jnp.where(diagonal, scores[0], 0.0), axis=1, keepdims=True)
    loss_part = jnp.sum(jnp.log(total) - positive, axis=0, keepdims=True)
    loss_send[...] = jnp.broadcast_to(loss_part, (1, 128))
    for d in range(N_SUB):
        coef = exp_batch[d] / total
        if d == 0:
            coef = coef - jnp.where(diagonal, 1.0, 0.0)
        cb_send[block(d), :] = coef.astype(BF16)
        cbm[:, block(d)] = coef.astype(BF16)
        slot_total = jnp.sum(ft[d] * total, axis=0, keepdims=True) + (1.0 - used[d])
        hard_coef = (exp_hard[d] / slot_total).astype(BF16)
        hard_idx = dot_nt(jnp.broadcast_to(loc_row + 1, (8, HARD)).astype(F32).astype(BF16), slot_by_up[block(d), :])
        g_send[d] = lanes_for((N_SUB - d) % N_SUB, hard_coef, 0) + lanes_for(
            (N_SUB - d) % N_SUB, hard_idx[0:1, :].astype(BF16), MSG
        )
        weight = dot(jnp.broadcast_to(hard_coef, (8, ROWS)), spread_t())[0:1, :]
        fk[d] = (fk[d].astype(F32) * weight).astype(BF16)
    for e, mate in mates:
        send(g_send.at[e], g_recv.at[N_SUB - e], t_s.at[2], t_r.at[2], (dp, mate))
    g_recv[0] = g_send[0]
    to_mates(cb_send, cb_recv, 3)

    def share_loss(dst, index, sem, devices):
        for device in devices:
            send(loss_send, dst.at[index], t_s.at[sem], t_r.at[sem], device)
        dst[index] = loss_send[...]

    def add_loss(src, sem, count):
        landed(src.at[pl.ds(0, count - 1)], t_r.at[sem])
        landed(src.at[pl.ds(0, count - 1)], t_s.at[sem])
        added = src[0]
        for i in range(1, count):
            added = added + src[i]
        loss_send[...] = added

    share_loss(loss_z, z, 4, [(dp, mate) for _, mate in mates])

    scale = 1.0 / sharpness_divisor

    def query_terms(a):
        grad = jnp.zeros((GROUP, CW), F32)
        for n, d in ((2 + a, 0), (4 + 3 * a, 1), (5 + 3 * a, 3), (6 + 3 * a, 2)):
            grad += dot(fk[d], rows_of(n))
        for j in range(SLICES):
            batch = dot(cbm[...], pall[:, a, block(j), :].reshape(GROUP, CW))
            qg[:, columns(a, j)] = (grad[block(j), :] + batch) * scale

    gather_pass_on(qall, 1, 1)
    queries(3)
    landed(g_recv.at[pl.ds(0, N_SUB - 1)], t_r.at[2])
    w_send[:, 0, :] = g_recv[0] + g_recv[1] + g_recv[2] + g_recv[3]
    to_plane(w_send, w_recv, 5)
    add_loss(loss_z, 4, N_SUB)
    share_loss(loss_x, x, 6, [at(mate, y, core) for mate in mates_x])
    serve(14, fs[3], qall[3, 1])
    first_leg(14)
    query_terms(0)
    gather_done(qall, 1, 1)
    serve(15, fs[2], qall[2, 1])
    first_leg(15)
    second_leg(13)
    query_terms(1)
    add_loss(loss_x, 6, SIDE)
    share_loss(loss_y, y, 7, [at(x, mate, core) for mate in mates_y])

    landed(cb_recv.at[pl.ds(0, GROUP - ROWS)], t_r.at[3])
    cbt[...] = jnp.transpose(cb_recv[...].astype(F32)).astype(BF16)
    for a in range(HALVES):
        for j in range(SLICES):
            pacc[a, block(j), :] = dot(cbt[...], qall[:, a, block(j), :].reshape(GROUP, CW)) * scale

    second_leg(14)
    second_leg(15)

    landed(w_recv.at[pl.ds(0, N_DP - 1)], t_r.at[5])
    told = w_recv[:, 0, :].astype(BF16)
    by_slot = dot(one_hot(iota((SLOTS, N_DP), 0) // MSG == iota((SLOTS, N_DP), 1)), told)
    by_slot_t = lax.dot_general(
        told, one_hot(iota((N_DP, SLOTS), 0) == iota((N_DP, SLOTS), 1) // MSG),
        (((0,), (0,)), ((), ())), preferred_element_type=F32,
    )
    for d in range(N_SUB):
        weight_lane = iota((SLOTS, ROWS), 1) == d * CAP + iota((SLOTS, ROWS), 0) % CAP
        weight = jnp.sum(jnp.where(weight_lane, by_slot, 0.0), axis=1, keepdims=True)
        wcol[d] = jnp.broadcast_to(weight * scale, (SLOTS, 128))
        lane = iota((ROWS, SLOTS), 0)
        row_lane = lane == MSG + d * CAP + iota((ROWS, SLOTS), 1) % CAP
        row = jnp.sum(jnp.where(row_lane, by_slot_t, 0.0), axis=0, keepdims=True)
        by_slice_t(es, d, one_hot((lane + 1).astype(F32) == row))
    last_table[...] = es[2]
    last_weight[...] = wcol[2]

    def passage_terms(n, d, a):
        arrived(n)
        pacc[a] += dot(es[d], slot_grads(rows_of(n), wcol[d]))

    passage_terms(0, 0, 0)
    add_loss(loss_y, 7, SIDE)
    share_loss(loss_c, core, 8, [at(x, y, 1 - core)])
    passage_terms(1, 0, 1)

    inv = qinv[:, :1]
    inner = jnp.zeros((ROWS, 1), F32)
    for a in range(HALVES):
        for j in range(SLICES):
            inner += jnp.sum(qf[:, columns(a, j)] * inv * qg[:, columns(a, j)], axis=1, keepdims=True)
    for a in range(HALVES):
        for j in range(SLICES):
            cols = columns(a, j)
            qg[:, cols] = (qg[:, cols] - qf[:, cols] * inv * inner) * inv

    def more_passage_terms(t, carry):
        d, a, _ = turn(t)
        passage_terms(10 + t, d, a)
        return carry

    inv = stats[0, :, :1]

    lax.fori_loop(0, 3, more_passage_terms, 0)
    first = inner_with(pf, inv, pacc.at[0], 0)
    add_loss(loss_c, 8, 2)
    loss_ref[...] = loss_send[...] / (ROWS * N_DP * N_SUB)
    stats[1] = jnp.broadcast_to(first, (ROWS, 128))
    lax.fori_loop(3, 5, more_passage_terms, 0)
    arrived(15)
    last_rows[...] = rows_of(15)

    landed(e_send.at[pl.ds(0, N_DP - 1)], t_s.at[0])
    landed(f_send.at[pl.ds(0, GROUP - ROWS)], t_s.at[1])
    landed(g_send.at[pl.ds(0, N_SUB - 1)], t_s.at[2])
    landed(cb_send.at[pl.ds(0, GROUP - ROWS)], t_s.at[3])
    landed(w_send.at[pl.ds(0, N_DP - 1)], t_s.at[5])
    landed(pall.at[pl.ds(0, 3)], sent.at[0])
    landed(qall.at[pl.ds(0, 3)], sent.at[1])
    landed(mbuf.at[pl.ds(0, 12)], sent.at[2])
    landed(mbuf.at[pl.ds(0, 14)], sent.at[3])


def write_out(
    loss_in, q_in, pacc, pf, stats, last_rows, last_table, last_weight,
    loss_hbm, q_hbm, p_hbm,
    out, grad, loss, sem,
):
    loss[...] = loss_in[:, :1]
    copies = [pltpu.make_async_copy(loss, loss_hbm, sem.at[2, 0])] + [
        pltpu.make_async_copy(q_in.at[pl.ds(i * 32, 32)], q_hbm.at[pl.ds(i * 32, 32)], sem.at[0, i])
        for i in range(4)
    ]
    for copy in copies:
        copy.start()
    grad[...] = pacc[1] + dot(last_table[...], slot_grads(last_rows[...], last_weight[...]))
    inners = stats[1, :, :1] + inner_with(pf, stats[0, :, :1], grad, 1)
    for i in range(4):
        rows = slice(i * 32, (i + 1) * 32)
        inv = stats[0, rows, :1]
        inner = inners[rows, :]
        for j in range(SLICES):
            part = slice(j * ROWS + i * 32, j * ROWS + (i + 1) * 32)
            cols = columns(0, j)
            out[rows, cols] = (pacc[0, part, :] - pf[rows, cols] * inv * inner) * inv
            cols = columns(1, j)
            out[rows, cols] = (grad[part, :] - pf[rows, cols] * inv * inner) * inv
        copy = pltpu.make_async_copy(out.at[pl.ds(i * 32, 32)], p_hbm.at[pl.ds(i * 32, 32)], sem.at[1, i])
        copy.start()
        copies.append(copy)
    for copy in copies:
        copy.wait()


def local(queries, passages, counts, hard_owner, hard_local):
    vmem = pl.BlockSpec(memory_space=pltpu.VMEM)
    any_space = pl.BlockSpec(memory_space=pl.ANY)
    hbm = pl.BlockSpec(memory_space=pltpu.HBM)
    dma = pltpu.SemaphoreType.DMA
    table = pltpu.VMEM((SLOTS, 128), BF16)
    gathered = pltpu.VMEM((N_SUB, HALVES, GROUP, CW), BF16)
    routed = pltpu.VMEM((ITEMS, 2 * SIDE, SIDE, 2 * MSG, HW), BF16)
    masks = pltpu.VMEM((N_SUB, SLOTS, GROUP), BF16)
    one_loss = pltpu.VMEM((1, 128), F32)
    plane = pltpu.VMEM((N_DP, 1, 128), F32)
    mate = pltpu.VMEM((N_SUB, N_DP, 128), F32)
    rows = pltpu.VMEM((ROWS, WIDTH), F32)
    held = pl.pallas_call(
        kernel,
        out_shape=(
            one_loss, rows, pltpu.VMEM((HALVES, GROUP, CW), F32), rows, pltpu.VMEM((2, ROWS, 128), F32),
            pltpu.VMEM((SLOTS, CW), BF16), pltpu.VMEM((GROUP, SLOTS), BF16), pltpu.VMEM((SLOTS, 128), F32),
        ),
        in_specs=[hbm] * 5,
        out_specs=(vmem,) * 8,
        scratch_shapes=[
            pltpu.VMEM((1, ROWS), jnp.int32), pltpu.VMEM((1, HARD), jnp.int32), pltpu.VMEM((1, HARD), jnp.int32),
            rows, gathered, gathered, routed, routed, routed,
            plane, plane, table, table, table, table, mate, mate, plane, plane,
            one_loss, pltpu.VMEM((N_SUB, 1, 128), F32),
            pltpu.VMEM((SIDE, 1, 128), F32), pltpu.VMEM((SIDE, 1, 128), F32), pltpu.VMEM((2, 1, 128), F32),
            pltpu.VMEM((N_SUB, ROWS, ROWS), F32), pltpu.VMEM((8, SLOTS), F32), masks, masks, masks,
            pltpu.VMEM((N_SUB, ROWS, ROWS), F32), pltpu.VMEM((ROWS, GROUP), BF16), pltpu.VMEM((ROWS, GROUP), BF16),
            pltpu.VMEM((ROWS, 128), F32), pltpu.VMEM((N_SUB, SLOTS, 128), F32),
            dma((5,)), dma((4,)), dma((2, HALVES, 3)), dma((ITEMS,)), dma((ITEMS,)), dma((9,)), dma((9,)),
        ],
        compiler_params=pltpu.CompilerParams(
            collective_id=0, has_side_effects=True, vmem_limit_bytes=51 * 2**20
        ),
        name="contrastive",
    )(*[
        pltpu.with_memory_space_constraint(v, pltpu.HBM)
        for v in (passages, queries, counts, hard_owner.reshape(1, HARD), hard_local)
    ])
    loss, query_grad, passage_grad = pl.pallas_call(
        write_out,
        out_shape=(
            jax.ShapeDtypeStruct((1, 1), F32),
            jax.ShapeDtypeStruct((ROWS, WIDTH), F32),
            jax.ShapeDtypeStruct((ROWS, WIDTH), F32),
        ),
        in_specs=[vmem] * 8,
        out_specs=(any_space,) * 3,
        scratch_shapes=[rows, pltpu.VMEM((GROUP, CW), F32), pltpu.VMEM((1, 1), F32), dma((3, 4))],
        compiler_params=pltpu.CompilerParams(vmem_limit_bytes=10 * 2**20),
        name="write_out",
    )(*[pltpu.with_memory_space_constraint(v, pltpu.VMEM) for v in held])
    return loss.reshape(()), query_grad, passage_grad


def solution(mesh):
    in_specs = (
        P(("dp", "sub"), None),
        P(("dp", "sub"), None),
        P(("dp", "sub"), None),
        P(("dp", "sub"), None, None),
        P(("dp", "sub"), None),
    )
    out_specs = (P(), P(("dp", "sub"), None), P(("dp", "sub"), None))
    return jax.shard_map(local, mesh=mesh, in_specs=in_specs, out_specs=out_specs, check_vma=False)
```

```python
import jax
import jax.numpy as jnp
from jax import lax
from jax.experimental import pallas as pl
from jax.experimental.pallas import tpu as pltpu
from jax.sharding import PartitionSpec as P

MESH = pl.DeviceIdType.MESH
F32 = jnp.float32
BF16 = jnp.bfloat16

sharpness_divisor = 0.02
epsilon = 1e-06

ROWS = 128
WIDTH = 4096
HARD = 256
CAP = 4
N_SUB = 4
N_DP = 32
SIDE = 4
GROUP = ROWS * N_SUB
SLOTS = N_DP * N_SUB * CAP
MSG = N_SUB * CAP
HALVES = 2
SLICES = 4
CW = WIDTH // (HALVES * SLICES)
HW = CW // 2
ITEMS = 16


def dot(a, b):
    return lax.dot_general(a, b, (((1,), (0,)), ((), ())), preferred_element_type=F32)


def dot_nt(a, b):
    return lax.dot_general(a, b, (((1,), (1,)), ((), ())), preferred_element_type=F32)


def iota(shape, dim):
    return lax.broadcasted_iota(jnp.int32, shape, dim)


def one_hot(mask):
    return jnp.where(mask, 1.0, 0.0).astype(BF16)


def columns(a, j):
    start = (j * HALVES + a) * CW
    return slice(start, start + CW)


def block(j):
    return slice(j * ROWS, (j + 1) * ROWS)


def slot_grads(rows, weights):
    parts = [rows[:, c : c + 128].astype(F32) * weights for c in range(0, CW, 128)]
    return jnp.concatenate(parts, axis=1).astype(BF16)


def inner_with(pf, inv, grad, a):
    inner = jnp.zeros((ROWS, 1), F32)
    for j in range(SLICES):
        inner += jnp.sum(pf[:, columns(a, j)] * inv * grad[block(j), :], axis=1, keepdims=True)
    return inner


def kernel(
    p_hbm, q_hbm, cnt_hbm, own_hbm, loc_hbm,
    loss_ref, qg, pacc, pf, stats, last_rows, last_table, last_weight,
    cnt_ref, own_ref, loc_ref, qf, pall, qall, sbuf, mbuf, rbuf,
    e_send, e_recv, f_send, f_recv, cb_send, cb_recv, g_send, g_recv, w_send, w_recv,
    loss_send, loss_z, loss_x, loss_y, loss_c,
    sacc, hacc, es, fs, fk, ft, cbm, cbt, qinv, wcol,
    in_sem, sent, ag_r, a_r, b_r, t_s, t_r,
):
    dp = lax.axis_index("dp")
    z = lax.axis_index("sub")
    core = lax.rem(dp, 2)
    x = lax.rem(dp // 2, SIDE)
    y = dp // (2 * SIDE)
    above, below = lax.rem(z + 1, N_SUB), lax.rem(z + 3, N_SUB)
    mates = [(e, lax.rem(z + e, N_SUB)) for e in (1, 3, 2)]
    mates_x = [lax.rem(x + d, SIDE) for d in (2, 1, 3)]
    mates_y = [lax.rem(y + d, SIDE) for d in (2, 1, 3)]

    def at(x_, y_, c_):
        return ((y_ * SIDE + x_) * 2 + c_, z)

    def each_peer(body):
        def one(i, carry):
            body(lax.rem(dp + i, N_DP))
            return carry

        lax.fori_loop(1, N_DP, one, 0)

    def send(src, dst, send_sem, recv_sem, device):
        pltpu.make_async_remote_copy(
            src_ref=src, dst_ref=dst, send_sem=send_sem, recv_sem=recv_sem,
            device_id=device, device_id_type=MESH,
        ).start()

    def landed(part, sem):
        pltpu.make_async_copy(part, part, sem).wait()

    ints_in = [
        pltpu.make_async_copy(src, dst, in_sem.at[2 + i])
        for i, (src, dst) in enumerate(((cnt_hbm, cnt_ref), (own_hbm, own_ref), (loc_hbm, loc_ref)))
    ]
    p_in = pltpu.make_async_copy(p_hbm, pf, in_sem.at[0])
    q_in = pltpu.make_async_copy(q_hbm, qf, in_sem.at[1])
    for copy in (*ints_in, q_in):
        copy.start()

    barrier = pltpu.get_barrier_semaphore()
    each_peer(lambda peer: pl.semaphore_signal(barrier, inc=1, device_id=(peer, z), device_id_type=MESH))
    for _, mate in mates:
        pl.semaphore_signal(barrier, inc=1, device_id=(dp, mate), device_id_type=MESH)

    def span(index, rows):
        return pl.ds(pl.multiple_of(index * rows, rows), rows)

    def to_plane(src, dst, sem):
        each_peer(lambda peer: send(src.at[peer], dst.at[dp], t_s.at[sem], t_r.at[sem], (peer, z)))
        dst[dp] = src[dp]

    def to_mates(src, dst, sem):
        for e, mate in mates:
            send(
                src.at[pl.ds(e * ROWS, ROWS)], dst.at[pl.ds((N_SUB - e) * ROWS, ROWS)],
                t_s.at[sem], t_r.at[sem], (dp, mate),
            )
        dst[block(0), :] = src[block(0), :]

    def gather_start(buf, a, which):
        for i in range(4):
            part = pl.ds(i * ROWS, ROWS)
            send(buf.at[0, a, part], buf.at[3, a, part], sent.at[which], ag_r.at[which, a, 0], (dp, above))
            send(buf.at[0, a, part], buf.at[1, a, part], sent.at[which], ag_r.at[which, a, 1], (dp, below))

    def gather_pass_on(buf, a, which):
        landed(buf.at[3, a], ag_r.at[which, a, 0])
        upper, lower = pl.ds(0, GROUP // 2), pl.ds(GROUP // 2, GROUP // 2)
        send(buf.at[3, a, upper], buf.at[2, a, upper], sent.at[which], ag_r.at[which, a, 2], (dp, above))
        landed(buf.at[1, a], ag_r.at[which, a, 1])
        send(buf.at[1, a, lower], buf.at[2, a, lower], sent.at[which], ag_r.at[which, a, 2], (dp, below))

    def gather_done(buf, a, which):
        landed(buf.at[2, a], ag_r.at[which, a, 2])

    low, high = pl.ds(0, SIDE), pl.ds(SIDE, SIDE)

    def first_leg(n):
        for i in range(3):
            send(sbuf.at[n, low, mates_x[i]], mbuf.at[n, x], sent.at[2], a_r.at[n], at(mates_x[i], y, core))
            send(sbuf.at[n, SIDE + mates_y[i]], mbuf.at[n, SIDE + y], sent.at[2], a_r.at[n], at(x, mates_y[i], core))
        mbuf[n, x] = sbuf[n, low, x]
        mbuf[n, SIDE + y] = sbuf[n, SIDE + y]

    def second_leg(n):
        mine = span(core, MSG)
        other = span(1 - core, MSG)
        landed(mbuf.at[n, pl.ds(0, 6)], a_r.at[n])

        def pair(x_, y_, part, c):
            send(mbuf.at[n, low, y_, part], rbuf.at[n, y, :, mine], sent.at[3], b_r.at[n], at(x, y_, c))
            send(mbuf.at[n, high, x_, part], rbuf.at[n, high, x, mine], sent.at[3], b_r.at[n], at(x_, y, c))

        for part, c in ((other, 1 - core), (mine, core)):
            for i in range(3):
                pair(mates_x[i], mates_y[i], part, c)
        pair(x, y, other, 1 - core)
        rbuf[n, y, :, mine] = mbuf[n, low, y, mine]
        rbuf[n, high, x, mine] = mbuf[n, high, x, mine]

    def arrived(n):
        landed(rbuf.at[n, pl.ds(0, 7)], b_r.at[n])

    def serve(n, table, src):
        rows = dot(table, src).astype(BF16)
        for h in range(2):
            sbuf[n, pl.ds(h * SIDE, SIDE)] = rows[:, h * HW : (h + 1) * HW].reshape(SIDE, SIDE, 2 * MSG, HW)

    def rows_of(n):
        parts = [rbuf[n, pl.ds(h * SIDE, SIDE)].reshape(SLOTS, HW) for h in range(2)]
        return jnp.concatenate(parts, axis=1)

    def normalize(src, dst):
        total = jnp.zeros((ROWS, 1), F32)
        for a in range(HALVES):
            for j in range(SLICES):
                v = src[:, columns(a, j)]
                total += jnp.sum(v * v, axis=1, keepdims=True)
        inv = 1.0 / jnp.sqrt(total + epsilon)
        for a in range(HALVES):
            for j in range(SLICES):
                dst[0, a, block(j), :] = (src[:, columns(a, j)] * inv).astype(BF16)
        return jnp.broadcast_to(inv, (ROWS, 128))

    with jax.named_scope("integers_in"):
        for copy in ints_in:
            copy.wait()
    own_row = own_ref[...]
    loc_row = loc_ref[...]
    cnt_row = cnt_ref[...]
    square = (HARD, HARD)
    row_b = jnp.broadcast_to(own_row, square)
    own_col = jnp.sum(jnp.where(iota(square, 0) == iota(square, 1), row_b, 0), axis=1, keepdims=True)
    earlier = (own_col == row_b) & (iota(square, 0) < iota(square, 1))
    rank = jnp.sum(jnp.where(earlier, 1, 0), axis=0, keepdims=True)
    up = (own_row + (N_SUB - z)) % N_SUB
    owner_dp = own_row // N_SUB
    slot_at_own = one_hot(iota((ROWS, HARD), 0) == jnp.where(up == 0, owner_dp * CAP + rank, ROWS))
    cnt_b = jnp.broadcast_to(cnt_row, (ROWS, ROWS))
    upto = iota((ROWS, ROWS), 1) <= iota((ROWS, ROWS), 0)
    before = iota((ROWS, ROWS), 1) < iota((ROWS, ROWS), 0)
    ends = jnp.sum(jnp.where(upto, cnt_b, 0), axis=1, keepdims=True)
    starts = jnp.sum(jnp.where(before, cnt_b, 0), axis=1, keepdims=True)
    slot_id = iota((ROWS, HARD), 1)
    query_t = one_hot((slot_id >= starts) & (slot_id < ends))

    def match(n_dp, n_mid, shape, dim):
        i = iota(shape, dim)
        return i // (n_mid * CAP), (i // CAP) % n_mid, i % CAP

    def spread():
        r = match(N_DP, SLICES, (SLOTS, ROWS), 0)
        c = match(N_DP, 1, (SLOTS, ROWS), 1)
        return one_hot((r[0] == c[0]) & (r[2] == c[2]))

    def spread_t():
        r = match(N_DP, 1, (ROWS, SLOTS), 0)
        c = match(N_DP, SLICES, (ROWS, SLOTS), 1)
        return one_hot((r[0] == c[0]) & (r[2] == c[2]))

    def by_slice(dst, d, rows):
        slice_of = (iota((SLOTS, ROWS), 0) // CAP) % SLICES
        rows = rows.astype(BF16)
        for j in range(SLICES):
            dst[d, :, block(j)] = jnp.where(slice_of == j, rows, jnp.zeros_like(rows))

    def by_slice_t(dst, d, rows):
        slice_of = (iota((ROWS, SLOTS), 1) // CAP) % SLICES
        rows = rows.astype(BF16)
        for j in range(SLICES):
            dst[d, block(j), :] = jnp.where(slice_of == j, rows, jnp.zeros_like(rows))

    by_slice(fs, 0, dot(spread(), dot_nt(slot_at_own, query_t).astype(BF16)))

    with jax.named_scope("queries_in"):
        q_in.wait()
    p_in.start()
    qinv[...] = normalize(qf, qall)
    serve(0, fs[0], qall[0, 0])
    with jax.named_scope("entry_barrier"):
        pl.semaphore_wait(barrier, N_DP - 1 + N_SUB - 1)
    first_leg(0)
    with jax.named_scope("passages_in"):
        p_in.wait()
    stats[0] = normalize(pf, pall)
    gather_start(pall, 0, 0)
    asks = one_hot(iota((N_DP, HARD), 0) == owner_dp)
    row_at = jnp.where(iota((ROWS, HARD), 0) == up * CAP + rank, loc_row + 1, 0).astype(F32).astype(BF16)
    e_send[:, 0, :] = dot_nt(asks, row_at)
    to_plane(e_send, e_recv, 0)
    serve(1, fs[0], qall[0, 1])
    first_leg(1)
    slot_by_up = one_hot(iota((SLOTS, HARD), 0) == up * ROWS + owner_dp * CAP + rank)
    f_send[...] = dot_nt(slot_by_up, query_t).astype(BF16)
    to_mates(f_send, f_recv, 1)
    second_leg(0)
    second_leg(1)

    def asked_passages(d):
        r = match(N_DP, SLICES, (SLOTS, ROWS), 0)
        lane = iota((SLOTS, ROWS), 1)
        asked = dot(one_hot(iota((SLOTS, N_DP), 0) // MSG == iota((SLOTS, N_DP), 1)), e_recv[:, 0, :].astype(BF16))
        row = jnp.sum(jnp.where(lane == d * CAP + r[2], asked, 0.0), axis=1, keepdims=True)
        by_slice(es, d, one_hot((lane + 1).astype(F32) == row))

    landed(e_recv.at[pl.ds(0, N_DP - 1)], t_r.at[0])
    asked_passages(0)

    def score_batch(d, a):
        part = jnp.zeros((ROWS, ROWS), F32)
        for j in range(SLICES):
            part += dot_nt(qall[0, a, block(j), :], pall[d, a, block(j), :])
        sacc[d] += part

    def score_hard(n, d, a):
        arrived(n)
        pairs = dot_nt(qall[0, a], rows_of(n)) * fk[d].astype(F32)
        hacc[pl.ds(d, 1), :] += jnp.sum(pairs, axis=0, keepdims=True)

    sacc[...] = jnp.zeros_like(sacc)
    hacc[...] = jnp.zeros_like(hacc)
    serve(2, es[0], pall[0, 0])
    first_leg(2)
    for d in range(N_SUB):
        mine = dot_nt(query_t, slot_by_up[block(d), :])
        ft[d] = mine
        by_slice_t(fk, d, dot(mine.astype(BF16), spread_t()))
    serve(3, es[0], pall[0, 1])
    first_leg(3)
    gather_pass_on(pall, 0, 0)
    gather_start(pall, 1, 0)
    second_leg(2)
    for d in range(1, N_SUB):
        asked_passages(d)
    score_batch(0, 0)
    score_batch(0, 1)

    def turn(t):
        i = t % 3
        return 1 + 2 * i - 3 * (i // 2), t // 3, i

    def passages(t, carry):
        d, a, i = turn(t)

        @pl.when(i == 2)
        def _():
            gather_done(pall, a, 0)

        serve(4 + t, es[d], pall[d, a])
        first_leg(4 + t)
        second_leg(3 + t)
        score_batch(d, a)

        @pl.when(t == 2)
        def _():
            gather_pass_on(pall, 1, 0)
            gather_start(qall, 0, 1)

        @pl.when(t == 5)
        def _():
            gather_pass_on(qall, 0, 1)
            gather_start(qall, 1, 1)

        @pl.when((t == 1) | (t == 2))
        def _():
            score_hard(1 + t, 0, t - 1)

        @pl.when(t >= 3)
        def _():
            before_d, before_a, _ = turn(t - 3)
            score_hard(1 + t, before_d, before_a)

        return carry

    lax.fori_loop(0, 6, passages, 0)

    landed(f_recv.at[pl.ds(0, GROUP - ROWS)], t_r.at[1])
    for d in range(1, N_SUB):
        by_slice(fs, d, dot(spread(), f_recv[block(d), :]))

    def queries(t):
        d, a, i = turn(t)
        serve(10 + t, fs[d], qall[d, a])
        first_leg(10 + t)
        second_leg(9 + t)

    def queries_first(t, carry):
        @pl.when(t == 2)
        def _():
            gather_done(qall, 0, 1)

        queries(t)
        before_d, before_a, _ = turn(t + 3)
        score_hard(7 + t, before_d, before_a)
        return carry

    lax.fori_loop(0, 3, queries_first, 0)

    scores = [sacc[d] / sharpness_divisor for d in range(N_SUB)]
    exp_batch = [jnp.exp(v) for v in scores]
    fold = spread().astype(F32)
    hard_scores = (
        lax.dot_general(
            hacc[...], fold, (((1,), (0,)), ((), ())),
            precision=lax.Precision.HIGHEST, preferred_element_type=F32,
        )
        / sharpness_divisor
    )
    used = [jnp.sum(ft[d], axis=0, keepdims=True) for d in range(N_SUB)]
    exp_hard = [jnp.where(used[d] > 0.5, jnp.exp(hard_scores[d : d + 1, :]), 0.0) for d in range(N_SUB)]

    def lanes_for(d, row, start):
        shape = (N_DP, ROWS)
        spread_row = jnp.broadcast_to(row.astype(F32), shape)
        by_row = jnp.where(iota(shape, 0) == iota(shape, 1) // CAP, spread_row, 0.0).astype(BF16)
        place = one_hot(iota((ROWS, ROWS), 1) == start + d * CAP + iota((ROWS, ROWS), 0) % CAP)
        return dot(by_row, place)

    total = jnp.zeros((ROWS, 1), F32)
    for d in range(N_SUB):
        total += jnp.sum(exp_batch[d] + ft[d] * exp_hard[d], axis=1, keepdims=True)
    diagonal = iota((ROWS, ROWS), 1) == iota((ROWS, ROWS), 0)
    positive = jnp.sum(jnp.where(diagonal, scores[0], 0.0), axis=1, keepdims=True)
    loss_part = jnp.sum(jnp.log(total) - positive, axis=0, keepdims=True)
    loss_send[...] = jnp.broadcast_to(loss_part, (1, 128))
    for d in range(N_SUB):
        coef = exp_batch[d] / total
        if d == 0:
            coef = coef - jnp.where(diagonal, 1.0, 0.0)
        cb_send[block(d), :] = coef.astype(BF16)
        cbm[:, block(d)] = coef.astype(BF16)
        slot_total = jnp.sum(ft[d] * total, axis=0, keepdims=True) + (1.0 - used[d])
        hard_coef = (exp_hard[d] / slot_total).astype(BF16)
        hard_idx = dot_nt(jnp.broadcast_to(loc_row + 1, (8, HARD)).astype(F32).astype(BF16), slot_by_up[block(d), :])
        g_send[d] = lanes_for((N_SUB - d) % N_SUB, hard_coef, 0) + lanes_for(
            (N_SUB - d) % N_SUB, hard_idx[0:1, :].astype(BF16), MSG
        )
        weight = dot(jnp.broadcast_to(hard_coef, (8, ROWS)), spread_t())[0:1, :]
        fk[d] = (fk[d].astype(F32) * weight).astype(BF16)
    for e, mate in mates:
        send(g_send.at[e], g_recv.at[N_SUB - e], t_s.at[2], t_r.at[2], (dp, mate))
    g_recv[0] = g_send[0]
    to_mates(cb_send, cb_recv, 3)

    def share_loss(dst, index, sem, devices):
        for device in devices:
            send(loss_send, dst.at[index], t_s.at[sem], t_r.at[sem], device)
        dst[index] = loss_send[...]

    def add_loss(src, sem, count):
        landed(src.at[pl.ds(0, count - 1)], t_r.at[sem])
        landed(src.at[pl.ds(0, count - 1)], t_s.at[sem])
        added = src[0]
        for i in range(1, count):
            added = added + src[i]
        loss_send[...] = added

    share_loss(loss_z, z, 4, [(dp, mate) for _, mate in mates])

    scale = 1.0 / sharpness_divisor

    def query_terms(a):
        grad = jnp.zeros((GROUP, CW), F32)
        for n, d in ((2 + a, 0), (4 + 3 * a, 1), (5 + 3 * a, 3), (6 + 3 * a, 2)):
            grad += dot(fk[d], rows_of(n))
        for j in range(SLICES):
            batch = dot(cbm[...], pall[:, a, block(j), :].reshape(GROUP, CW))
            qg[:, columns(a, j)] = (grad[block(j), :] + batch) * scale

    gather_pass_on(qall, 1, 1)
    queries(3)
    landed(g_recv.at[pl.ds(0, N_SUB - 1)], t_r.at[2])
    w_send[:, 0, :] = g_recv[0] + g_recv[1] + g_recv[2] + g_recv[3]
    to_plane(w_send, w_recv, 5)
    add_loss(loss_z, 4, N_SUB)
    share_loss(loss_x, x, 6, [at(mate, y, core) for mate in mates_x])
    serve(14, fs[3], qall[3, 1])
    first_leg(14)
    query_terms(0)
    gather_done(qall, 1, 1)
    serve(15, fs[2], qall[2, 1])
    first_leg(15)
    second_leg(13)
    query_terms(1)
    add_loss(loss_x, 6, SIDE)
    share_loss(loss_y, y, 7, [at(x, mate, core) for mate in mates_y])

    landed(cb_recv.at[pl.ds(0, GROUP - ROWS)], t_r.at[3])
    cbt[...] = jnp.transpose(cb_recv[...].astype(F32)).astype(BF16)
    for a in range(HALVES):
        for j in range(SLICES):
            pacc[a, block(j), :] = dot(cbt[...], qall[:, a, block(j), :].reshape(GROUP, CW)) * scale

    second_leg(14)
    second_leg(15)

    landed(w_recv.at[pl.ds(0, N_DP - 1)], t_r.at[5])
    told = w_recv[:, 0, :].astype(BF16)
    by_slot = dot(one_hot(iota((SLOTS, N_DP), 0) // MSG == iota((SLOTS, N_DP), 1)), told)
    by_slot_t = lax.dot_general(
        told, one_hot(iota((N_DP, SLOTS), 0) == iota((N_DP, SLOTS), 1) // MSG),
        (((0,), (0,)), ((), ())), preferred_element_type=F32,
    )
    for d in range(N_SUB):
        weight_lane = iota((SLOTS, ROWS), 1) == d * CAP + iota((SLOTS, ROWS), 0) % CAP
        weight = jnp.sum(jnp.where(weight_lane, by_slot, 0.0), axis=1, keepdims=True)
        wcol[d] = jnp.broadcast_to(weight * scale, (SLOTS, 128))
        lane = iota((ROWS, SLOTS), 0)
        row_lane = lane == MSG + d * CAP + iota((ROWS, SLOTS), 1) % CAP
        row = jnp.sum(jnp.where(row_lane, by_slot_t, 0.0), axis=0, keepdims=True)
        by_slice_t(es, d, one_hot((lane + 1).astype(F32) == row))
    last_table[...] = es[2]
    last_weight[...] = wcol[2]

    def passage_terms(n, d, a):
        arrived(n)
        pacc[a] += dot(es[d], slot_grads(rows_of(n), wcol[d]))

    passage_terms(0, 0, 0)
    add_loss(loss_y, 7, SIDE)
    share_loss(loss_c, core, 8, [at(x, y, 1 - core)])
    passage_terms(1, 0, 1)

    inv = qinv[:, :1]
    inner = jnp.zeros((ROWS, 1), F32)
    for a in range(HALVES):
        for j in range(SLICES):
            inner += jnp.sum(qf[:, columns(a, j)] * inv * qg[:, columns(a, j)], axis=1, keepdims=True)
    for a in range(HALVES):
        for j in range(SLICES):
            cols = columns(a, j)
            qg[:, cols] = (qg[:, cols] - qf[:, cols] * inv * inner) * inv

    def more_passage_terms(t, carry):
        d, a, _ = turn(t)
        passage_terms(10 + t, d, a)
        return carry

    inv = stats[0, :, :1]

    lax.fori_loop(0, 3, more_passage_terms, 0)
    first = inner_with(pf, inv, pacc.at[0], 0)
    add_loss(loss_c, 8, 2)
    loss_ref[...] = loss_send[...] / (ROWS * N_DP * N_SUB)
    stats[1] = jnp.broadcast_to(first, (ROWS, 128))
    lax.fori_loop(3, 5, more_passage_terms, 0)
    arrived(15)
    last_rows[...] = rows_of(15)

    landed(e_send.at[pl.ds(0, N_DP - 1)], t_s.at[0])
    landed(f_send.at[pl.ds(0, GROUP - ROWS)], t_s.at[1])
    landed(g_send.at[pl.ds(0, N_SUB - 1)], t_s.at[2])
    landed(cb_send.at[pl.ds(0, GROUP - ROWS)], t_s.at[3])
    landed(w_send.at[pl.ds(0, N_DP - 1)], t_s.at[5])
    landed(pall.at[pl.ds(0, 3)], sent.at[0])
    landed(qall.at[pl.ds(0, 3)], sent.at[1])
    landed(mbuf.at[pl.ds(0, 12)], sent.at[2])
    landed(mbuf.at[pl.ds(0, 14)], sent.at[3])


def write_out(
    loss_in, q_in, pacc, pf, stats, last_rows, last_table, last_weight,
    loss_hbm, q_hbm, p_hbm,
    out, grad, loss, sem,
):
    loss[...] = loss_in[:, :1]
    copies = [pltpu.make_async_copy(loss, loss_hbm, sem.at[2, 0])] + [
        pltpu.make_async_copy(q_in.at[pl.ds(i * 32, 32)], q_hbm.at[pl.ds(i * 32, 32)], sem.at[0, i])
        for i in range(4)
    ]
    for copy in copies:
        copy.start()
    grad[...] = pacc[1] + dot(last_table[...], slot_grads(last_rows[...], last_weight[...]))
    inners = stats[1, :, :1] + inner_with(pf, stats[0, :, :1], grad, 1)
    for i in range(4):
        rows = slice(i * 32, (i + 1) * 32)
        inv = stats[0, rows, :1]
        inner = inners[rows, :]
        for j in range(SLICES):
            part = slice(j * ROWS + i * 32, j * ROWS + (i + 1) * 32)
            cols = columns(0, j)
            out[rows, cols] = (pacc[0, part, :] - pf[rows, cols] * inv * inner) * inv
            cols = columns(1, j)
            out[rows, cols] = (grad[part, :] - pf[rows, cols] * inv * inner) * inv
        copy = pltpu.make_async_copy(out.at[pl.ds(i * 32, 32)], p_hbm.at[pl.ds(i * 32, 32)], sem.at[1, i])
        copy.start()
        copies.append(copy)
    for copy in copies:
        copy.wait()


def local(queries, passages, counts, hard_owner, hard_local):
    vmem = pl.BlockSpec(memory_space=pltpu.VMEM)
    any_space = pl.BlockSpec(memory_space=pl.ANY)
    hbm = pl.BlockSpec(memory_space=pltpu.HBM)
    dma = pltpu.SemaphoreType.DMA
    table = pltpu.VMEM((SLOTS, 128), BF16)
    gathered = pltpu.VMEM((N_SUB, HALVES, GROUP, CW), BF16)
    routed = pltpu.VMEM((ITEMS, 2 * SIDE, SIDE, 2 * MSG, HW), BF16)
    masks = pltpu.VMEM((N_SUB, SLOTS, GROUP), BF16)
    one_loss = pltpu.VMEM((1, 128), F32)
    plane = pltpu.VMEM((N_DP, 1, 128), F32)
    mate = pltpu.VMEM((N_SUB, N_DP, 128), F32)
    rows = pltpu.VMEM((ROWS, WIDTH), F32)
    held = pl.pallas_call(
        kernel,
        out_shape=(
            one_loss, rows, pltpu.VMEM((HALVES, GROUP, CW), F32), rows, pltpu.VMEM((2, ROWS, 128), F32),
            pltpu.VMEM((SLOTS, CW), BF16), pltpu.VMEM((GROUP, SLOTS), BF16), pltpu.VMEM((SLOTS, 128), F32),
        ),
        in_specs=[hbm] * 5,
        out_specs=(vmem,) * 8,
        scratch_shapes=[
            pltpu.VMEM((1, ROWS), jnp.int32), pltpu.VMEM((1, HARD), jnp.int32), pltpu.VMEM((1, HARD), jnp.int32),
            rows, gathered, gathered, routed, routed, routed,
            plane, plane, table, table, table, table, mate, mate, plane, plane,
            one_loss, pltpu.VMEM((N_SUB, 1, 128), F32),
            pltpu.VMEM((SIDE, 1, 128), F32), pltpu.VMEM((SIDE, 1, 128), F32), pltpu.VMEM((2, 1, 128), F32),
            pltpu.VMEM((N_SUB, ROWS, ROWS), F32), pltpu.VMEM((8, SLOTS), F32), masks, masks, masks,
            pltpu.VMEM((N_SUB, ROWS, ROWS), F32), pltpu.VMEM((ROWS, GROUP), BF16), pltpu.VMEM((ROWS, GROUP), BF16),
            pltpu.VMEM((ROWS, 128), F32), pltpu.VMEM((N_SUB, SLOTS, 128), F32),
            dma((5,)), dma((4,)), dma((2, HALVES, 3)), dma((ITEMS,)), dma((ITEMS,)), dma((9,)), dma((9,)),
        ],
        compiler_params=pltpu.CompilerParams(
            collective_id=0, has_side_effects=True, vmem_limit_bytes=51 * 2**20
        ),
        name="contrastive",
    )(*[
        pltpu.with_memory_space_constraint(v, pltpu.HBM)
        for v in (passages, queries, counts, hard_owner.reshape(1, HARD), hard_local)
    ])
    loss, query_grad, passage_grad = pl.pallas_call(
        write_out,
        out_shape=(
            jax.ShapeDtypeStruct((1, 1), F32),
            jax.ShapeDtypeStruct((ROWS, WIDTH), F32),
            jax.ShapeDtypeStruct((ROWS, WIDTH), F32),
        ),
        in_specs=[vmem] * 8,
        out_specs=(any_space,) * 3,
        scratch_shapes=[rows, pltpu.VMEM((GROUP, CW), F32), pltpu.VMEM((1, 1), F32), dma((3, 4))],
        compiler_params=pltpu.CompilerParams(vmem_limit_bytes=10 * 2**20),
        name="write_out",
    )(*[pltpu.with_memory_space_constraint(v, pltpu.VMEM) for v in held])
    return loss.reshape(()), query_grad, passage_grad


def solution(mesh):
    in_specs = (
        P(("dp", "sub"), None),
        P(("dp", "sub"), None),
        P(("dp", "sub"), None),
        P(("dp", "sub"), None, None),
        P(("dp", "sub"), None),
    )
    out_specs = (P(), P(("dp", "sub"), None), P(("dp", "sub"), None))
    return jax.shard_map(local, mesh=mesh, in_specs=in_specs, out_specs=out_specs, check_vma=False)
```

```python
import jax
import jax.numpy as jnp
from jax import lax
from jax.experimental import pallas as pl
from jax.experimental.pallas import tpu as pltpu
from jax.sharding import PartitionSpec as P

MESH = pl.DeviceIdType.MESH
F32 = jnp.float32
BF16 = jnp.bfloat16

sharpness_divisor = 0.02
epsilon = 1e-06

ROWS = 128
WIDTH = 4096
HARD = 256
CAP = 4
N_SUB = 4
N_DP = 32
SIDE = 4
GROUP = ROWS * N_SUB
SLOTS = N_DP * N_SUB * CAP
MSG = N_SUB * CAP
HALVES = 2
SLICES = 4
CW = WIDTH // (HALVES * SLICES)
HW = CW // 2
ITEMS = 16


def dot(a, b):
    return lax.dot_general(a, b, (((1,), (0,)), ((), ())), preferred_element_type=F32)


def dot_nt(a, b):
    return lax.dot_general(a, b, (((1,), (1,)), ((), ())), preferred_element_type=F32)


def iota(shape, dim):
    return lax.broadcasted_iota(jnp.int32, shape, dim)


def one_hot(mask):
    return jnp.where(mask, 1.0, 0.0).astype(BF16)


def columns(a, j):
    start = (j * HALVES + a) * CW
    return slice(start, start + CW)


def block(j):
    return slice(j * ROWS, (j + 1) * ROWS)


def slot_grads(rows, weights):
    parts = [rows[:, c : c + 128].astype(F32) * weights for c in range(0, CW, 128)]
    return jnp.concatenate(parts, axis=1).astype(BF16)


def inner_with(pf, inv, grad, a):
    inner = jnp.zeros((ROWS, 1), F32)
    for j in range(SLICES):
        inner += jnp.sum(pf[:, columns(a, j)] * inv * grad[block(j), :], axis=1, keepdims=True)
    return inner


def kernel(
    p_hbm, q_hbm, cnt_hbm, own_hbm, loc_hbm,
    loss_ref, qg, pacc, pf, stats, last_rows, last_table, last_weight,
    cnt_ref, own_ref, loc_ref, qf, pall, qall, sbuf, mbuf, rbuf,
    e_send, e_recv, f_send, f_recv, cb_send, cb_recv, g_send, g_recv, w_send, w_recv,
    loss_send, loss_z, loss_x, loss_y, loss_c,
    sacc, hacc, es, fs, fk, ft, cbm, cbt, qinv, wcol,
    in_sem, sent, ag_r, a_r, b_r, t_s, t_r,
):
    dp = lax.axis_index("dp")
    z = lax.axis_index("sub")
    core = lax.rem(dp, 2)
    x = lax.rem(dp // 2, SIDE)
    y = dp // (2 * SIDE)
    above, below = lax.rem(z + 1, N_SUB), lax.rem(z + 3, N_SUB)
    mates = [(e, lax.rem(z + e, N_SUB)) for e in (1, 3, 2)]
    mates_x = [lax.rem(x + d, SIDE) for d in (2, 1, 3)]
    mates_y = [lax.rem(y + d, SIDE) for d in (2, 1, 3)]

    def at(x_, y_, c_):
        return ((y_ * SIDE + x_) * 2 + c_, z)

    def each_peer(body):
        def one(i, carry):
            body(lax.rem(dp + i, N_DP))
            return carry

        lax.fori_loop(1, N_DP, one, 0)

    def send(src, dst, send_sem, recv_sem, device):
        pltpu.make_async_remote_copy(
            src_ref=src, dst_ref=dst, send_sem=send_sem, recv_sem=recv_sem,
            device_id=device, device_id_type=MESH,
        ).start()

    def landed(part, sem):
        pltpu.make_async_copy(part, part, sem).wait()

    ints_in = [
        pltpu.make_async_copy(src, dst, in_sem.at[2 + i])
        for i, (src, dst) in enumerate(((cnt_hbm, cnt_ref), (own_hbm, own_ref), (loc_hbm, loc_ref)))
    ]
    p_in = pltpu.make_async_copy(p_hbm, pf, in_sem.at[0])
    q_in = pltpu.make_async_copy(q_hbm, qf, in_sem.at[1])
    for copy in (*ints_in, q_in):
        copy.start()

    barrier = pltpu.get_barrier_semaphore()
    each_peer(lambda peer: pl.semaphore_signal(barrier, inc=1, device_id=(peer, z), device_id_type=MESH))
    for _, mate in mates:
        pl.semaphore_signal(barrier, inc=1, device_id=(dp, mate), device_id_type=MESH)

    def span(index, rows):
        return pl.ds(pl.multiple_of(index * rows, rows), rows)

    def to_plane(src, dst, sem):
        each_peer(lambda peer: send(src.at[peer], dst.at[dp], t_s.at[sem], t_r.at[sem], (peer, z)))
        dst[dp] = src[dp]

    def to_mates(src, dst, sem):
        for e, mate in mates:
            send(
                src.at[pl.ds(e * ROWS, ROWS)], dst.at[pl.ds((N_SUB - e) * ROWS, ROWS)],
                t_s.at[sem], t_r.at[sem], (dp, mate),
            )
        dst[block(0), :] = src[block(0), :]

    def gather_start(buf, a, which):
        for i in range(4):
            part = pl.ds(i * ROWS, ROWS)
            send(buf.at[0, a, part], buf.at[3, a, part], sent.at[which], ag_r.at[which, a, 0], (dp, above))
            send(buf.at[0, a, part], buf.at[1, a, part], sent.at[which], ag_r.at[which, a, 1], (dp, below))

    def gather_pass_on(buf, a, which):
        landed(buf.at[3, a], ag_r.at[which, a, 0])
        upper, lower = pl.ds(0, GROUP // 2), pl.ds(GROUP // 2, GROUP // 2)
        send(buf.at[3, a, upper], buf.at[2, a, upper], sent.at[which], ag_r.at[which, a, 2], (dp, above))
        landed(buf.at[1, a], ag_r.at[which, a, 1])
        send(buf.at[1, a, lower], buf.at[2, a, lower], sent.at[which], ag_r.at[which, a, 2], (dp, below))

    def gather_done(buf, a, which):
        landed(buf.at[2, a], ag_r.at[which, a, 2])

    low, high = pl.ds(0, SIDE), pl.ds(SIDE, SIDE)

    def first_leg(n):
        for i in range(3):
            send(sbuf.at[n, low, mates_x[i]], mbuf.at[n, x], sent.at[2], a_r.at[n], at(mates_x[i], y, core))
            send(sbuf.at[n, SIDE + mates_y[i]], mbuf.at[n, SIDE + y], sent.at[2], a_r.at[n], at(x, mates_y[i], core))
        mbuf[n, x] = sbuf[n, low, x]
        mbuf[n, SIDE + y] = sbuf[n, SIDE + y]

    def second_leg(n):
        mine = span(core, MSG)
        other = span(1 - core, MSG)
        landed(mbuf.at[n, pl.ds(0, 6)], a_r.at[n])

        def pair(x_, y_, part, c):
            send(mbuf.at[n, low, y_, part], rbuf.at[n, y, :, mine], sent.at[3], b_r.at[n], at(x, y_, c))
            send(mbuf.at[n, high, x_, part], rbuf.at[n, high, x, mine], sent.at[3], b_r.at[n], at(x_, y, c))

        for part, c in ((other, 1 - core), (mine, core)):
            for i in range(3):
                pair(mates_x[i], mates_y[i], part, c)
        pair(x, y, other, 1 - core)
        rbuf[n, y, :, mine] = mbuf[n, low, y, mine]
        rbuf[n, high, x, mine] = mbuf[n, high, x, mine]

    def arrived(n):
        landed(rbuf.at[n, pl.ds(0, 7)], b_r.at[n])

    def serve(n, table, src):
        rows = dot(table, src).astype(BF16)
        for h in range(2):
            sbuf[n, pl.ds(h * SIDE, SIDE)] = rows[:, h * HW : (h + 1) * HW].reshape(SIDE, SIDE, 2 * MSG, HW)

    def rows_of(n):
        parts = [rbuf[n, pl.ds(h * SIDE, SIDE)].reshape(SLOTS, HW) for h in range(2)]
        return jnp.concatenate(parts, axis=1)

    def normalize(src, dst):
        total = jnp.zeros((ROWS, 1), F32)
        for a in range(HALVES):
            for j in range(SLICES):
                v = src[:, columns(a, j)]
                total += jnp.sum(v * v, axis=1, keepdims=True)
        inv = 1.0 / jnp.sqrt(total + epsilon)
        for a in range(HALVES):
            for j in range(SLICES):
                dst[0, a, block(j), :] = (src[:, columns(a, j)] * inv).astype(BF16)
        return jnp.broadcast_to(inv, (ROWS, 128))

    with jax.named_scope("integers_in"):
        for copy in ints_in:
            copy.wait()
    own_row = own_ref[...]
    loc_row = loc_ref[...]
    cnt_row = cnt_ref[...]
    square = (HARD, HARD)
    row_b = jnp.broadcast_to(own_row, square)
    own_col = jnp.sum(jnp.where(iota(square, 0) == iota(square, 1), row_b, 0), axis=1, keepdims=True)
    earlier = (own_col == row_b) & (iota(square, 0) < iota(square, 1))
    rank = jnp.sum(jnp.where(earlier, 1, 0), axis=0, keepdims=True)
    up = (own_row + (N_SUB - z)) % N_SUB
    owner_dp = own_row // N_SUB
    slot_at_own = one_hot(iota((ROWS, HARD), 0) == jnp.where(up == 0, owner_dp * CAP + rank, ROWS))
    cnt_b = jnp.broadcast_to(cnt_row, (ROWS, ROWS))
    upto = iota((ROWS, ROWS), 1) <= iota((ROWS, ROWS), 0)
    before = iota((ROWS, ROWS), 1) < iota((ROWS, ROWS), 0)
    ends = jnp.sum(jnp.where(upto, cnt_b, 0), axis=1, keepdims=True)
    starts = jnp.sum(jnp.where(before, cnt_b, 0), axis=1, keepdims=True)
    slot_id = iota((ROWS, HARD), 1)
    query_t = one_hot((slot_id >= starts) & (slot_id < ends))

    def match(n_dp, n_mid, shape, dim):
        i = iota(shape, dim)
        return i // (n_mid * CAP), (i // CAP) % n_mid, i % CAP

    def spread():
        r = match(N_DP, SLICES, (SLOTS, ROWS), 0)
        c = match(N_DP, 1, (SLOTS, ROWS), 1)
        return one_hot((r[0] == c[0]) & (r[2] == c[2]))

    def spread_t():
        r = match(N_DP, 1, (ROWS, SLOTS), 0)
        c = match(N_DP, SLICES, (ROWS, SLOTS), 1)
        return one_hot((r[0] == c[0]) & (r[2] == c[2]))

    def by_slice(dst, d, rows):
        slice_of = (iota((SLOTS, ROWS), 0) // CAP) % SLICES
        rows = rows.astype(BF16)
        for j in range(SLICES):
            dst[d, :, block(j)] = jnp.where(slice_of == j, rows, jnp.zeros_like(rows))

    def by_slice_t(dst, d, rows):
        slice_of = (iota((ROWS, SLOTS), 1) // CAP) % SLICES
        rows = rows.astype(BF16)
        for j in range(SLICES):
            dst[d, block(j), :] = jnp.where(slice_of == j, rows, jnp.zeros_like(rows))

    by_slice(fs, 0, dot(spread(), dot_nt(slot_at_own, query_t).astype(BF16)))

    with jax.named_scope("queries_in"):
        q_in.wait()
    p_in.start()
    qinv[...] = normalize(qf, qall)
    serve(0, fs[0], qall[0, 0])
    with jax.named_scope("entry_barrier"):
        pl.semaphore_wait(barrier, N_DP - 1 + N_SUB - 1)
    first_leg(0)
    with jax.named_scope("passages_in"):
        p_in.wait()
    stats[0] = normalize(pf, pall)
    gather_start(pall, 0, 0)
    asks = one_hot(iota((N_DP, HARD), 0) == owner_dp)
    row_at = jnp.where(iota((ROWS, HARD), 0) == up * CAP + rank, loc_row + 1, 0).astype(F32).astype(BF16)
    e_send[:, 0, :] = dot_nt(asks, row_at)
    to_plane(e_send, e_recv, 0)
    serve(1, fs[0], qall[0, 1])
    first_leg(1)
    slot_by_up = one_hot(iota((SLOTS, HARD), 0) == up * ROWS + owner_dp * CAP + rank)
    f_send[...] = dot_nt(slot_by_up, query_t).astype(BF16)
    to_mates(f_send, f_recv, 1)
    second_leg(0)
    second_leg(1)

    def asked_passages(d):
        r = match(N_DP, SLICES, (SLOTS, ROWS), 0)
        lane = iota((SLOTS, ROWS), 1)
        asked = dot(one_hot(iota((SLOTS, N_DP), 0) // MSG == iota((SLOTS, N_DP), 1)), e_recv[:, 0, :].astype(BF16))
        row = jnp.sum(jnp.where(lane == d * CAP + r[2], asked, 0.0), axis=1, keepdims=True)
        by_slice(es, d, one_hot((lane + 1).astype(F32) == row))

    landed(e_recv.at[pl.ds(0, N_DP - 1)], t_r.at[0])
    asked_passages(0)

    def score_batch(d, a):
        part = jnp.zeros((ROWS, ROWS), F32)
        for j in range(SLICES):
            part += dot_nt(qall[0, a, block(j), :], pall[d, a, block(j), :])
        sacc[d] += part

    def score_hard(n, d, a):
        arrived(n)
        pairs = dot_nt(qall[0, a], rows_of(n)) * fk[d].astype(F32)
        hacc[pl.ds(d, 1), :] += jnp.sum(pairs, axis=0, keepdims=True)

    sacc[...] = jnp.zeros_like(sacc)
    hacc[...] = jnp.zeros_like(hacc)
    serve(2, es[0], pall[0, 0])
    first_leg(2)
    for d in range(N_SUB):
        mine = dot_nt(query_t, slot_by_up[block(d), :])
        ft[d] = mine
        by_slice_t(fk, d, dot(mine.astype(BF16), spread_t()))
    serve(3, es[0], pall[0, 1])
    first_leg(3)
    gather_pass_on(pall, 0, 0)
    gather_start(pall, 1, 0)
    second_leg(2)
    for d in range(1, N_SUB):
        asked_passages(d)
    score_batch(0, 0)
    score_batch(0, 1)

    def turn(t):
        i = t % 3
        return 1 + 2 * i - 3 * (i // 2), t // 3, i

    def passages(t, carry):
        d, a, i = turn(t)

        @pl.when(i == 2)
        def _():
            gather_done(pall, a, 0)

        serve(4 + t, es[d], pall[d, a])
        first_leg(4 + t)
        second_leg(3 + t)
        score_batch(d, a)

        @pl.when(t == 2)
        def _():
            gather_pass_on(pall, 1, 0)
            gather_start(qall, 0, 1)

        @pl.when(t == 5)
        def _():
            gather_pass_on(qall, 0, 1)
            gather_start(qall, 1, 1)

        @pl.when((t == 1) | (t == 2))
        def _():
            score_hard(1 + t, 0, t - 1)

        @pl.when(t >= 3)
        def _():
            before_d, before_a, _ = turn(t - 3)
            score_hard(1 + t, before_d, before_a)

        return carry

    lax.fori_loop(0, 6, passages, 0)

    landed(f_recv.at[pl.ds(0, GROUP - ROWS)], t_r.at[1])
    for d in range(1, N_SUB):
        by_slice(fs, d, dot(spread(), f_recv[block(d), :]))

    def queries(t):
        d, a, i = turn(t)
        serve(10 + t, fs[d], qall[d, a])
        first_leg(10 + t)
        second_leg(9 + t)

    def queries_first(t, carry):
        @pl.when(t == 2)
        def _():
            gather_done(qall, 0, 1)

        queries(t)
        before_d, before_a, _ = turn(t + 3)
        score_hard(7 + t, before_d, before_a)
        return carry

    lax.fori_loop(0, 3, queries_first, 0)

    scores = [sacc[d] / sharpness_divisor for d in range(N_SUB)]
    exp_batch = [jnp.exp(v) for v in scores]
    fold = spread().astype(F32)
    hard_scores = (
        lax.dot_general(
            hacc[...], fold, (((1,), (0,)), ((), ())),
            precision=lax.Precision.HIGHEST, preferred_element_type=F32,
        )
        / sharpness_divisor
    )
    used = [jnp.sum(ft[d], axis=0, keepdims=True) for d in range(N_SUB)]
    exp_hard = [jnp.where(used[d] > 0.5, jnp.exp(hard_scores[d : d + 1, :]), 0.0) for d in range(N_SUB)]

    def lanes_for(d, row, start):
        shape = (N_DP, ROWS)
        spread_row = jnp.broadcast_to(row.astype(F32), shape)
        by_row = jnp.where(iota(shape, 0) == iota(shape, 1) // CAP, spread_row, 0.0).astype(BF16)
        place = one_hot(iota((ROWS, ROWS), 1) == start + d * CAP + iota((ROWS, ROWS), 0) % CAP)
        return dot(by_row, place)

    total = jnp.zeros((ROWS, 1), F32)
    for d in range(N_SUB):
        total += jnp.sum(exp_batch[d] + ft[d] * exp_hard[d], axis=1, keepdims=True)
    diagonal = iota((ROWS, ROWS), 1) == iota((ROWS, ROWS), 0)
    positive = jnp.sum(jnp.where(diagonal, scores[0], 0.0), axis=1, keepdims=True)
    loss_part = jnp.sum(jnp.log(total) - positive, axis=0, keepdims=True)
    loss_send[...] = jnp.broadcast_to(loss_part, (1, 128))
    for d in range(N_SUB):
        coef = exp_batch[d] / total
        if d == 0:
            coef = coef - jnp.where(diagonal, 1.0, 0.0)
        cb_send[block(d), :] = coef.astype(BF16)
        cbm[:, block(d)] = coef.astype(BF16)
        slot_total = jnp.sum(ft[d] * total, axis=0, keepdims=True) + (1.0 - used[d])
        hard_coef = (exp_hard[d] / slot_total).astype(BF16)
        hard_idx = dot_nt(jnp.broadcast_to(loc_row + 1, (8, HARD)).astype(F32).astype(BF16), slot_by_up[block(d), :])
        g_send[d] = lanes_for((N_SUB - d) % N_SUB, hard_coef, 0) + lanes_for(
            (N_SUB - d) % N_SUB, hard_idx[0:1, :].astype(BF16), MSG
        )
        weight = dot(jnp.broadcast_to(hard_coef, (8, ROWS)), spread_t())[0:1, :]
        fk[d] = (fk[d].astype(F32) * weight).astype(BF16)
    for e, mate in mates:
        send(g_send.at[e], g_recv.at[N_SUB - e], t_s.at[2], t_r.at[2], (dp, mate))
    g_recv[0] = g_send[0]
    to_mates(cb_send, cb_recv, 3)

    def share_loss(dst, index, sem, devices):
        for device in devices:
            send(loss_send, dst.at[index], t_s.at[sem], t_r.at[sem], device)
        dst[index] = loss_send[...]

    def add_loss(src, sem, count):
        landed(src.at[pl.ds(0, count - 1)], t_r.at[sem])
        landed(src.at[pl.ds(0, count - 1)], t_s.at[sem])
        added = src[0]
        for i in range(1, count):
            added = added + src[i]
        loss_send[...] = added

    share_loss(loss_z, z, 4, [(dp, mate) for _, mate in mates])

    scale = 1.0 / sharpness_divisor

    def query_terms(a):
        grad = jnp.zeros((GROUP, CW), F32)
        for n, d in ((2 + a, 0), (4 + 3 * a, 1), (5 + 3 * a, 3), (6 + 3 * a, 2)):
            grad += dot(fk[d], rows_of(n))
        for j in range(SLICES):
            batch = dot(cbm[...], pall[:, a, block(j), :].reshape(GROUP, CW))
            qg[:, columns(a, j)] = (grad[block(j), :] + batch) * scale

    gather_pass_on(qall, 1, 1)
    queries(3)
    landed(g_recv.at[pl.ds(0, N_SUB - 1)], t_r.at[2])
    w_send[:, 0, :] = g_recv[0] + g_recv[1] + g_recv[2] + g_recv[3]
    to_plane(w_send, w_recv, 5)
    add_loss(loss_z, 4, N_SUB)
    share_loss(loss_x, x, 6, [at(mate, y, core) for mate in mates_x])
    serve(14, fs[3], qall[3, 1])
    first_leg(14)
    query_terms(0)
    gather_done(qall, 1, 1)
    serve(15, fs[2], qall[2, 1])
    first_leg(15)
    second_leg(13)
    query_terms(1)
    add_loss(loss_x, 6, SIDE)
    share_loss(loss_y, y, 7, [at(x, mate, core) for mate in mates_y])

    landed(cb_recv.at[pl.ds(0, GROUP - ROWS)], t_r.at[3])
    cbt[...] = jnp.transpose(cb_recv[...].astype(F32)).astype(BF16)
    for a in range(HALVES):
        for j in range(SLICES):
            pacc[a, block(j), :] = dot(cbt[...], qall[:, a, block(j), :].reshape(GROUP, CW)) * scale

    second_leg(14)
    second_leg(15)

    landed(w_recv.at[pl.ds(0, N_DP - 1)], t_r.at[5])
    told = w_recv[:, 0, :].astype(BF16)
    by_slot = dot(one_hot(iota((SLOTS, N_DP), 0) // MSG == iota((SLOTS, N_DP), 1)), told)
    by_slot_t = lax.dot_general(
        told, one_hot(iota((N_DP, SLOTS), 0) == iota((N_DP, SLOTS), 1) // MSG),
        (((0,), (0,)), ((), ())), preferred_element_type=F32,
    )
    for d in range(N_SUB):
        weight_lane = iota((SLOTS, ROWS), 1) == d * CAP + iota((SLOTS, ROWS), 0) % CAP
        weight = jnp.sum(jnp.where(weight_lane, by_slot, 0.0), axis=1, keepdims=True)
        wcol[d] = jnp.broadcast_to(weight * scale, (SLOTS, 128))
        lane = iota((ROWS, SLOTS), 0)
        row_lane = lane == MSG + d * CAP + iota((ROWS, SLOTS), 1) % CAP
        row = jnp.sum(jnp.where(row_lane, by_slot_t, 0.0), axis=0, keepdims=True)
        by_slice_t(es, d, one_hot((lane + 1).astype(F32) == row))
    last_table[...] = es[2]
    last_weight[...] = wcol[2]

    def passage_terms(n, d, a):
        arrived(n)
        pacc[a] += dot(es[d], slot_grads(rows_of(n), wcol[d]))

    passage_terms(0, 0, 0)
    add_loss(loss_y, 7, SIDE)
    share_loss(loss_c, core, 8, [at(x, y, 1 - core)])
    passage_terms(1, 0, 1)

    inv = qinv[:, :1]
    inner = jnp.zeros((ROWS, 1), F32)
    for a in range(HALVES):
        for j in range(SLICES):
            inner += jnp.sum(qf[:, columns(a, j)] * inv * qg[:, columns(a, j)], axis=1, keepdims=True)
    for a in range(HALVES):
        for j in range(SLICES):
            cols = columns(a, j)
            qg[:, cols] = (qg[:, cols] - qf[:, cols] * inv * inner) * inv

    def more_passage_terms(t, carry):
        d, a, _ = turn(t)
        passage_terms(10 + t, d, a)
        return carry

    inv = stats[0, :, :1]

    lax.fori_loop(0, 3, more_passage_terms, 0)
    first = inner_with(pf, inv, pacc.at[0], 0)
    stats[1] = jnp.broadcast_to(first, (ROWS, 128))
    lax.fori_loop(3, 5, more_passage_terms, 0)
    add_loss(loss_c, 8, 2)
    loss_ref[...] = loss_send[...] / (ROWS * N_DP * N_SUB)
    arrived(15)
    last_rows[...] = rows_of(15)

    landed(e_send.at[pl.ds(0, N_DP - 1)], t_s.at[0])
    landed(f_send.at[pl.ds(0, GROUP - ROWS)], t_s.at[1])
    landed(g_send.at[pl.ds(0, N_SUB - 1)], t_s.at[2])
    landed(cb_send.at[pl.ds(0, GROUP - ROWS)], t_s.at[3])
    landed(w_send.at[pl.ds(0, N_DP - 1)], t_s.at[5])
    landed(pall.at[pl.ds(0, 3)], sent.at[0])
    landed(qall.at[pl.ds(0, 3)], sent.at[1])
    landed(mbuf.at[pl.ds(0, 12)], sent.at[2])
    landed(mbuf.at[pl.ds(0, 14)], sent.at[3])


def write_out(
    loss_in, q_in, pacc, pf, stats, last_rows, last_table, last_weight,
    loss_hbm, q_hbm, p_hbm,
    out, grad, loss, sem,
):
    loss[...] = loss_in[:, :1]
    copies = [pltpu.make_async_copy(loss, loss_hbm, sem.at[2, 0])] + [
        pltpu.make_async_copy(q_in.at[pl.ds(i * 32, 32)], q_hbm.at[pl.ds(i * 32, 32)], sem.at[0, i])
        for i in range(4)
    ]
    for copy in copies:
        copy.start()
    grad[...] = pacc[1] + dot(last_table[...], slot_grads(last_rows[...], last_weight[...]))
    inners = stats[1, :, :1] + inner_with(pf, stats[0, :, :1], grad, 1)
    for i in range(4):
        rows = slice(i * 32, (i + 1) * 32)
        inv = stats[0, rows, :1]
        inner = inners[rows, :]
        for j in range(SLICES):
            part = slice(j * ROWS + i * 32, j * ROWS + (i + 1) * 32)
            cols = columns(0, j)
            out[rows, cols] = (pacc[0, part, :] - pf[rows, cols] * inv * inner) * inv
            cols = columns(1, j)
            out[rows, cols] = (grad[part, :] - pf[rows, cols] * inv * inner) * inv
        copy = pltpu.make_async_copy(out.at[pl.ds(i * 32, 32)], p_hbm.at[pl.ds(i * 32, 32)], sem.at[1, i])
        copy.start()
        copies.append(copy)
    for copy in copies:
        copy.wait()


def local(queries, passages, counts, hard_owner, hard_local):
    vmem = pl.BlockSpec(memory_space=pltpu.VMEM)
    any_space = pl.BlockSpec(memory_space=pl.ANY)
    hbm = pl.BlockSpec(memory_space=pltpu.HBM)
    dma = pltpu.SemaphoreType.DMA
    table = pltpu.VMEM((SLOTS, 128), BF16)
    gathered = pltpu.VMEM((N_SUB, HALVES, GROUP, CW), BF16)
    routed = pltpu.VMEM((ITEMS, 2 * SIDE, SIDE, 2 * MSG, HW), BF16)
    masks = pltpu.VMEM((N_SUB, SLOTS, GROUP), BF16)
    one_loss = pltpu.VMEM((1, 128), F32)
    plane = pltpu.VMEM((N_DP, 1, 128), F32)
    mate = pltpu.VMEM((N_SUB, N_DP, 128), F32)
    rows = pltpu.VMEM((ROWS, WIDTH), F32)
    held = pl.pallas_call(
        kernel,
        out_shape=(
            one_loss, rows, pltpu.VMEM((HALVES, GROUP, CW), F32), rows, pltpu.VMEM((2, ROWS, 128), F32),
            pltpu.VMEM((SLOTS, CW), BF16), pltpu.VMEM((GROUP, SLOTS), BF16), pltpu.VMEM((SLOTS, 128), F32),
        ),
        in_specs=[hbm] * 5,
        out_specs=(vmem,) * 8,
        scratch_shapes=[
            pltpu.VMEM((1, ROWS), jnp.int32), pltpu.VMEM((1, HARD), jnp.int32), pltpu.VMEM((1, HARD), jnp.int32),
            rows, gathered, gathered, routed, routed, routed,
            plane, plane, table, table, table, table, mate, mate, plane, plane,
            one_loss, pltpu.VMEM((N_SUB, 1, 128), F32),
            pltpu.VMEM((SIDE, 1, 128), F32), pltpu.VMEM((SIDE, 1, 128), F32), pltpu.VMEM((2, 1, 128), F32),
            pltpu.VMEM((N_SUB, ROWS, ROWS), F32), pltpu.VMEM((8, SLOTS), F32), masks, masks, masks,
            pltpu.VMEM((N_SUB, ROWS, ROWS), F32), pltpu.VMEM((ROWS, GROUP), BF16), pltpu.VMEM((ROWS, GROUP), BF16),
            pltpu.VMEM((ROWS, 128), F32), pltpu.VMEM((N_SUB, SLOTS, 128), F32),
            dma((5,)), dma((4,)), dma((2, HALVES, 3)), dma((ITEMS,)), dma((ITEMS,)), dma((9,)), dma((9,)),
        ],
        compiler_params=pltpu.CompilerParams(
            collective_id=0, has_side_effects=True, vmem_limit_bytes=51 * 2**20
        ),
        name="contrastive",
    )(*[
        pltpu.with_memory_space_constraint(v, pltpu.HBM)
        for v in (passages, queries, counts, hard_owner.reshape(1, HARD), hard_local)
    ])
    loss, query_grad, passage_grad = pl.pallas_call(
        write_out,
        out_shape=(
            jax.ShapeDtypeStruct((1, 1), F32),
            jax.ShapeDtypeStruct((ROWS, WIDTH), F32),
            jax.ShapeDtypeStruct((ROWS, WIDTH), F32),
        ),
        in_specs=[vmem] * 8,
        out_specs=(any_space,) * 3,
        scratch_shapes=[rows, pltpu.VMEM((GROUP, CW), F32), pltpu.VMEM((1, 1), F32), dma((3, 4))],
        compiler_params=pltpu.CompilerParams(vmem_limit_bytes=10 * 2**20),
        name="write_out",
    )(*[pltpu.with_memory_space_constraint(v, pltpu.VMEM) for v in held])
    return loss.reshape(()), query_grad, passage_grad


def solution(mesh):
    in_specs = (
        P(("dp", "sub"), None),
        P(("dp", "sub"), None),
        P(("dp", "sub"), None),
        P(("dp", "sub"), None, None),
        P(("dp", "sub"), None),
    )
    out_specs = (P(), P(("dp", "sub"), None), P(("dp", "sub"), None))
    return jax.shard_map(local, mesh=mesh, in_specs=in_specs, out_specs=out_specs, check_vma=False)
```
